32 devices in a mesh: grp: 4 (over y, x), sub: 8 (over z, core).
Axes of the slice: x: 2, y: 2, z: 4, core: 2. Of those that a mesh axis runs over, the one named last changes fastest.
Arguments:
- right_side: float32 [64, 16384], P(None, ('grp', 'sub')), may hold values from -6 to 6
- order: int32 [16384], P(('grp', 'sub')), may hold values from 0 to 16383, as said below
- leaf_split: int32 [32], P(('grp', 'sub')), may hold values from 128 to 384
- leaf_inverse: float32 [16384, 512], P(('grp', 'sub')), may hold values from -2 to 2
- basis_left: float32 [6, 16384, 128], P(None, ('grp', 'sub')), may hold values from -0.5 to 0.5
- basis_right: float32 [6, 16384, 128], P(None, ('grp', 'sub')), may hold values from -1.5 to 1.5
- coupling: float32 [32, 6, 256, 256], P(('grp', 'sub')), may hold values from -0.5 to 0.5, as said below
Outputs:
- solution: float32 [64, 16384], P(None, ('grp', 'sub'))
The draws below stay inside these ranges and needn't reach their ends.
Inputs may be any that keep to these rules, and one draw needn't show every extreme that they name: order[i] lies in the same block of 512 positions as i, and each block's entries are a permutation of that block's indices. coupling[d, k] is the same for all device blocks d with the same d // 2^(5 - k).
All inputs are finite; a program needn't handle non-finite values.
Results may differ from the reference program's by a relative error of at most 0.0001.
Values sent between devices are 32-bit elements; how exact they have to be, the bound alone decides.
No kernel may reach another device: no remote copies, remote signals or barrier semaphores. Data moves between devices by JAX's collectives and lax.ppermute only.
A program may use at most 64 MiB of HBM per device.

```python
import jax
import jax.numpy as jnp
from jax import lax

FACTOR_RANK = 128
NRHS = 64
ROWS_DEV = 512
BLOCKS = 32
TOP = 5
LEVELS = 6
N = 16384


def draw_order(key, part):
    key = jax.random.fold_in(key, 11)
    keys = jax.random.split(key, BLOCKS)
    shuffled = jax.vmap(lambda single: jax.random.permutation(single, ROWS_DEV))(keys)
    offsets = jnp.arange(BLOCKS, dtype=jnp.int32)[:, None] * ROWS_DEV
    return (shuffled.astype(jnp.int32) + offsets).reshape(N).astype(jnp.int32)


def draw_leaf_split(key, part):
    key = jax.random.fold_in(key, 12)
    lowest = ROWS_DEV // 4
    highest_level = 3 * ROWS_DEV // 4
    splits = jax.random.randint(key, (BLOCKS,), lowest, highest_level + 1, dtype=jnp.int32)
    splits = splits.at[0].set(lowest)
    splits = splits.at[1].set(highest_level)
    return splits.astype(jnp.int32)


def noise_field(key, shape):
    return jnp.clip(jax.random.normal(key, shape, jnp.float32), -6.0, 6.0)


def draw_leaf_inverse(key, part):
    key = jax.random.fold_in(key, 13)
    key_noise, key_diag = jax.random.split(key)
    spread = noise_field(key_noise, (N, ROWS_DEV)) * (0.5 / jnp.sqrt(ROWS_DEV / 2.0))
    diagonal = jax.random.uniform(key_diag, (N, ROWS_DEV), jnp.float32, 1.0, 2.0)
    row_index = jax.lax.broadcasted_iota(jnp.int32, (N, ROWS_DEV), 0) % ROWS_DEV
    column_index = jax.lax.broadcasted_iota(jnp.int32, (N, ROWS_DEV), 1)
    return jnp.where(row_index == column_index, diagonal, spread).astype(jnp.float32)


def draw_basis_right(key, part):
    key = jax.random.fold_in(key, 14)
    levels_axis = jnp.arange(LEVELS, dtype=jnp.float32)
    child_rows = N / 2.0 ** (levels_axis + 1.0)
    scales = 1.0 / jnp.sqrt(child_rows)
    return (noise_field(key, (LEVELS, N, FACTOR_RANK)) * scales[:, None, None]).astype(jnp.float32)


def draw_coupling(key, part):
    key = jax.random.fold_in(key, 15)

    def one_entry(device_id, tree_level):
        node_id = jnp.right_shift(device_id, TOP - tree_level)
        node_key = jax.random.fold_in(jax.random.fold_in(key, tree_level), node_id)
        return noise_field(node_key, (2 * FACTOR_RANK, 2 * FACTOR_RANK)) * (0.3 / jnp.sqrt(2.0 * FACTOR_RANK))
    devices_axis = jnp.arange(BLOCKS, dtype=jnp.int32)
    levels_axis = jnp.arange(LEVELS, dtype=jnp.int32)
    table = jax.vmap(lambda device_id: jax.vmap(lambda tree_level: one_entry(device_id, tree_level))(levels_axis))(devices_axis)
    return table.astype(jnp.float32)


def steps_of(key, dims, shards, least, largest):
    factor_of, own = 1.0, jax.random.fold_in(key, 6)
    for axis_at, shards_of in shards:
        draws = jnp.exp(jax.random.uniform(jax.random.fold_in(own, axis_at), (shards_of,), jnp.float32, least / len(shards), largest / len(shards)))
        factor_of = factor_of * jnp.repeat(draws, dims[axis_at] // shards_of).reshape([-1 if axis == axis_at else 1 for axis in range(len(dims))])
    return factor_of


def normal_values(own_key, dims, scale, bound, cuts=(), kind=jnp.bfloat16):
    result = scale * jax.random.normal(own_key, dims, jnp.float32)
    if cuts:
        result = result * steps_of(own_key, dims, cuts, -0.22, 0.18)
    return jnp.clip(result, -bound, bound).astype(kind)


def setup_inputs(seed: int = 0) -> dict:
    arg_keys = jax.random.split(jax.random.key(seed), 8)
    return {
        "right_side": normal_values(arg_keys[0], (NRHS, N), 1.0, 6.0, ((1, 32),), jnp.float32),
        "order": draw_order(jax.random.fold_in(arg_keys[7], 71), 0),
        "leaf_split": draw_leaf_split(jax.random.fold_in(arg_keys[7], 71), 0),
        "leaf_inverse": draw_leaf_inverse(jax.random.fold_in(arg_keys[7], 71), 0),
        "basis_left": normal_values(arg_keys[4], (LEVELS, N, FACTOR_RANK), FACTOR_RANK ** -0.5, 0.5, ((1, 32),), jnp.float32),
        "basis_right": draw_basis_right(jax.random.fold_in(arg_keys[7], 71), 0),
        "coupling": draw_coupling(jax.random.fold_in(arg_keys[7], 71), 0),
    }


def reference(right_side, order, leaf_split, leaf_inverse, basis_left, basis_right, coupling):
    highest_level = lax.Precision.HIGHEST
    current = right_side[:, order]
    blocks = leaf_split.shape[0]
    row_count = current.shape[1] // blocks
    positions = jnp.arange(row_count, dtype=jnp.int32)
    is_left = positions[None, :] < leaf_split[:, None]
    block_mask = is_left[:, :, None] == is_left[:, None, :]
    leaf_block_list = jnp.where(block_mask, leaf_inverse.reshape(blocks, row_count, row_count), 0.0)
    reshaped_rows = current.reshape(NRHS, blocks, row_count)
    reshaped_rows = jnp.einsum('lhx,hxo->lho', reshaped_rows, leaf_block_list, precision=highest_level)
    left_row_slice = jnp.where(is_left[None], reshaped_rows, 0.0)
    right_row_slice = jnp.where(is_left[None], 0.0, reshaped_rows)
    local_right_factor = basis_right[TOP].reshape(blocks, row_count, FACTOR_RANK)
    local_left_factor = basis_left[TOP].reshape(blocks, row_count, FACTOR_RANK)
    weights = jnp.concatenate([
        jnp.einsum('pkz,kzx->kpx', left_row_slice, local_right_factor, precision=highest_level),
        jnp.einsum('pkz,kzx->kpx', right_row_slice, local_right_factor, precision=highest_level)], axis=2)
    coupled_system = jnp.einsum('dbj,djk->dbk', weights, coupling[:, TOP], precision=highest_level)
    upper_update = jnp.einsum('aqx,atx->qat', coupled_system[..., :FACTOR_RANK], local_left_factor, precision=highest_level)
    lower_update = jnp.einsum('aqx,atx->qat', coupled_system[..., FACTOR_RANK:], local_left_factor, precision=highest_level)
    reshaped_rows = reshaped_rows - jnp.where(is_left[None], upper_update, lower_update)
    current = reshaped_rows.reshape(NRHS, N)
    for tree_level in range(TOP - 1, -1, -1):
        nodes = 2 ** tree_level
        child = N // (2 * nodes)
        reshaped_rows = current.reshape(NRHS, nodes, 2, child)
        level_right = basis_right[tree_level].reshape(nodes, 2, child, FACTOR_RANK)
        level_left = basis_left[tree_level].reshape(nodes, 2, child, FACTOR_RANK)
        weights = jnp.einsum('bnsc,nscr->nbsr', reshaped_rows, level_right, precision=highest_level)
        weights = weights.reshape(nodes, NRHS, 2 * FACTOR_RANK)
        level_coupling = coupling[::blocks // nodes, tree_level]
        coupled_system = jnp.einsum('nbj,njk->nbk', weights, level_coupling, precision=highest_level)
        coupled_system = coupled_system.reshape(nodes, NRHS, 2, FACTOR_RANK)
        correction = jnp.einsum('nbsr,nscr->bnsc', coupled_system, level_left, precision=highest_level)
        current = (reshaped_rows - correction).reshape(NRHS, N)
    return current
```

```python
import jax
import jax.numpy as jnp
from jax import lax
from jax.sharding import PartitionSpec as P

AXES = ("grp", "sub")
HIGH = lax.Precision.HIGHEST


def dot(a, b):
    return jnp.dot(a, b, precision=HIGH, preferred_element_type=jnp.float32)


def dot_nt(a, b):
    return lax.dot_general(
        a, b, (((1,), (1,)), ((), ())), precision=HIGH, preferred_element_type=jnp.float32
    )


def dot_tn(a, b):
    return lax.dot_general(
        a, b, (((0,), (0,)), ((), ())), precision=HIGH, preferred_element_type=jnp.float32
    )


def odd_partner(value, bit):
    return lax.ppermute(value, AXES, [(i, i ^ 1 << bit) for i in range(1, lax.axis_size(AXES), 2)])


def to_odd(value):
    return lax.ppermute(value, AXES, [(i, i + 1) for i in range(0, lax.axis_size(AXES), 2)])


def to_even(value):
    return lax.ppermute(value, AXES, [(i, i - 1) for i in range(1, lax.axis_size(AXES), 2)])


def per_device(right_side, order, leaf_split, leaf_inverse, basis_left, basis_right, coupling):
    row_count = right_side.shape[1]
    rank = basis_left.shape[2]
    top = basis_left.shape[0] - 1
    device_id = lax.axis_index(AXES)
    right_cols = jnp.concatenate([basis_right[k] for k in range(top)], axis=1)
    gram = {k: dot_tn(basis_left[k], right_cols[:, : k * rank]) for k in range(1, top)}
    gram_even = {k: to_odd(gram[k]) for k in range(1, top)}

    gathered = jnp.take(right_side, order % row_count, axis=1)
    is_left = lax.iota(jnp.int32, row_count) < leaf_split[0]
    leaf = jnp.where(is_left[:, None] == is_left[None, :], leaf_inverse, 0.0)
    current = dot(gathered, leaf)
    rows = current.shape[0]
    halves = jnp.concatenate(
        [jnp.where(is_left[None, :], current, 0.0), jnp.where(is_left[None, :], 0.0, current)], axis=0
    )
    w = dot(halves, basis_right[top])
    w = jnp.concatenate([w[:rows], w[rows:]], axis=1)
    z = dot(w, coupling[0, top])
    both = dot_nt(jnp.concatenate([z[:, :rank], z[:, rank:]], axis=0), basis_left[top])
    current = current - jnp.where(is_left[None, :], both[:rows], both[rows:])

    sums = dot(current, right_cols)
    left_sums, right_sums = to_odd(sums), sums
    left_gram, right_gram = gram_even, gram
    chosen = []
    for bit in range(top):
        k = top - 1 - bit
        own = slice(k * rank, (k + 1) * rank)
        z = dot(jnp.concatenate([left_sums[:, own], right_sums[:, own]], axis=1), coupling[0, k])
        if bit == 0:
            chosen.append((z[:, rank:], z[:, :rank]))
        else:
            side = jnp.where(on_right, z[:, rank:], z[:, :rank])
            chosen.append((side, side))
        if k == 0:
            break
        gram_pair = jnp.concatenate([left_gram[k], right_gram[k]], axis=0)
        sums = left_sums[:, : k * rank] + right_sums[:, : k * rank] - dot(z, gram_pair)
        gram = {j: left_gram[j] + right_gram[j] for j in range(1, k)}
        on_right = (device_id >> (bit + 1)) & 1 == 1
        got_sums = odd_partner(sums, bit + 1)
        left_sums = jnp.where(on_right, got_sums, sums)
        right_sums = jnp.where(on_right, sums, got_sums)
        got = {j: odd_partner(gram[j], bit + 1) for j in range(1, k)}
        left_gram = {j: jnp.where(on_right, got[j], gram[j]) for j in range(1, k)}
        right_gram = {j: jnp.where(on_right, gram[j], got[j]) for j in range(1, k)}
    is_odd = device_id & 1 == 1
    z_all = jnp.concatenate(
        [jnp.where(is_odd, mine, to_even(other)) for mine, other in chosen], axis=1
    )
    left_cols = jnp.concatenate([basis_left[top - 1 - bit] for bit in range(top)], axis=1)
    return current - dot_nt(z_all, left_cols)


def solution(mesh):
    in_specs = (
        P(None, AXES),
        P(AXES),
        P(AXES),
        P(AXES, None),
        P(None, AXES, None),
        P(None, AXES, None),
        P(AXES, None, None, None),
    )
    return jax.shard_map(
        per_device, mesh=mesh, in_specs=in_specs, out_specs=P(None, AXES), check_vma=False
    )
```

```python
import jax
import jax.numpy as jnp
from jax import lax
from jax.sharding import PartitionSpec as P

AXES = ("grp", "sub")
HIGH = lax.Precision.HIGH


def dot(a, b):
    return jnp.dot(a, b, precision=HIGH, preferred_element_type=jnp.float32)


def dot_nt(a, b):
    return lax.dot_general(
        a, b, (((1,), (1,)), ((), ())), precision=HIGH, preferred_element_type=jnp.float32
    )


def dot_tn(a, b):
    return lax.dot_general(
        a, b, (((0,), (0,)), ((), ())), precision=HIGH, preferred_element_type=jnp.float32
    )


def exchange(value, mask):
    return lax.ppermute(value, AXES, [(i, i ^ mask) for i in range(lax.axis_size(AXES))])


def split(value, half):
    n = value.shape[0] // 2
    return jnp.where(half, value[n:], value[:n]), jnp.where(half, value[:n], value[n:])


def join(mine, other, half):
    return jnp.where(
        half, jnp.concatenate([other, mine], axis=0), jnp.concatenate([mine, other], axis=0)
    )


def ordered(own, got, on_right):
    return jnp.where(on_right, got, own), jnp.where(on_right, own, got)


def per_device(right_side, order, leaf_split, leaf_inverse, basis_left, basis_right, coupling):
    row_count = right_side.shape[1]
    rank = basis_left.shape[2]
    top = basis_left.shape[0] - 1
    device_id = lax.axis_index(AXES)
    parity = device_id & 1
    for bit in range(1, top):
        parity = parity ^ ((device_id >> bit) & 1)
    half = parity == 1
    right_cols = jnp.concatenate([basis_right[k] for k in range(top)], axis=1)
    gram = {k: dot_tn(basis_left[k], right_cols[:, : k * rank]) for k in range(1, top)}
    on_right = device_id & 1 == 1
    lower = jnp.concatenate([gram[k] for k in range(top - 2, 0, -1)], axis=1)
    low_keep, low_send = split(lower, half)
    low_width = lower.shape[1]
    n = rank // 2
    first = jnp.concatenate([low_send, gram[top - 1][:n], gram[top - 1][n:]], axis=1)
    got = exchange(first, 1)
    low = low_keep + got[:, :low_width]
    w = (top - 1) * rank
    got_top = jnp.concatenate([got[:, low_width : low_width + w], got[:, low_width + w :]], axis=0)
    gram_pair = jnp.concatenate(ordered(gram[top - 1], got_top, on_right), axis=0)
    pairs = {top - 1: gram_pair}
    for k in range(top - 2, 0, -1):
        bit = top - 1 - k
        right = (device_id >> bit) & 1 == 1
        got_low = exchange(low, 1 << bit | 1)
        w = k * rank
        mine = jnp.concatenate([low[:, :w], got_low[:, :w]], axis=0)
        other = exchange(mine, 1)
        own_full = join(mine[:n], other[:n], half)
        got_full = join(mine[n:], other[n:], half)
        pairs[k] = jnp.concatenate(ordered(own_full, got_full, right), axis=0)
        low = low[:, w:] + got_low[:, w:]

    gathered = jnp.take(right_side, order % row_count, axis=1)
    is_left = lax.iota(jnp.int32, row_count) < leaf_split[0]
    leaf = jnp.where(is_left[:, None] == is_left[None, :], leaf_inverse, 0.0)
    current = dot(gathered, leaf)
    rows = current.shape[0]
    halves = jnp.concatenate(
        [jnp.where(is_left[None, :], current, 0.0), jnp.where(is_left[None, :], 0.0, current)], axis=0
    )
    w = dot(halves, basis_right[top])
    w = jnp.concatenate([w[:rows], w[rows:]], axis=1)
    z = dot(w, coupling[0, top])
    both = dot_nt(jnp.concatenate([z[:, :rank], z[:, rank:]], axis=0), basis_left[top])
    current = current - jnp.where(is_left[None, :], both[:rows], both[rows:])

    sums, send = split(dot(current, right_cols), half)
    got_sums = exchange(send, 1)
    chosen = []
    for bit in range(top):
        k = top - 1 - bit
        own = slice(k * rank, (k + 1) * rank)
        right = (device_id >> bit) & 1 == 1
        if bit > 0:
            got_sums = exchange(sums, 1 << bit | 1)
        left_sums, right_sums = ordered(sums, got_sums, right)
        z = dot(jnp.concatenate([left_sums[:, own], right_sums[:, own]], axis=1), coupling[0, k])
        side = jnp.where(right, z[:, rank:], z[:, :rank])
        chosen.append((side, jnp.where(right, z[:, :rank], z[:, rank:]) if bit == 0 else side))
        if k > 0:
            sums = sums[:, : k * rank] + got_sums[:, : k * rank] - dot(z, pairs[k])
    mine = jnp.concatenate([a for a, _ in chosen], axis=1)
    other = exchange(jnp.concatenate([b for _, b in chosen], axis=1), 1)
    z_all = join(mine, other, half)
    left_cols = jnp.concatenate([basis_left[top - 1 - bit] for bit in range(top)], axis=1)
    return current - dot_nt(z_all, left_cols)


def solution(mesh):
    in_specs = (
        P(None, AXES),
        P(AXES),
        P(AXES),
        P(AXES, None),
        P(None, AXES, None),
        P(None, AXES, None),
        P(AXES, None, None, None),
    )
    return jax.shard_map(
        per_device, mesh=mesh, in_specs=in_specs, out_specs=P(None, AXES), check_vma=False
    )
```

```python
import functools

import jax
import jax.numpy as jnp
from jax import lax
from jax.experimental import pallas as pl
from jax.experimental.pallas import tpu as pltpu
from jax.sharding import PartitionSpec as P

AXES = ("grp", "sub")
F32, BF16 = jnp.float32, jnp.bfloat16
NN = (((1,), (0,)), ((), ()))
NT = (((1,), (1,)), ((), ()))
TN = (((0,), (0,)), ((), ()))
ANY = pl.BlockSpec(memory_space=pl.ANY)
VMEM = pl.BlockSpec(memory_space=pltpu.VMEM)
SMEM = pl.BlockSpec(memory_space=pltpu.SMEM)
LIMIT = 40 * 1024 * 1024


def parts(x):
    high = x.astype(BF16)
    return high, (x - high.astype(F32)).astype(BF16)


def product(a, b, dims):
    return lax.dot_general(a, b, dims, preferred_element_type=F32)


def dot(a, b, dims=NN):
    ah, al = parts(a)
    bh, bl = parts(b)
    if dims[0][0] == (0,):
        return product(ah, bh, dims) + (product(al, bh, dims) + product(ah, bl, dims))
    rows = a.shape[0]
    both = product(jnp.concatenate([ah, al], axis=0), bh, dims)
    return both[:rows] + (both[rows:] + product(ah, bl, dims))


def parity_of(device_id, bits):
    parity = device_id & 1
    for bit in range(1, bits):
        parity = parity ^ ((device_id >> bit) & 1)
    return parity


def gram_kernel(top, left, right, low_keep, first, gram_top, left_v, right_v, sems):
    rank = left.shape[2]
    n = rank // 2
    copies = []
    for j in range(top - 1):
        cols = slice(j * rank, (j + 1) * rank)
        copies.append(pltpu.make_async_copy(right.at[j], right_v.at[:, cols], sems.at[0, j]))
        copies.append(pltpu.make_async_copy(left.at[j + 1], left_v.at[:, cols], sems.at[1, j]))
    for copy in copies:
        copy.start()
    for copy in copies:
        copy.wait()
    half = parity_of(lax.axis_index(AXES), top) == 1
    at = 0
    for k in range(top - 1, 0, -1):
        value = dot(left_v[:, (k - 1) * rank : k * rank], right_v[:, : k * rank], TN)
        w = k * rank
        if k == top - 1:
            gram_top[...] = value
            base = first.shape[1] - 2 * w
            first[:, base : base + w] = value[:n]
            first[:, base + w :] = value[n:]
        else:
            low_keep[:, at : at + w] = jnp.where(half, value[n:], value[:n])
            first[:, at : at + w] = jnp.where(half, value[:n], value[n:])
            at += w


def local_kernel(
    top, order, split, rhs, leaf, left, right, coupling, current_out, keep, send,
    rhs_v, leaf_v, left_v, right_top, right_v, coupling_v, sems,
):
    rank = left.shape[2]
    count, size = rhs_v.shape
    device_id = lax.axis_index(AXES)
    c_rhs = pltpu.make_async_copy(rhs, rhs_v, sems.at[0])
    c_leaf = pltpu.make_async_copy(leaf, leaf_v, sems.at[1])
    c_rtop = pltpu.make_async_copy(right.at[top], right_top, sems.at[2])
    c_coup = pltpu.make_async_copy(coupling.at[0, top], coupling_v, sems.at[3])
    c_left = pltpu.make_async_copy(left.at[top], left_v, sems.at[4])
    c_right = [
        pltpu.make_async_copy(right.at[j], right_v.at[:, j * rank : (j + 1) * rank], sems.at[5 + j])
        for j in range(top)
    ]
    for copy in [c_rhs, c_leaf, c_rtop, c_coup, c_left] + c_right:
        copy.start()
    local = order[...] - device_id * size
    pick = (lax.broadcasted_iota(jnp.int32, (size, size), 0) == local).astype(F32).astype(BF16)
    c_rhs.wait()
    high, low = parts(rhs_v[...])
    moved = product(jnp.concatenate([high, low], axis=0), pick, NN).astype(BF16)
    is_left = lax.broadcasted_iota(jnp.int32, (1, size), 1) < split[0]
    left_rows = lax.broadcasted_iota(jnp.int32, (size, 1), 0) < split[0]
    c_leaf.wait()
    lh, ll = parts(jnp.where(left_rows == is_left, leaf_v[...], 0.0))
    both = product(moved, lh, NN)
    current = both[:count] + (both[count:] + product(moved[:count], ll, NN))
    c_rtop.wait()
    halves = jnp.concatenate(
        [jnp.where(is_left, current, 0.0), jnp.where(is_left, 0.0, current)], axis=0
    )
    w = dot(halves, right_top[...])
    c_coup.wait()
    z = dot(jnp.concatenate([w[:count], w[count:]], axis=1), coupling_v[...])
    c_left.wait()
    update = dot(jnp.concatenate([z[:, :rank], z[:, rank:]], axis=0), left_v[...], NT)
    current = current - jnp.where(is_left, update[:count], update[count:])
    current_out[...] = current
    for copy in c_right:
        copy.wait()
    sums = dot(current, right_v[...])
    half = parity_of(device_id, top) == 1
    n = count // 2
    keep[...] = jnp.where(half, sums[n:], sums[:n])
    send[...] = jnp.where(half, sums[:n], sums[n:])


def pair_kernel_top(gram_top, low_keep, first, coupling, d_out, low_out, pair):
    rank, w = gram_top.shape
    n = rank // 2
    right = lax.axis_index(AXES) & 1
    low_w = low_keep.shape[1]
    low_out[...] = low_keep[...] + first[:, :low_w]
    own, got = pl.multiple_of(right * rank, rank), pl.multiple_of((1 - right) * rank, rank)
    pair[pl.ds(own, rank), :] = gram_top[...]
    pair[pl.ds(got, n), :] = first[:, low_w : low_w + w]
    pair[pl.ds(got + n, n), :] = first[:, low_w + w :]
    d_out[...] = dot(coupling[...], pair[...])


def pair_kernel(top, bit, mine, other, coupling, d_out, pair):
    n, rank = mine.shape[0] // 2, mine.shape[0]
    device_id = lax.axis_index(AXES)
    half = parity_of(device_id, top)
    right = (device_id >> bit) & 1
    for child, rows in ((right, slice(0, n)), (1 - right, slice(n, 2 * n))):
        pair[pl.ds(pl.multiple_of(child * rank + half * n, n), n), :] = mine[rows, :]
        pair[pl.ds(pl.multiple_of(child * rank + (1 - half) * n, n), n), :] = other[rows, :]
    d_out[...] = dot(coupling[...], pair[...])


def last_kernel(top, current, mine, other, left, out, left_v, z_v, sems):
    rank = left.shape[2]
    copies = [
        pltpu.make_async_copy(left.at[j], left_v.at[:, j * rank : (j + 1) * rank], sems.at[j])
        for j in range(top)
    ]
    for copy in copies:
        copy.start()
    half = parity_of(lax.axis_index(AXES), top)
    n = mine.shape[0]
    z_v[pl.ds(pl.multiple_of(half * n, n), n), :] = mine[...]
    z_v[pl.ds(pl.multiple_of((1 - half) * n, n), n), :] = other[...]
    for copy in copies:
        copy.wait()
    out[...] = current[...] - dot(z_v[...], left_v[...], NT)


def call(kernel, outs, in_specs, out_specs, scratch, *args):
    return pl.pallas_call(
        kernel,
        out_shape=outs,
        in_specs=in_specs,
        out_specs=out_specs,
        scratch_shapes=scratch,
        compiler_params=pltpu.CompilerParams(vmem_limit_bytes=LIMIT),
    )(*args)


def shape(*dims):
    return jax.ShapeDtypeStruct(dims, F32)


def xdot(a, b):
    return jnp.dot(a, b, precision=lax.Precision.HIGH, preferred_element_type=F32)


def exchange(value, mask):
    return lax.ppermute(value, AXES, [(i, i ^ mask) for i in range(lax.axis_size(AXES))])


def ordered(own, got, on_right):
    return jnp.where(on_right, got, own), jnp.where(on_right, own, got)


def per_device(right_side, order, leaf_split, leaf_inverse, basis_left, basis_right, coupling):
    count, size = right_side.shape
    rank = basis_left.shape[2]
    top = basis_left.shape[0] - 1
    n = rank // 2
    device_id = lax.axis_index(AXES)
    low_w = rank * (top - 1) * (top - 2) // 2
    top_w = (top - 1) * rank
    dma = pltpu.SemaphoreType.DMA
    low_keep, first, gram_top = call(
        functools.partial(gram_kernel, top),
        [shape(n, low_w), shape(n, low_w + 2 * top_w), shape(rank, top_w)],
        [ANY, ANY],
        [VMEM] * 3,
        [pltpu.VMEM((size, top_w), F32), pltpu.VMEM((size, top_w), F32), dma((2, top - 1))],
        basis_left,
        basis_right,
    )
    got_first = exchange(first, 1)
    current, keep, send = call(
        functools.partial(local_kernel, top),
        [shape(count, size), shape(count // 2, top * rank), shape(count // 2, top * rank)],
        [VMEM, SMEM, ANY, ANY, ANY, ANY, ANY],
        [VMEM] * 3,
        [
            pltpu.VMEM((count, size), F32),
            pltpu.VMEM((size, size), F32),
            pltpu.VMEM((size, rank), F32),
            pltpu.VMEM((size, rank), F32),
            pltpu.VMEM((size, top * rank), F32),
            pltpu.VMEM((2 * rank, 2 * rank), F32),
            dma((5 + top,)),
        ],
        order.reshape(1, size),
        leaf_split,
        right_side,
        leaf_inverse,
        basis_left,
        basis_right,
        coupling,
    )
    got_sums = exchange(send, 1)
    factors = {}
    factors[top - 1], low = call(
        pair_kernel_top,
        [shape(2 * rank, top_w), shape(n, low_w)],
        [VMEM] * 4,
        [VMEM] * 2,
        [pltpu.VMEM((2 * rank, top_w), F32)],
        gram_top,
        low_keep,
        got_first,
        coupling[0, top - 1],
    )
    for k in range(top - 2, 0, -1):
        bit = top - 1 - k
        got_low = exchange(low, 1 << bit | 1)
        w = k * rank
        mine = jnp.concatenate([low[:, :w], got_low[:, :w]], axis=0)
        other = exchange(mine, 1)
        factors[k] = call(
            functools.partial(pair_kernel, top, bit),
            shape(2 * rank, w),
            [VMEM] * 3,
            VMEM,
            [pltpu.VMEM((2 * rank, w), F32)],
            mine,
            other,
            coupling[0, k],
        )
        low = low[:, w:] + got_low[:, w:]

    sums = keep
    chosen = []
    for bit in range(top):
        k = top - 1 - bit
        own = slice(k * rank, (k + 1) * rank)
        right = (device_id >> bit) & 1 == 1
        if bit > 0:
            got_sums = exchange(sums, 1 << bit | 1)
        left_sums, right_sums = ordered(sums[:, own], got_sums[:, own], right)
        w = jnp.concatenate([left_sums, right_sums], axis=1)
        z = xdot(w, coupling[0, k])
        side = jnp.where(right, z[:, rank:], z[:, :rank])
        chosen.append((side, jnp.where(right, z[:, :rank], z[:, rank:]) if bit == 0 else side))
        if k > 0:
            sums = sums[:, : k * rank] + got_sums[:, : k * rank] - xdot(w, factors[k])
    mine = jnp.concatenate([a for a, _ in chosen[::-1]], axis=1)
    other = exchange(jnp.concatenate([b for _, b in chosen[::-1]], axis=1), 1)
    return call(
        functools.partial(last_kernel, top),
        shape(count, size),
        [VMEM, VMEM, VMEM, ANY],
        VMEM,
        [pltpu.VMEM((size, top * rank), F32), pltpu.VMEM((count, top * rank), F32), dma((top,))],
        current,
        mine,
        other,
        basis_left,
    )


def solution(mesh):
    in_specs = (
        P(None, AXES),
        P(AXES),
        P(AXES),
        P(AXES, None),
        P(None, AXES, None),
        P(None, AXES, None),
        P(AXES, None, None, None),
    )
    return jax.shard_map(
        per_device, mesh=mesh, in_specs=in_specs, out_specs=P(None, AXES), check_vma=False
    )
```

```python
import functools

import jax
import jax.numpy as jnp
from jax import lax
from jax.experimental import pallas as pl
from jax.experimental.pallas import tpu as pltpu
from jax.sharding import PartitionSpec as P

AXES = ("grp", "sub")
F32, BF16 = jnp.float32, jnp.bfloat16
NN = (((1,), (0,)), ((), ()))
NT = (((1,), (1,)), ((), ()))
TN = (((0,), (0,)), ((), ()))
HBM = pl.BlockSpec(memory_space=pltpu.HBM)
VMEM = pl.BlockSpec(memory_space=pltpu.VMEM)
SMEM = pl.BlockSpec(memory_space=pltpu.SMEM)
LIMIT = 24 * 1024 * 1024


def parts(x):
    high = x.astype(BF16)
    return high, (x - high.astype(F32)).astype(BF16)


def product(a, b, dims):
    return lax.dot_general(a, b, dims, preferred_element_type=F32)


def dot(a, b, dims=NN):
    ah, al = parts(a)
    bh, bl = parts(b)
    if dims[0][0] == (0,):
        return product(ah, bh, dims) + (product(al, bh, dims) + product(ah, bl, dims))
    rows = a.shape[0]
    both = product(jnp.concatenate([ah, al], axis=0), bh, dims)
    return both[:rows] + (both[rows:] + product(ah, bl, dims))


def parity_of(device_id, bits):
    parity = device_id & 1
    for bit in range(1, bits):
        parity = parity ^ ((device_id >> bit) & 1)
    return parity


def gram_kernel(
    top, left, right, coupling, rhs, leaf, low_keep, low_send, left_v, right_v, left_top, right_top,
    coupling_v, rhs_v, leaf_v, sems,
):
    rank = left.shape[2]
    n = rank // 2

    def cols(j):
        return slice(j * rank, (j + 1) * rank)

    used = []
    for j in range(top - 2):
        used.append(pltpu.make_async_copy(left.at[j + 1], left_v.at[:, cols(j + 1)], sems.at[0, j]))
        used.append(pltpu.make_async_copy(right.at[j], right_v.at[:, cols(j)], sems.at[1, j]))
    rest = [
        pltpu.make_async_copy(rhs, rhs_v, sems.at[2, 0]),
        pltpu.make_async_copy(leaf, leaf_v, sems.at[2, 1]),
        pltpu.make_async_copy(right.at[top], right_top, sems.at[2, 2]),
        pltpu.make_async_copy(coupling.at[0], coupling_v, sems.at[2, 3]),
        pltpu.make_async_copy(left.at[top], left_top, sems.at[2, 4]),
        pltpu.make_async_copy(left.at[0], left_v.at[:, cols(0)], sems.at[3, 0]),
        pltpu.make_async_copy(left.at[top - 1], left_v.at[:, cols(top - 1)], sems.at[3, 1]),
        pltpu.make_async_copy(right.at[top - 2], right_v.at[:, cols(top - 2)], sems.at[3, 2]),
        pltpu.make_async_copy(right.at[top - 1], right_v.at[:, cols(top - 1)], sems.at[3, 3]),
    ]
    for copy in used + rest:
        copy.start()
    for copy in used:
        copy.wait()
    half = parity_of(lax.axis_index(AXES), top) == 1
    at = 0
    for k in range(top - 2, 0, -1):
        w = k * rank
        value = dot(left_v[:, cols(k)], right_v[:, :w], TN)
        low_keep[:, at : at + w] = jnp.where(half, value[n:], value[:n])
        low_send[:, at : at + w] = jnp.where(half, value[:n], value[n:])
        at += w
    for copy in rest:
        copy.wait()


def leaf_kernel(top, order, split, rhs, leaf, left, right, current, gram_top):
    rank = left.shape[1] // top
    count, size = rhs.shape
    local = order[...] - lax.axis_index(AXES) * size
    pick = (lax.broadcasted_iota(jnp.int32, (size, size), 0) == local).astype(F32).astype(BF16)
    high, low = parts(rhs[...])
    moved = product(jnp.concatenate([high, low], axis=0), pick, NN).astype(BF16)
    is_left = lax.broadcasted_iota(jnp.int32, (1, size), 1) < split[0]
    left_rows = lax.broadcasted_iota(jnp.int32, (size, 1), 0) < split[0]
    lh, ll = parts(jnp.where(left_rows == is_left, leaf[...], 0.0))
    both = product(moved, lh, NN)
    current[...] = both[:count] + (both[count:] + product(moved[:count], ll, NN))
    w = (top - 1) * rank
    gram_top[...] = dot(left[:, w:], right[:, :w], TN)


def local_kernel(
    top, split, first, left_top, right_top, right, coupling, gram_top, current_out, keep, send
):
    rank = left_top.shape[1]
    count, size = first.shape
    current = first[...]
    is_left = lax.broadcasted_iota(jnp.int32, (1, size), 1) < split[0]
    halves = jnp.concatenate(
        [jnp.where(is_left, current, 0.0), jnp.where(is_left, 0.0, current)], axis=0
    )
    w = dot(halves, right_top[...])
    z = dot(jnp.concatenate([w[:count], w[count:]], axis=1), coupling[top])
    update = dot(jnp.concatenate([z[:, :rank], z[:, rank:]], axis=0), left_top[...], NT)
    current = current - jnp.where(is_left, update[:count], update[count:])
    current_out[...] = current
    sums = dot(current, right[...])
    half = parity_of(lax.axis_index(AXES), top) == 1
    n = count // 2
    keep[...] = jnp.where(half, sums[n:], sums[:n])
    send[:, : top * rank] = jnp.where(half, sums[:n], sums[n:])
    at = top * rank
    for row in range(0, rank, n):
        send[:, at : at + (top - 1) * rank] = gram_top[row : row + n, :]
        at += (top - 1) * rank


def top_kernel(top, keep, got, gram_top, coupling, sums, z_mine, z_other, pair):
    n, rank = keep.shape[0], gram_top.shape[0]
    w = (top - 1) * rank
    right = lax.axis_index(AXES) & 1
    own_at, got_at = right * rank, (1 - right) * rank
    pair[pl.ds(pl.multiple_of(own_at, rank), rank), :] = gram_top[...]
    at = top * rank
    for row in range(0, rank, n):
        pair[pl.ds(pl.multiple_of(got_at + row, n), n), :] = got[:, at : at + w]
        at += w
    mine, other = keep[:, w:], got[:, w : top * rank]
    is_right = right == 1
    both = jnp.concatenate(
        [jnp.where(is_right, other, mine), jnp.where(is_right, mine, other)], axis=1
    )
    z = dot(both, coupling[top - 1])
    sums[...] = keep[:, :w] + got[:, :w] - dot(z, pair[...])
    z_mine[...] = jnp.where(is_right, z[:, rank:], z[:, :rank])
    z_other[...] = jnp.where(is_right, z[:, :rank], z[:, rank:])


def pair_kernel(top, bit, mine, other, coupling, d_out, pair):
    n, rank = mine.shape[0] // 2, mine.shape[0]
    device_id = lax.axis_index(AXES)
    half = parity_of(device_id, top)
    right = (device_id >> bit) & 1
    for child, rows in ((right, slice(0, n)), (1 - right, slice(n, 2 * n))):
        pair[pl.ds(pl.multiple_of(child * rank + half * n, n), n), :] = mine[rows, :]
        pair[pl.ds(pl.multiple_of(child * rank + (1 - half) * n, n), n), :] = other[rows, :]
    d_out[...] = dot(coupling[top - 1 - bit], pair[...])


def joined(mine, other, top):
    half = parity_of(lax.axis_index(AXES), top) == 1
    return jnp.concatenate(
        [jnp.where(half, other, mine), jnp.where(half, mine, other)], axis=0
    )


def early_kernel(top, current, mine, other, left, coupling, out, factor):
    rank = left.shape[1] // top
    z = joined(mine[...], other[...], top)
    out[...] = current[...] - dot(z, left[:, rank:], NT)
    right = (lax.axis_index(AXES) >> (top - 1)) & 1 == 1
    side = jnp.where(right, coupling[0, :, rank:], coupling[0, :, :rank])
    factor[...] = dot(side, left[:, :rank], NT)


def last_kernel(top, current, mine, other, factor, out):
    out[...] = current[...] - dot(joined(mine[...], other[...], top), factor[...])


def call(kernel, outs, in_specs, out_specs, scratch, *args):
    return pl.pallas_call(
        kernel,
        out_shape=outs,
        in_specs=in_specs,
        out_specs=out_specs,
        scratch_shapes=scratch,
        compiler_params=pltpu.CompilerParams(vmem_limit_bytes=LIMIT),
    )(*args)


def shape(*dims):
    return jax.ShapeDtypeStruct(dims, F32)


def xdot(a, b):
    return jnp.dot(a, b, precision=lax.Precision.HIGH, preferred_element_type=F32)


def exchange(value, mask):
    return lax.ppermute(value, AXES, [(i, i ^ mask) for i in range(lax.axis_size(AXES))])


def level_sums(sums, got, k, rank, on_right):
    own, other = sums[:, k * rank :], got[:, k * rank :]
    both = jnp.concatenate(
        [jnp.where(on_right, other, own), jnp.where(on_right, own, other)], axis=1
    )
    return both, lambda z: jnp.where(on_right, z[:, rank:], z[:, :rank])


def per_device(right_side, order, leaf_split, leaf_inverse, basis_left, basis_right, coupling):
    count, size = right_side.shape
    rank = basis_left.shape[2]
    levels = basis_left.shape[0]
    top = levels - 1
    n = rank // 2
    device_id = lax.axis_index(AXES)
    low_w = rank * (top - 1) * (top - 2) // 2
    wide = top * rank
    rows = count // 2
    low_keep, low_send, left, right, left_top, right_top, coup, rhs, leaf = call(
        functools.partial(gram_kernel, top),
        [
            shape(n, low_w),
            shape(n, low_w),
            shape(size, wide),
            shape(size, wide),
            shape(size, rank),
            shape(size, rank),
            shape(levels, 2 * rank, 2 * rank),
            shape(count, size),
            shape(size, size),
        ],
        [HBM] * 5,
        [VMEM] * 9,
        [pltpu.SemaphoreType.DMA((4, max(5, top)))],
        *[
            pltpu.with_memory_space_constraint(x, pltpu.HBM)
            for x in (basis_left, basis_right, coupling, right_side, leaf_inverse)
        ],
    )
    got_low = exchange(low_send, 1)
    current, gram_top = call(
        functools.partial(leaf_kernel, top),
        [shape(count, size), shape(rank, wide - rank)],
        [VMEM, SMEM] + [VMEM] * 4,
        [VMEM] * 2,
        [],
        order.reshape(1, size),
        leaf_split,
        rhs,
        leaf,
        left,
        right,
    )
    low = low_keep + got_low
    current, low = lax.optimization_barrier((current, low))
    current, keep, send = call(
        functools.partial(local_kernel, top),
        [shape(count, size), shape(rows, wide), shape(rows, wide + rank // rows * (wide - rank))],
        [SMEM] + [VMEM] * 6,
        [VMEM] * 3,
        [],
        leaf_split,
        current,
        left_top,
        right_top,
        right,
        coup,
        gram_top,
    )
    got = exchange(send, 1)
    sums, z_mine, z_other = call(
        functools.partial(top_kernel, top),
        [shape(rows, wide - rank), shape(rows, rank), shape(rows, rank)],
        [VMEM] * 4,
        [VMEM] * 3,
        [pltpu.VMEM((2 * rank, wide - rank), F32)],
        keep,
        got,
        gram_top,
        coup,
    )
    z_mine, z_other = [z_mine], [z_other]
    for k in range(top - 2, 0, -1):
        bit = top - 1 - k
        w = k * rank
        got_low = exchange(low, 1 << bit | 1)
        got_sums = exchange(sums, 1 << bit | 1)
        mine = jnp.concatenate([low[:, :w], got_low[:, :w]], axis=0)
        other = exchange(mine, 1)
        factor = call(
            functools.partial(pair_kernel, top, bit),
            shape(2 * rank, w),
            [VMEM] * 3,
            VMEM,
            [pltpu.VMEM((2 * rank, w), F32)],
            mine,
            other,
            coup,
        )
        next_low = low[:, w:] + got_low[:, w:]
        both, side = level_sums(sums, got_sums, k, rank, (device_id >> bit) & 1 == 1)
        z = xdot(both, coup[k])
        z_mine.append(side(z))
        z_other.append(z_mine[-1])
        sums = sums[:, :w] + got_sums[:, :w] - xdot(both, factor)
        if k > 1:
            low, sums = lax.optimization_barrier((next_low, sums))
    got_sums = exchange(sums, 1 << (top - 1) | 1)
    mine = jnp.concatenate(z_mine[::-1], axis=1)
    other = exchange(jnp.concatenate(z_other[::-1], axis=1), 1)
    current, factor = call(
        functools.partial(early_kernel, top),
        [shape(count, size), shape(2 * rank, size)],
        [VMEM] * 5,
        [VMEM] * 2,
        [],
        current,
        mine,
        other,
        left,
        coup,
    )
    both, _ = level_sums(sums, got_sums, 0, rank, (device_id >> (top - 1)) & 1 == 1)
    return call(
        functools.partial(last_kernel, top),
        shape(count, size),
        [VMEM] * 4,
        VMEM,
        [],
        current,
        both,
        exchange(both, 1),
        factor,
    )


def solution(mesh):
    in_specs = (
        P(None, AXES),
        P(AXES),
        P(AXES),
        P(AXES, None),
        P(None, AXES, None),
        P(None, AXES, None),
        P(AXES, None, None, None),
    )
    return jax.shard_map(
        per_device, mesh=mesh, in_specs=in_specs, out_specs=P(None, AXES), check_vma=False
    )
```

```python
import functools

import jax
import jax.numpy as jnp
from jax import lax
from jax.experimental import pallas as pl
from jax.experimental.pallas import tpu as pltpu
from jax.sharding import PartitionSpec as P

AXES = ("grp", "sub")
F32, BF16 = jnp.float32, jnp.bfloat16
NN = (((1,), (0,)), ((), ()))
NT = (((1,), (1,)), ((), ()))
TN = (((0,), (0,)), ((), ()))
ANY = pl.BlockSpec(memory_space=pl.ANY)
HBM = pl.BlockSpec(memory_space=pltpu.HBM)
VMEM = pl.BlockSpec(memory_space=pltpu.VMEM)
SMEM = pl.BlockSpec(memory_space=pltpu.SMEM)
LIMIT = 24 * 1024 * 1024


def parts(x):
    high = x.astype(BF16)
    return high, (x - high.astype(F32)).astype(BF16)


def product(a, b, dims):
    return lax.dot_general(a, b, dims, preferred_element_type=F32)


def dot(a, b, dims=NN):
    ah, al = parts(a)
    bh, bl = parts(b)
    if dims[0][0] == (0,):
        return product(ah, bh, dims) + (product(al, bh, dims) + product(ah, bl, dims))
    rows = a.shape[0]
    both = product(jnp.concatenate([ah, al], axis=0), bh, dims)
    return both[:rows] + (both[rows:] + product(ah, bl, dims))


def parity_of(device_id, bits):
    parity = device_id & 1
    for bit in range(1, bits):
        parity = parity ^ ((device_id >> bit) & 1)
    return parity


def gram_kernel(
    top, left, right, coupling, rhs, leaf, low_keep, send, gram_next, left_v, right_v, left_top, right_top,
    coupling_v, rhs_v, leaf_v, sems,
):
    rank = left.shape[2]
    n = rank // 2

    def cols(j):
        return slice(j * rank, (j + 1) * rank)

    used = []
    for j in range(top - 2):
        used.append(pltpu.make_async_copy(left.at[j + 1], left_v.at[:, cols(j + 1)], sems.at[0, j]))
        used.append(pltpu.make_async_copy(right.at[j], right_v.at[:, cols(j)], sems.at[1, j]))
    rest = [
        pltpu.make_async_copy(rhs, rhs_v, sems.at[2, 0]),
        pltpu.make_async_copy(leaf, leaf_v, sems.at[2, 1]),
        pltpu.make_async_copy(right.at[top], right_top, sems.at[2, 2]),
        pltpu.make_async_copy(coupling.at[0], coupling_v, sems.at[2, 3]),
        pltpu.make_async_copy(left.at[top], left_top, sems.at[2, 4]),
        pltpu.make_async_copy(left.at[0], left_v.at[:, cols(0)], sems.at[3, 0]),
        pltpu.make_async_copy(left.at[top - 1], left_v.at[:, cols(top - 1)], sems.at[3, 1]),
        pltpu.make_async_copy(right.at[top - 2], right_v.at[:, cols(top - 2)], sems.at[3, 2]),
        pltpu.make_async_copy(right.at[top - 1], right_v.at[:, cols(top - 1)], sems.at[3, 3]),
    ]
    for copy in used + rest:
        copy.start()
    for copy in used:
        copy.wait()
    half = parity_of(lax.axis_index(AXES), top) == 1
    for k in range(top - 2, 0, -1):
        w = k * rank
        value = dot(left_v[:, cols(k)], right_v[:, :w], TN)
        if k == top - 2:
            gram_next[...] = value
            send[:, :w] = value[:n]
            send[:, w : 2 * w] = value[n:]
            at, skip = 0, 2 * w
            continue
        low_keep[:, at : at + w] = jnp.where(half, value[n:], value[:n])
        send[:, skip + at : skip + at + w] = jnp.where(half, value[:n], value[n:])
        at += w
    for copy in rest:
        copy.wait()


def leaf_kernel(top, order, split, rhs, leaf, left, right, current, gram_top):
    rank = left.shape[1] // top
    count, size = rhs.shape
    local = order[...] - lax.axis_index(AXES) * size
    pick = (lax.broadcasted_iota(jnp.int32, (size, size), 0) == local).astype(F32).astype(BF16)
    high, low = parts(rhs[...])
    moved = product(jnp.concatenate([high, low], axis=0), pick, NN).astype(BF16)
    is_left = lax.broadcasted_iota(jnp.int32, (1, size), 1) < split[0]
    left_rows = lax.broadcasted_iota(jnp.int32, (size, 1), 0) < split[0]
    lh, ll = parts(jnp.where(left_rows == is_left, leaf[...], 0.0))
    both = product(moved, lh, NN)
    current[...] = both[:count] + (both[count:] + product(moved[:count], ll, NN))
    w = (top - 1) * rank
    gram_top[...] = dot(left[:, w:], right[:, :w], TN)


def local_kernel(
    top, split, first, left_top, right_top, right, coupling, gram_top, _, current_out, keep, send
):
    rank = left_top.shape[1]
    count, size = first.shape
    current = first[...]
    is_left = lax.broadcasted_iota(jnp.int32, (1, size), 1) < split[0]
    halves = jnp.concatenate(
        [jnp.where(is_left, current, 0.0), jnp.where(is_left, 0.0, current)], axis=0
    )
    w = dot(halves, right_top[...])
    z = dot(jnp.concatenate([w[:count], w[count:]], axis=1), coupling[top])
    update = dot(jnp.concatenate([z[:, :rank], z[:, rank:]], axis=0), left_top[...], NT)
    current = current - jnp.where(is_left, update[:count], update[count:])
    current_out[...] = current
    sums = dot(current, right[...])
    half = parity_of(lax.axis_index(AXES), top) == 1
    n = count // 2
    keep[...] = jnp.where(half, sums[n:], sums[:n])
    send[:, : top * rank] = jnp.where(half, sums[:n], sums[n:])
    at = top * rank
    for row in range(0, rank, n):
        send[:, at : at + (top - 1) * rank] = gram_top[row : row + n, :]
        at += (top - 1) * rank


def top_kernel(top, keep, got, gram_top, coupling, sums, next_sums, z_mine, z_other, pair):
    n, rank = keep.shape[0], gram_top.shape[0]
    w = (top - 1) * rank
    right = lax.axis_index(AXES) & 1
    own_at, got_at = right * rank, (1 - right) * rank
    pair[pl.ds(pl.multiple_of(own_at, rank), rank), :] = gram_top[...]
    at = top * rank
    for row in range(0, rank, n):
        pair[pl.ds(pl.multiple_of(got_at + row, n), n), :] = got[:, at : at + w]
        at += w
    mine, other = keep[:, w:], got[:, w : top * rank]
    is_right = right == 1
    both = jnp.concatenate(
        [jnp.where(is_right, other, mine), jnp.where(is_right, mine, other)], axis=1
    )
    z = dot(both, coupling[top - 1])
    value = keep[:, :w] + got[:, :w] - dot(z, pair[...])
    sums[...] = value[:, : w - rank]
    next_sums[...] = value[:, w - rank :]
    z_mine[...] = jnp.where(is_right, z[:, rank:], z[:, :rank])
    z_other[...] = jnp.where(is_right, z[:, :rank], z[:, rank:])


def next_kernel(top, mine, got, sums, gram_next, got_gram, coupling, z_out, sums_out):
    rank, w = gram_next.shape
    n = rank // 2
    right = (lax.axis_index(AXES) >> 1) & 1 == 1
    both = jnp.concatenate(
        [jnp.where(right, got[...], mine[...]), jnp.where(right, mine[...], got[...])], axis=1
    )
    k = top - 2
    z = dot(both, jnp.where(right, coupling[k, :, rank:], coupling[k, :, :rank]))
    gram = gram_next[...] + jnp.concatenate([got_gram[:, :w], got_gram[:, w : 2 * w]], axis=0)
    z_out[...] = z
    sums_out[...] = sums[...] - dot(z, gram)


def merge_kernel(low, got, _, mine):
    n, w = low.shape[0], mine.shape[1]
    mine[:n, :] = low[:, :w]
    mine[n:, :] = got[:, :w]


def pair_kernel(top, bit, low, got, other, coupling, d_out, *rest):
    (n, rank), w = (low.shape[0], 2 * low.shape[0]), d_out.shape[1]
    pair = rest[-1]
    device_id = lax.axis_index(AXES)
    half = parity_of(device_id, top)
    right = (device_id >> bit) & 1
    for child, value, rows in ((right, low, slice(0, n)), (1 - right, got, slice(n, 2 * n))):
        pair[pl.ds(pl.multiple_of(child * rank + half * n, n), n), :] = value[:, :w]
        pair[pl.ds(pl.multiple_of(child * rank + (1 - half) * n, n), n), :] = other[rows, :]
    d_out[...] = dot(coupling[top - 1 - bit], pair[...])
    if len(rest) > 1:
        rest[0][...] = low[:, w:] + got[:, w:]


def sums_kernel(bit, sums, got, factor, both, out):
    w = out.shape[1]
    on_right = (lax.axis_index(AXES) >> bit) & 1 == 1
    own, other = sums[:, w:], got[:, w:]
    pair = jnp.concatenate(
        [jnp.where(on_right, other, own), jnp.where(on_right, own, other)], axis=1
    )
    both[...] = pair
    out[...] = sums[:, :w] + got[:, :w] - dot(pair, factor[...])


def joined(mine, other, top):
    half = parity_of(lax.axis_index(AXES), top) == 1
    return jnp.concatenate(
        [jnp.where(half, other, mine), jnp.where(half, mine, other)], axis=0
    )


def early_kernel(top, current, *refs):
    left, coupling, out, factor = refs[-4:]
    rank = left.shape[1] // top
    device_id = lax.axis_index(AXES)

    def side(k):
        right = (device_id >> (top - 1 - k)) & 1 == 1
        return jnp.where(right, coupling[k, :, rank:], coupling[k, :, :rank])

    z = []
    for k in range(1, top):
        pair = joined(refs[2 * k - 2][...], refs[2 * k - 1][...], top)
        z.append(pair if k >= top - 2 else dot(pair, side(k)))
    out[...] = current[...] - dot(jnp.concatenate(z, axis=1), left[:, rank:], NT)
    factor[...] = dot(side(0), left[:, :rank], NT)


def last_kernel(top, current, mine, other, factor, out):
    out[...] = current[...] - dot(joined(mine[...], other[...], top), factor[...])


def call(kernel, outs, in_specs, out_specs, scratch, *args):
    return pl.pallas_call(
        kernel,
        out_shape=outs,
        in_specs=in_specs,
        out_specs=out_specs,
        scratch_shapes=scratch,
        cost_estimate=pl.CostEstimate(flops=1, bytes_accessed=1, transcendentals=0),
        compiler_params=pltpu.CompilerParams(vmem_limit_bytes=LIMIT),
    )(*args)


def shape(*dims):
    return jax.ShapeDtypeStruct(dims, F32)


def exchange(value, mask):
    return lax.ppermute(value, AXES, [(i, i ^ mask) for i in range(lax.axis_size(AXES))])


def per_device(right_side, order, leaf_split, leaf_inverse, basis_left, basis_right, coupling):
    count, size = right_side.shape
    rank = basis_left.shape[2]
    levels = basis_left.shape[0]
    top = levels - 1
    n = rank // 2
    device_id = lax.axis_index(AXES)
    low_w = rank * (top - 2) * (top - 3) // 2
    next_w = (top - 2) * rank
    wide = top * rank
    rows = count // 2
    low_keep, send, gram_next, left, right, left_top, right_top, coup, rhs, leaf = call(
        functools.partial(gram_kernel, top),
        [
            shape(n, low_w),
            shape(n, 2 * next_w + low_w),
            shape(rank, next_w),
            shape(size, wide),
            shape(size, wide),
            shape(size, rank),
            shape(size, rank),
            shape(levels, 2 * rank, 2 * rank),
            shape(count, size),
            shape(size, size),
        ],
        [HBM] * 5,
        [VMEM] * 10,
        [pltpu.SemaphoreType.DMA((4, max(5, top)))],
        *[
            pltpu.with_memory_space_constraint(x, pltpu.HBM)
            for x in (basis_left, basis_right, coupling, right_side, leaf_inverse)
        ],
    )
    got_gram = exchange(send, 1)
    current, gram_top = call(
        functools.partial(leaf_kernel, top),
        [shape(count, size), shape(rank, wide - rank)],
        [VMEM, SMEM] + [VMEM] * 4,
        [VMEM] * 2,
        [],
        order.reshape(1, size),
        leaf_split,
        rhs,
        leaf,
        left,
        right,
    )
    low = low_keep + got_gram[:, 2 * next_w :]
    current, keep, send = call(
        functools.partial(local_kernel, top),
        [shape(count, size), shape(rows, wide), shape(rows, wide + rank // rows * (wide - rank))],
        [SMEM] + [VMEM] * 6 + [ANY],
        [VMEM] * 3,
        [],
        leaf_split,
        current,
        left_top,
        right_top,
        right,
        coup,
        gram_top,
        low,
    )
    got = exchange(send, 1)
    sums, next_sums, z_mine, z_other = call(
        functools.partial(top_kernel, top),
        [shape(rows, next_w), shape(rows, rank), shape(rows, rank), shape(rows, rank)],
        [VMEM] * 4,
        [VMEM] * 4,
        [pltpu.VMEM((2 * rank, wide - rank), F32)],
        keep,
        got,
        gram_top,
        coup,
    )
    known = {top - 1: (z_mine, z_other)}
    got_low = exchange(low, 3)
    z, sums = call(
        functools.partial(next_kernel, top),
        [shape(rows, rank), shape(rows, next_w)],
        [VMEM] * 6,
        [VMEM] * 2,
        [],
        next_sums,
        exchange(next_sums, 3),
        sums,
        gram_next,
        got_gram,
        coup,
    )
    known[top - 2] = (z, z)
    sums = sums + exchange(sums, 3)
    low = low + got_low
    for k in range(top - 3, 0, -1):
        bit = top - 1 - k
        w = k * rank
        got_sums = exchange(sums, 1 << bit | 1)
        got_low = exchange(low, 1 << bit | 1)
        mine = call(
            merge_kernel, shape(rank, w), [VMEM, VMEM, ANY], VMEM, [], low, got_low, got_sums
        )
        outs = [shape(2 * rank, w), shape(n, low.shape[1] - w)][: 2 if k > 1 else 1]
        factor, *low = call(
            functools.partial(pair_kernel, top, bit),
            outs,
            [VMEM] * 4,
            [VMEM] * len(outs),
            [pltpu.VMEM((2 * rank, w), F32)],
            low,
            got_low,
            exchange(mine, 1),
            coup,
        )
        low = low[0] if low else None
        both, sums = call(
            functools.partial(sums_kernel, bit),
            [shape(rows, 2 * rank), shape(rows, w)],
            [VMEM] * 3,
            [VMEM] * 2,
            [],
            sums,
            got_sums,
            factor,
        )
        known[k] = (both, both)
    got_sums = exchange(sums, 1 << (top - 1) | 1)
    names = range(1, top)
    others = exchange(jnp.concatenate([known[k][1] for k in names], axis=1), 1)
    args, at = [], 0
    for k in names:
        mine = known[k][0]
        args += [mine, others[:, at : at + mine.shape[1]]]
        at += mine.shape[1]
    current, factor = call(
        functools.partial(early_kernel, top),
        [shape(count, size), shape(2 * rank, size)],
        [VMEM] * (3 + len(args)),
        [VMEM] * 2,
        [],
        current,
        *args,
        left,
        coup,
    )
    on_right = (device_id >> (top - 1)) & 1 == 1
    both = jnp.concatenate(
        [jnp.where(on_right, got_sums, sums), jnp.where(on_right, sums, got_sums)], axis=1
    )
    return call(
        functools.partial(last_kernel, top),
        shape(count, size),
        [VMEM] * 4,
        VMEM,
        [],
        current,
        both,
        exchange(both, 1),
        factor,
    )


def solution(mesh):
    in_specs = (
        P(None, AXES),
        P(AXES),
        P(AXES),
        P(AXES, None),
        P(None, AXES, None),
        P(None, AXES, None),
        P(AXES, None, None, None),
    )
    return jax.shard_map(
        per_device, mesh=mesh, in_specs=in_specs, out_specs=P(None, AXES), check_vma=False
    )
```

```python
import functools

import jax
import jax.numpy as jnp
from jax import lax
from jax.experimental import pallas as pl
from jax.experimental.pallas import tpu as pltpu
from jax.sharding import PartitionSpec as P

AXES = ("grp", "sub")
F32, BF16 = jnp.float32, jnp.bfloat16
NN = (((1,), (0,)), ((), ()))
NT = (((1,), (1,)), ((), ()))
TN = (((0,), (0,)), ((), ()))
ANY = pl.BlockSpec(memory_space=pl.ANY)
HBM = pl.BlockSpec(memory_space=pltpu.HBM)
VMEM = pl.BlockSpec(memory_space=pltpu.VMEM)
LIMIT = 24 * 1024 * 1024


def parts(x):
    high = x.astype(BF16)
    return high, (x - high.astype(F32)).astype(BF16)


def product(a, b, dims):
    return lax.dot_general(a, b, dims, preferred_element_type=F32)


def dot(a, b, dims=NN):
    if dims == TN:
        a, dims = a.T, NN
    ah, al = parts(a)
    bh, bl = parts(b)
    rows = a.shape[0]
    both = product(jnp.concatenate([ah, al], axis=0), bh, dims)
    return both[:rows] + (both[rows:] + product(ah, bl, dims))


def parity_of(device_id, bits):
    parity = device_id & 1
    for bit in range(1, bits):
        parity = parity ^ ((device_id >> bit) & 1)
    return parity


def low_kernel(
    top, left, right, rhs, leaf, order, keep, send, left_v, right_v, rhs_v, leaf_v, order_v, sems,
):
    rank = left.shape[2]
    n = rank // 2
    count = top - 3
    bases = []
    for j in range(count):
        cols = slice(j * rank, (j + 1) * rank)
        bases.append(pltpu.make_async_copy(left.at[j + 1], left_v.at[:, cols], sems.at[0, j]))
        bases.append(pltpu.make_async_copy(right.at[j], right_v.at[:, cols], sems.at[1, j]))
    rest = [
        pltpu.make_async_copy(order, order_v, sems.at[2, 1]),
        pltpu.make_async_copy(rhs, rhs_v, sems.at[2, 2]),
        pltpu.make_async_copy(leaf, leaf_v, sems.at[2, 3]),
    ]
    for copy in bases + rest:
        copy.start()
    for copy in bases:
        copy.wait()
    half = parity_of(lax.axis_index(AXES), top) == 1
    grams = dot(left_v[...], right_v[...], TN)
    at = 0
    for k in range(count, 0, -1):
        w = k * rank
        value = grams[w - rank : w, :w]
        keep[:, at : at + w] = jnp.where(half, value[n:], value[:n])
        send[:, at : at + w] = jnp.where(half, value[:n], value[n:])
        at += w
    for copy in rest:
        copy.wait()


def sides(split, size):
    border = split[...]
    return (
        lax.broadcasted_iota(jnp.int32, (1, size), 1) < border,
        lax.broadcasted_iota(jnp.int32, (size, 1), 0) < border,
    )


def leaf_kernel(
    top, order, split, rhs, leaf, right_low, left, right, coupling, current, gram_top, gram_next,
    left_v, right_v, left_top, right_top, coupling_v, sems,
):
    rank = left_top.shape[1]
    count, size = rhs.shape
    copies = [
        pltpu.make_async_copy(left.at[top - 2], left_v.at[:, rank : 2 * rank], sems.at[0]),
        pltpu.make_async_copy(left.at[top - 1], left_v.at[:, 2 * rank :], sems.at[1]),
        pltpu.make_async_copy(right.at[top - 3], right_v.at[:, :rank], sems.at[2]),
        pltpu.make_async_copy(right.at[top - 2], right_v.at[:, rank : 2 * rank], sems.at[3]),
        pltpu.make_async_copy(right.at[top], right_top, sems.at[4]),
        pltpu.make_async_copy(coupling.at[0], coupling_v, sems.at[5]),
        pltpu.make_async_copy(left.at[top], left_top, sems.at[6]),
        pltpu.make_async_copy(right.at[top - 1], right_v.at[:, 2 * rank :], sems.at[7]),
        pltpu.make_async_copy(left.at[0], left_v.at[:, :rank], sems.at[8]),
    ]
    for copy in copies:
        copy.start()
    local = order[...] - lax.axis_index(AXES) * size
    pick = (lax.broadcasted_iota(jnp.int32, (size, size), 0) == local).astype(F32).astype(BF16)
    high, low = parts(rhs[...])
    moved = product(jnp.concatenate([high, low], axis=0), pick, NN).astype(BF16)
    columns, rows = sides(split, size)
    lh, ll = parts(jnp.where(rows == columns, leaf[...], 0.0))
    both = product(moved, lh, NN)
    current[...] = both[:count] + (both[count:] + product(moved[:count], ll, NN))
    for copy in copies[:4]:
        copy.wait()
    low_w = right_low.shape[1]
    upper = left_v[:, rank:]
    value = dot(upper, right_low[...], TN)
    gram_next[:, :low_w] = value[:rank]
    gram_top[:, :low_w] = value[rank:]
    value = dot(upper, right_v[:, : 2 * rank], TN)
    gram_next[:, low_w:] = value[:rank, :rank]
    gram_top[:, low_w:] = value[rank:]
    for copy in copies[4:]:
        copy.wait()


def put_rows(out, at, value):
    rows, w = out.shape[0], value.shape[1]
    for row in range(0, value.shape[0], rows):
        out[:, at : at + w] = value[row : row + rows, :]
        at += w
    return at


def take_rows(packed, at, height, w):
    rows = packed.shape[0]
    return jnp.concatenate(
        [packed[:, at + i * w : at + (i + 1) * w] for i in range(height // rows)], axis=0
    )


def local_kernel(
    top, split, first, left_top, right_top, right_low, right_v, coupling, gram_top, gram_next, _,
    current_out, keep, send,
):
    rank = left_top.shape[1]
    count, size = first.shape
    current = first[...]
    is_left, _ = sides(split, size)
    halves = jnp.concatenate(
        [jnp.where(is_left, current, 0.0), jnp.where(is_left, 0.0, current)], axis=0
    )
    w = dot(halves, right_top[...])
    z = dot(jnp.concatenate([w[:count], w[count:]], axis=1), coupling[top])
    update = dot(jnp.concatenate([z[:, :rank], z[:, rank:]], axis=0), left_top[...], NT)
    current = current - jnp.where(is_left, update[:count], update[count:])
    current_out[...] = current
    half = parity_of(lax.axis_index(AXES), top) == 1
    n = count // 2
    at = 0
    for basis in (right_low, right_v):
        sums = dot(current, basis[...])
        w = basis.shape[1]
        keep[:, at : at + w] = jnp.where(half, sums[n:], sums[:n])
        send[:, at : at + w] = jnp.where(half, sums[:n], sums[n:])
        at += w
    at = put_rows(send, at, gram_top[...])
    put_rows(send, at, gram_next[...])


def beside(own, got, on_right):
    return jnp.concatenate(
        [jnp.where(on_right, got, own), jnp.where(on_right, own, got)], axis=1
    )


def top_kernel(top, keep, got, gram_top, coupling, sums, next_sums, z_mine, z_other, pair):
    rank = gram_top.shape[0]
    w = (top - 1) * rank
    right = lax.axis_index(AXES) & 1
    own_at, got_at = right * rank, (1 - right) * rank
    pair[pl.ds(pl.multiple_of(own_at, rank), rank), :] = gram_top[...]
    pair[pl.ds(pl.multiple_of(got_at, rank), rank), :] = take_rows(got, top * rank, rank, w)
    is_right = right == 1
    z = dot(beside(keep[:, w:], got[:, w : top * rank], is_right), coupling[top - 1])
    value = keep[:, :w] + got[:, :w] - dot(z, pair[...])
    sums[...] = value[:, : w - rank]
    next_sums[...] = value[:, w - rank :]
    z_mine[...] = jnp.where(is_right, z[:, rank:], z[:, :rank])
    z_other[...] = jnp.where(is_right, z[:, :rank], z[:, rank:])


def side_of(coupling, k, right):
    rank = coupling.shape[2] // 2
    return jnp.where(right, coupling[k, :, rank:], coupling[k, :, :rank])


def next_kernel(top, mine, got, sums, gram_next, got_gram, coupling, z_out, sums_out):
    rank, w = gram_next.shape
    right = (lax.axis_index(AXES) >> 1) & 1 == 1
    z = dot(beside(mine[...], got[...], right), side_of(coupling, top - 2, right))
    at = top * rank + rank // got_gram.shape[0] * (w + rank)
    gram = gram_next[...] + take_rows(got_gram, at, rank, w)
    z_out[...] = z
    sums_out[...] = sums[...] - dot(z, gram)


def merge_kernel(last, low, got, _, mine, rest):
    lower = low.shape[1] - rest.shape[1]
    rest[...] = low[:, lower:] + got[:, lower:]
    mine[:, :lower] = low[:, :lower]
    mine[:, lower : 2 * lower] = got[:, :lower]
    if last:
        mine[:, 2 * lower :] = rest[...]


def couple_kernel(top, k, sums, got, coupling, both, z):
    rank = both.shape[1] // 2
    right = (lax.axis_index(AXES) >> (top - 1 - k)) & 1 == 1
    w = k * rank
    both[...] = beside(sums[:, w:], got[:, w:], right)
    z[...] = dot(both[...], coupling[k])


def level_kernel(top, k, sums, got, z, low, got_low, rest, other, out, pair):
    n = low.shape[0]
    rank, w = 2 * n, k * 2 * n
    bit = top - 1 - k
    device_id = lax.axis_index(AXES)
    half = parity_of(device_id, top)
    right = (device_id >> bit) & 1

    def put(child, mine, theirs):
        pair[pl.ds(pl.multiple_of(child * rank + half * n, n), n), :] = mine
        pair[pl.ds(pl.multiple_of(child * rank + (1 - half) * n, n), n), :] = theirs

    put(right, low[:, :w], other[:, :w])
    put(1 - right, got_low[:, :w], other[:, w : 2 * w])
    out[:, :w] = sums[:, :w] + got[:, :w] - dot(z[...], pair[...])
    if k == 2:
        mine, theirs = rest[...], other[:, 2 * w :]
        is_upper = half == 1
        gram = jnp.concatenate(
            [jnp.where(is_upper, theirs, mine), jnp.where(is_upper, mine, theirs)], axis=0
        )
        put_rows(out, w, gram)


def first_kernel(top, packed, got, coupling, out, both, pair):
    rank = out.shape[1]
    right = (lax.axis_index(AXES) >> (top - 2)) & 1
    for child, value in ((right, packed), (1 - right, got)):
        pair[pl.ds(pl.multiple_of(child * rank, rank), rank), :] = take_rows(
            value, 2 * rank, rank, rank
        )
    both[...] = beside(packed[:, rank : 2 * rank], got[:, rank : 2 * rank], right == 1)
    z = dot(both[...], coupling[1])
    out[...] = packed[:, :rank] + got[:, :rank] - dot(z, pair[...])


def joined(mine, other, top):
    half = parity_of(lax.axis_index(AXES), top) == 1
    return jnp.concatenate(
        [jnp.where(half, other, mine), jnp.where(half, mine, other)], axis=0
    )


def early_kernel(top, current, *refs):
    left_low, left_v, coupling, out, factor = refs[-5:]
    rank = left_v.shape[1] // 3
    device_id = lax.axis_index(AXES)
    z = []
    for k in range(1, top):
        pair = joined(refs[2 * k - 2][...], refs[2 * k - 1][...], top)
        right = (device_id >> (top - 1 - k)) & 1 == 1
        z.append(pair if k >= top - 2 else dot(pair, side_of(coupling, k, right)))
    low = dot(jnp.concatenate(z[: top - 3], axis=1), left_low[...], NT)
    high = dot(jnp.concatenate(z[top - 3 :], axis=1), left_v[:, rank:], NT)
    out[...] = current[...] - (low + high)
    right = (device_id >> (top - 1)) & 1 == 1
    factor[...] = dot(side_of(coupling, 0, right), left_v[:, :rank], NT)


def last_kernel(top, current, mine, other, factor, out):
    out[...] = current[...] - dot(joined(mine[...], other[...], top), factor[...])


def call(kernel, outs, in_specs, out_specs, scratch, *args):
    return pl.pallas_call(
        kernel,
        out_shape=outs,
        in_specs=in_specs,
        out_specs=out_specs,
        scratch_shapes=scratch,
        cost_estimate=pl.CostEstimate(flops=1, bytes_accessed=1, transcendentals=0),
        compiler_params=pltpu.CompilerParams(vmem_limit_bytes=LIMIT),
    )(*args)


def shape(*dims, dtype=F32):
    return jax.ShapeDtypeStruct(dims, dtype)


def in_hbm(*arrays):
    return [pltpu.with_memory_space_constraint(x, pltpu.HBM) for x in arrays]


def exchange(value, mask):
    return lax.ppermute(value, AXES, [(i, i ^ mask) for i in range(lax.axis_size(AXES))])


def per_device(right_side, order, leaf_split, leaf_inverse, basis_left, basis_right, coupling):
    count, size = right_side.shape
    levels, _, rank = basis_left.shape
    top = levels - 1
    n = rank // 2
    rows = count // 2
    wide = top * rank
    low_w = rank * (top - 2) * (top - 3) // 2
    next_w = (top - 2) * rank
    device_id = lax.axis_index(AXES)
    split = leaf_split.reshape(1, 1)
    keep, send, left_low, right_low, rhs, leaf, order = call(
        functools.partial(low_kernel, top),
        [
            shape(n, low_w),
            shape(n, low_w),
            shape(size, (top - 3) * rank),
            shape(size, (top - 3) * rank),
            shape(count, size),
            shape(size, size),
            shape(1, size, dtype=jnp.int32),
        ],
        [HBM] * 5,
        [VMEM] * 7,
        [pltpu.SemaphoreType.DMA((3, max(4, top - 3)))],
        *in_hbm(basis_left, basis_right, right_side, leaf_inverse, order.reshape(1, size)),
    )
    got_low = exchange(send, 1)
    current, gram_top, gram_next, left, right, left_top, right_top, coup = call(
        functools.partial(leaf_kernel, top),
        [
            shape(count, size),
            shape(rank, wide - rank),
            shape(rank, next_w),
            shape(size, 3 * rank),
            shape(size, 3 * rank),
            shape(size, rank),
            shape(size, rank),
            shape(levels, 2 * rank, 2 * rank),
        ],
        [VMEM] * 5 + [HBM] * 3,
        [VMEM] * 8,
        [pltpu.SemaphoreType.DMA((9,))],
        order,
        split,
        rhs,
        leaf,
        right_low,
        *in_hbm(basis_left, basis_right, coupling),
    )
    low = keep + got_low
    current, keep, send = call(
        functools.partial(local_kernel, top),
        [
            shape(count, size),
            shape(rows, wide),
            shape(rows, wide + rank // rows * (wide - rank + next_w)),
        ],
        [VMEM] * 9 + [ANY],
        [VMEM] * 3,
        [],
        split,
        current,
        left_top,
        right_top,
        right_low,
        right,
        coup,
        gram_top,
        gram_next,
        low,
    )
    got = exchange(send, 1)
    sums, next_sums, z_mine, z_other = call(
        functools.partial(top_kernel, top),
        [shape(rows, next_w), shape(rows, rank), shape(rows, rank), shape(rows, rank)],
        [VMEM] * 4,
        [VMEM] * 4,
        [pltpu.VMEM((2 * rank, wide - rank), F32)],
        keep,
        got,
        gram_top,
        coup,
    )
    known = {top - 1: (z_mine, z_other)}
    got_low = exchange(low, 3)
    z, sums = call(
        functools.partial(next_kernel, top),
        [shape(rows, rank), shape(rows, next_w)],
        [VMEM] * 6,
        [VMEM] * 2,
        [],
        next_sums,
        exchange(next_sums, 3),
        sums,
        gram_next,
        got,
        coup,
    )
    known[top - 2] = (z, z)
    low = low + got_low
    sums = sums + exchange(sums, 3)
    for k in range(top - 3, 1, -1):
        mask = 1 << (top - 1 - k) | 1
        w = k * rank
        last = k == 2
        got_low = exchange(low, mask)
        got = exchange(sums, mask)
        mine, rest = call(
            functools.partial(merge_kernel, last),
            [shape(n, 2 * w + (rank if last else 0)), shape(n, low.shape[1] - w)],
            [VMEM, VMEM, ANY],
            [VMEM] * 2,
            [],
            low,
            got_low,
            got,
        )
        both, z = call(
            functools.partial(couple_kernel, top, k),
            [shape(rows, 2 * rank), shape(rows, 2 * rank)],
            [VMEM] * 3,
            [VMEM] * 2,
            [],
            sums,
            got,
            coup,
        )
        sums = call(
            functools.partial(level_kernel, top, k),
            shape(rows, w + (rank // rows * rank if last else 0)),
            [VMEM] * 7,
            VMEM,
            [pltpu.VMEM((2 * rank, w), F32)],
            sums,
            got,
            z,
            low,
            got_low,
            rest,
            exchange(mine, 1),
        )
        known[k] = (both, both)
        low = rest
    sums, both = call(
        functools.partial(first_kernel, top),
        [shape(rows, rank), shape(rows, 2 * rank)],
        [VMEM] * 3,
        [VMEM] * 2,
        [pltpu.VMEM((2 * rank, rank), F32)],
        sums,
        exchange(sums, 1 << (top - 2) | 1),
        coup,
    )
    known[1] = (both, both)
    got_sums = exchange(sums, 1 << (top - 1) | 1)
    names = range(1, top)
    others = exchange(jnp.concatenate([known[k][1] for k in names], axis=1), 1)
    args, at = [], 0
    for k in names:
        mine = known[k][0]
        args += [mine, others[:, at : at + mine.shape[1]]]
        at += mine.shape[1]
    current, factor = call(
        functools.partial(early_kernel, top),
        [shape(count, size), shape(2 * rank, size)],
        [VMEM] * (4 + len(args)),
        [VMEM] * 2,
        [],
        current,
        *args,
        left_low,
        left,
        coup,
    )
    both = beside(sums, got_sums, (device_id >> (top - 1)) & 1 == 1)
    return call(
        functools.partial(last_kernel, top),
        shape(count, size),
        [VMEM] * 4,
        VMEM,
        [],
        current,
        both,
        exchange(both, 1),
        factor,
    )


def solution(mesh):
    in_specs = (
        P(None, AXES),
        P(AXES),
        P(AXES),
        P(AXES, None),
        P(None, AXES, None),
        P(None, AXES, None),
        P(AXES, None, None, None),
    )
    return jax.shard_map(
        per_device, mesh=mesh, in_specs=in_specs, out_specs=P(None, AXES), check_vma=False
    )
```

```python
import functools

import jax
import jax.numpy as jnp
from jax import lax
from jax.experimental import pallas as pl
from jax.experimental.pallas import tpu as pltpu
from jax.sharding import PartitionSpec as P

AXES = ("grp", "sub")
F32, BF16 = jnp.float32, jnp.bfloat16
NN = (((1,), (0,)), ((), ()))
NT = (((1,), (1,)), ((), ()))
TN = (((0,), (0,)), ((), ()))
ANY = pl.BlockSpec(memory_space=pl.ANY)
HBM = pl.BlockSpec(memory_space=pltpu.HBM)
VMEM = pl.BlockSpec(memory_space=pltpu.VMEM)
LIMIT = 24 * 1024 * 1024


def parts(x):
    high = x.astype(BF16)
    return high, (x - high.astype(F32)).astype(BF16)


def product(a, b, dims):
    return lax.dot_general(a, b, dims, preferred_element_type=F32)


def dot(a, b, dims=NN):
    if dims == TN:
        a, dims = a.T, NN
    ah, al = parts(a)
    bh, bl = parts(b)
    rows = a.shape[0]
    both = product(jnp.concatenate([ah, al], axis=0), bh, dims)
    return both[:rows] + (both[rows:] + product(ah, bl, dims))


def parity_of(device_id, bits):
    parity = device_id & 1
    for bit in range(1, bits):
        parity = parity ^ ((device_id >> bit) & 1)
    return parity


def low_kernel(
    top, left, right, rhs, leaf, order, keep, send, left_v, right_v, rhs_v, leaf_v, order_v,
    left_mid, right_mid, sems,
):
    rank = left.shape[2]
    n = rank // 2
    count = top - 3
    bases = []
    for j in range(count):
        cols = slice(j * rank, (j + 1) * rank)
        bases.append(pltpu.make_async_copy(left.at[j + 1], left_v.at[:, cols], sems.at[0, j]))
        bases.append(pltpu.make_async_copy(right.at[j], right_v.at[:, cols], sems.at[1, j]))
    rest = [
        pltpu.make_async_copy(order, order_v, sems.at[2, 1]),
        pltpu.make_async_copy(rhs, rhs_v, sems.at[2, 2]),
        pltpu.make_async_copy(leaf, leaf_v, sems.at[2, 3]),
        pltpu.make_async_copy(left.at[top - 2], left_mid.at[:, :rank], sems.at[3, 0]),
        pltpu.make_async_copy(left.at[top - 1], left_mid.at[:, rank:], sems.at[3, 1]),
        pltpu.make_async_copy(right.at[top - 3], right_mid.at[:, :rank], sems.at[3, 2]),
        pltpu.make_async_copy(right.at[top - 2], right_mid.at[:, rank:], sems.at[3, 3]),
    ]
    for copy in bases + rest:
        copy.start()
    for copy in bases:
        copy.wait()
    half = parity_of(lax.axis_index(AXES), top) == 1
    grams = dot(left_v[...], right_v[...], TN)
    at = 0
    for k in range(count, 0, -1):
        w = k * rank
        value = grams[w - rank : w, :w]
        keep[:, at : at + w] = jnp.where(half, value[n:], value[:n])
        send[:, at : at + w] = jnp.where(half, value[:n], value[n:])
        at += w
    for copy in rest:
        copy.wait()


def sides(split, size):
    border = split[...]
    return (
        lax.broadcasted_iota(jnp.int32, (1, size), 1) < border,
        lax.broadcasted_iota(jnp.int32, (size, 1), 0) < border,
    )


def leaf_kernel(
    top, order, split, rhs, leaf, right_low, left_mid, right_mid, left, right, coupling, current,
    gram_top, gram_next, left_first, right_last, left_top, right_top, coupling_v, sems,
):
    rank = left_top.shape[1]
    count, size = rhs.shape
    copies = [
        pltpu.make_async_copy(right.at[top], right_top, sems.at[0]),
        pltpu.make_async_copy(coupling.at[0], coupling_v, sems.at[1]),
        pltpu.make_async_copy(left.at[top], left_top, sems.at[2]),
        pltpu.make_async_copy(right.at[top - 1], right_last, sems.at[3]),
        pltpu.make_async_copy(left.at[0], left_first, sems.at[4]),
    ]
    for copy in copies:
        copy.start()
    local = order[...] - lax.axis_index(AXES) * size
    pick = (lax.broadcasted_iota(jnp.int32, (size, size), 0) == local).astype(F32).astype(BF16)
    high, low = parts(rhs[...])
    moved = product(jnp.concatenate([high, low], axis=0), pick, NN).astype(BF16)
    columns, rows = sides(split, size)
    lh, ll = parts(jnp.where(rows == columns, leaf[...], 0.0))
    both = product(moved, lh, NN)
    current[...] = both[:count] + (both[count:] + product(moved[:count], ll, NN))
    low_w = right_low.shape[1]
    upper = left_mid[...]
    value = dot(upper, right_low[...], TN)
    gram_next[:, :low_w] = value[:rank]
    gram_top[:, :low_w] = value[rank:]
    value = dot(upper, right_mid[...], TN)
    gram_next[:, low_w:] = value[:rank, :rank]
    gram_top[:, low_w:] = value[rank:]
    for copy in copies:
        copy.wait()


def put_rows(out, at, value):
    rows, w = out.shape[0], value.shape[1]
    for row in range(0, value.shape[0], rows):
        out[:, at : at + w] = value[row : row + rows, :]
        at += w
    return at


def take_rows(packed, at, height, w):
    rows = packed.shape[0]
    return jnp.concatenate(
        [packed[:, at + i * w : at + (i + 1) * w] for i in range(height // rows)], axis=0
    )


def local_kernel(
    top, split, first, left_top, right_top, right_low, right_mid, right_last, coupling, gram_top,
    gram_next, _, current_out, keep, send,
):
    rank = left_top.shape[1]
    count, size = first.shape
    current = first[...]
    is_left, _ = sides(split, size)
    halves = jnp.concatenate(
        [jnp.where(is_left, current, 0.0), jnp.where(is_left, 0.0, current)], axis=0
    )
    w = dot(halves, right_top[...])
    z = dot(jnp.concatenate([w[:count], w[count:]], axis=1), coupling[top])
    update = dot(jnp.concatenate([z[:, :rank], z[:, rank:]], axis=0), left_top[...], NT)
    current = current - jnp.where(is_left, update[:count], update[count:])
    current_out[...] = current
    half = parity_of(lax.axis_index(AXES), top) == 1
    n = count // 2
    at = 0
    for basis in (right_low, right_mid, right_last):
        sums = dot(current, basis[...])
        w = basis.shape[1]
        keep[:, at : at + w] = jnp.where(half, sums[n:], sums[:n])
        send[:, at : at + w] = jnp.where(half, sums[:n], sums[n:])
        at += w
    at = put_rows(send, at, gram_top[...])
    put_rows(send, at, gram_next[...])


def beside(own, got, on_right):
    return jnp.concatenate(
        [jnp.where(on_right, got, own), jnp.where(on_right, own, got)], axis=1
    )


def top_kernel(top, keep, got, gram_top, coupling, sums, next_sums, z_mine, z_other, pair):
    rank = gram_top.shape[0]
    w = (top - 1) * rank
    right = lax.axis_index(AXES) & 1
    own_at, got_at = right * rank, (1 - right) * rank
    pair[pl.ds(pl.multiple_of(own_at, rank), rank), :] = gram_top[...]
    pair[pl.ds(pl.multiple_of(got_at, rank), rank), :] = take_rows(got, top * rank, rank, w)
    is_right = right == 1
    z = dot(beside(keep[:, w:], got[:, w : top * rank], is_right), coupling[top - 1])
    value = keep[:, :w] + got[:, :w] - dot(z, pair[...])
    sums[...] = value[:, : w - rank]
    next_sums[...] = value[:, w - rank :]
    z_mine[...] = jnp.where(is_right, z[:, rank:], z[:, :rank])
    z_other[...] = jnp.where(is_right, z[:, :rank], z[:, rank:])


def side_of(coupling, k, right):
    rank = coupling.shape[2] // 2
    return jnp.where(right, coupling[k, :, rank:], coupling[k, :, :rank])


def next_kernel(top, mine, got, sums, gram_next, got_gram, coupling, z_out, sums_out):
    rank, w = gram_next.shape
    right = (lax.axis_index(AXES) >> 1) & 1 == 1
    z = dot(beside(mine[...], got[...], right), side_of(coupling, top - 2, right))
    at = top * rank + rank // got_gram.shape[0] * (w + rank)
    gram = gram_next[...] + take_rows(got_gram, at, rank, w)
    z_out[...] = z
    sums_out[...] = sums[...] - dot(z, gram)


def joined(mine, other, top):
    half = parity_of(lax.axis_index(AXES), top) == 1
    return jnp.concatenate(
        [jnp.where(half, other, mine), jnp.where(half, mine, other)], axis=0
    )


def add_kernel(low, got, _, out):
    out[...] = low[...] + got[...]


def cut_kernel(low, got, _, *out):
    rank = out[0].shape[1]
    w = (len(out) - 1) * rank
    for j, piece in enumerate(out[:-1]):
        piece[...] = got[:, j * rank : (j + 1) * rank]
    out[-1][...] = low[:, w:] + got[:, w:]


def couple_kernel(top, k, sums, got, coupling, both, z):
    rank = both.shape[1] // 2
    right = (lax.axis_index(AXES) >> (top - 1 - k)) & 1 == 1
    w = k * rank
    both[...] = beside(sums[:, w:], got[:, w:], right)
    z[...] = dot(both[...], coupling[k])


def level_kernel(top, k, sums, got, z, low, got_low, other, *refs):
    got_others, rests, (out, pair) = refs[:k], refs[k:-2], refs[-2:]
    n = low.shape[0]
    rank, w = 2 * n, k * 2 * n
    bit = top - 1 - k
    device_id = lax.axis_index(AXES)
    half = parity_of(device_id, top)
    right = (device_id >> bit) & 1

    def put(child, mine, theirs, cols):
        pair[pl.ds(pl.multiple_of(child * rank + half * n, n), n), cols] = mine
        pair[pl.ds(pl.multiple_of(child * rank + (1 - half) * n, n), n), cols] = theirs

    for j in range(k):
        cols = slice(j * rank, (j + 1) * rank)
        put(right, low[:, cols], other[:, cols], cols)
        put(1 - right, got_low[:, cols], got_others[j][...], cols)
    out[:, :w] = sums[:, :w] + got[:, :w] - dot(z[...], pair[...])
    if rests:
        put_rows(out, w, joined(rests[0][...], rests[1][...], top))


def first_kernel(top, packed, got, coupling, out, both, pair):
    rank = out.shape[1]
    right = (lax.axis_index(AXES) >> (top - 2)) & 1
    for child, value in ((right, packed), (1 - right, got)):
        pair[pl.ds(pl.multiple_of(child * rank, rank), rank), :] = take_rows(
            value, 2 * rank, rank, rank
        )
    both[...] = beside(packed[:, rank : 2 * rank], got[:, rank : 2 * rank], right == 1)
    z = dot(both[...], coupling[1])
    out[...] = packed[:, :rank] + got[:, :rank] - dot(z, pair[...])


def early_kernel(top, current, *refs):
    left_first, left_low, left_mid, coupling, out, factor = refs[-6:]
    rank = left_first.shape[1]
    device_id = lax.axis_index(AXES)
    z = []
    for k in range(1, top):
        pair = joined(refs[2 * k - 2][...], refs[2 * k - 1][...], top)
        right = (device_id >> (top - 1 - k)) & 1 == 1
        z.append(pair if k >= top - 2 else dot(pair, side_of(coupling, k, right)))
    low = dot(jnp.concatenate(z[: top - 3], axis=1), left_low[...], NT)
    high = dot(jnp.concatenate(z[top - 3 :], axis=1), left_mid[...], NT)
    out[...] = current[...] - (low + high)
    right = (device_id >> (top - 1)) & 1 == 1
    factor[...] = dot(side_of(coupling, 0, right), left_first[...], NT)


def last_kernel(top, current, mine, other, factor, out):
    out[...] = current[...] - dot(joined(mine[...], other[...], top), factor[...])


def call(kernel, outs, in_specs, out_specs, scratch, *args):
    return pl.pallas_call(
        kernel,
        out_shape=outs,
        in_specs=in_specs,
        out_specs=out_specs,
        scratch_shapes=scratch,
        cost_estimate=pl.CostEstimate(flops=1, bytes_accessed=1, transcendentals=0),
        compiler_params=pltpu.CompilerParams(vmem_limit_bytes=LIMIT),
    )(*args)


def shape(*dims, dtype=F32):
    return jax.ShapeDtypeStruct(dims, dtype)


def in_hbm(*arrays):
    return [pltpu.with_memory_space_constraint(x, pltpu.HBM) for x in arrays]


def exchange(value, mask):
    return lax.ppermute(value, AXES, [(i, i ^ mask) for i in range(lax.axis_size(AXES))])


def per_device(right_side, order, leaf_split, leaf_inverse, basis_left, basis_right, coupling):
    count, size = right_side.shape
    levels, _, rank = basis_left.shape
    top = levels - 1
    n = rank // 2
    rows = count // 2
    wide = top * rank
    low_w = rank * (top - 2) * (top - 3) // 2
    next_w = (top - 2) * rank
    device_id = lax.axis_index(AXES)
    split = leaf_split.reshape(1, 1)
    keep, send, left_low, right_low, rhs, leaf, order, left_mid, right_mid = call(
        functools.partial(low_kernel, top),
        [
            shape(n, low_w),
            shape(n, low_w),
            shape(size, (top - 3) * rank),
            shape(size, (top - 3) * rank),
            shape(count, size),
            shape(size, size),
            shape(1, size, dtype=jnp.int32),
            shape(size, 2 * rank),
            shape(size, 2 * rank),
        ],
        [HBM] * 5,
        [VMEM] * 9,
        [pltpu.SemaphoreType.DMA((4, max(4, top - 3)))],
        *in_hbm(basis_left, basis_right, right_side, leaf_inverse, order.reshape(1, size)),
    )
    got_low = exchange(send, 1)
    current, gram_top, gram_next, left_first, right_last, left_top, right_top, coup = call(
        functools.partial(leaf_kernel, top),
        [
            shape(count, size),
            shape(rank, wide - rank),
            shape(rank, next_w),
            shape(size, rank),
            shape(size, rank),
            shape(size, rank),
            shape(size, rank),
            shape(levels, 2 * rank, 2 * rank),
        ],
        [VMEM] * 7 + [HBM] * 3,
        [VMEM] * 8,
        [pltpu.SemaphoreType.DMA((5,))],
        order,
        split,
        rhs,
        leaf,
        right_low,
        left_mid,
        right_mid,
        *in_hbm(basis_left, basis_right, coupling),
    )
    low = keep + got_low
    current, keep, send = call(
        functools.partial(local_kernel, top),
        [
            shape(count, size),
            shape(rows, wide),
            shape(rows, wide + rank // rows * (wide - rank + next_w)),
        ],
        [VMEM] * 10 + [ANY],
        [VMEM] * 3,
        [],
        split,
        current,
        left_top,
        right_top,
        right_low,
        right_mid,
        right_last,
        coup,
        gram_top,
        gram_next,
        low,
    )
    got = exchange(send, 1)
    sums, next_sums, z_mine, z_other = call(
        functools.partial(top_kernel, top),
        [shape(rows, next_w), shape(rows, rank), shape(rows, rank), shape(rows, rank)],
        [VMEM] * 4,
        [VMEM] * 4,
        [pltpu.VMEM((2 * rank, wide - rank), F32)],
        keep,
        got,
        gram_top,
        coup,
    )
    known = {top - 1: (z_mine, z_other)}
    got_low = exchange(low, 3)
    got_next = exchange(next_sums, 3)
    z, sums = call(
        functools.partial(next_kernel, top),
        [shape(rows, rank), shape(rows, next_w)],
        [VMEM] * 6,
        [VMEM] * 2,
        [],
        next_sums,
        got_next,
        sums,
        gram_next,
        got,
        coup,
    )
    known[top - 2] = (z, z)
    low = call(add_kernel, shape(*low.shape), [VMEM, VMEM, ANY], VMEM, [], low, got_low, got_next)
    sums = sums + exchange(sums, 3)
    for k in range(top - 3, 1, -1):
        mask = 1 << (top - 1 - k) | 1
        w = k * rank
        last = k == 2
        got_low = exchange(low, mask)
        got = exchange(sums, mask)
        others = exchange(low[:, :w], 1)
        *pieces, rest = call(
            cut_kernel,
            [shape(n, rank)] * k + [shape(n, low.shape[1] - w)],
            [VMEM, VMEM, ANY],
            [VMEM] * (k + 1),
            [],
            low,
            got_low,
            sums,
        )
        pieces = [exchange(piece, 1) for piece in pieces]
        rests = [rest, exchange(rest, 1)] if last else []
        both, z = call(
            functools.partial(couple_kernel, top, k),
            [shape(rows, 2 * rank), shape(rows, 2 * rank)],
            [VMEM] * 3,
            [VMEM] * 2,
            [],
            sums,
            got,
            coup,
        )
        sums = call(
            functools.partial(level_kernel, top, k),
            shape(rows, w + (rank // rows * rank if last else 0)),
            [VMEM] * (6 + k + len(rests)),
            VMEM,
            [pltpu.VMEM((2 * rank, w), F32)],
            sums,
            got,
            z,
            low,
            got_low,
            others,
            *pieces,
            *rests,
        )
        known[k] = (both, both)
        low = rest
    sums, both = call(
        functools.partial(first_kernel, top),
        [shape(rows, rank), shape(rows, 2 * rank)],
        [VMEM] * 3,
        [VMEM] * 2,
        [pltpu.VMEM((2 * rank, rank), F32)],
        sums,
        exchange(sums, 1 << (top - 2) | 1),
        coup,
    )
    known[1] = (both, both)
    got_sums = exchange(sums, 1 << (top - 1) | 1)
    names = range(1, top)
    others = exchange(jnp.concatenate([known[k][1] for k in names], axis=1), 1)
    args, at = [], 0
    for k in names:
        mine = known[k][0]
        args += [mine, others[:, at : at + mine.shape[1]]]
        at += mine.shape[1]
    current, factor = call(
        functools.partial(early_kernel, top),
        [shape(count, size), shape(2 * rank, size)],
        [VMEM] * (5 + len(args)),
        [VMEM] * 2,
        [],
        current,
        *args,
        left_first,
        left_low,
        left_mid,
        coup,
    )
    both = beside(sums, got_sums, (device_id >> (top - 1)) & 1 == 1)
    return call(
        functools.partial(last_kernel, top),
        shape(count, size),
        [VMEM] * 4,
        VMEM,
        [],
        current,
        both,
        exchange(both, 1),
        factor,
    )


def solution(mesh):
    in_specs = (
        P(None, AXES),
        P(AXES),
        P(AXES),
        P(AXES, None),
        P(None, AXES, None),
        P(None, AXES, None),
        P(AXES, None, None, None),
    )
    return jax.shard_map(
        per_device, mesh=mesh, in_specs=in_specs, out_specs=P(None, AXES), check_vma=False
    )
```

```python
import functools

import jax
import jax.numpy as jnp
from jax import lax
from jax.experimental import pallas as pl
from jax.experimental.pallas import tpu as pltpu
from jax.sharding import PartitionSpec as P

AXES = ("grp", "sub")
F32, BF16 = jnp.float32, jnp.bfloat16
NN = (((1,), (0,)), ((), ()))
NT = (((1,), (1,)), ((), ()))
TN = (((0,), (0,)), ((), ()))
ANY = pl.BlockSpec(memory_space=pl.ANY)
HBM = pl.BlockSpec(memory_space=pltpu.HBM)
VMEM = pl.BlockSpec(memory_space=pltpu.VMEM)
LIMIT = 24 * 1024 * 1024


def parts(x):
    high = x.astype(BF16)
    return high, (x - high.astype(F32)).astype(BF16)


def product(a, b, dims):
    return lax.dot_general(a, b, dims, preferred_element_type=F32)


def dot(a, b, dims=NN):
    if dims == TN:
        a, dims = a.T, NN
    ah, al = parts(a)
    bh, bl = parts(b)
    rows = a.shape[0]
    both = product(jnp.concatenate([ah, al], axis=0), bh, dims)
    return both[:rows] + (both[rows:] + product(ah, bl, dims))


def parity_of(device_id, bits):
    parity = device_id & 1
    for bit in range(1, bits):
        parity = parity ^ ((device_id >> bit) & 1)
    return parity


def low_kernel(
    top, left, right, rhs, leaf, order, keep, send, left_v, right_v, rhs_v, leaf_v, order_v,
    left_mid, right_mid, sems,
):
    rank = left.shape[2]
    n = rank // 2
    count = top - 3
    bases = []
    for j in range(count):
        cols = slice(j * rank, (j + 1) * rank)
        bases.append(pltpu.make_async_copy(left.at[j + 1], left_v.at[:, cols], sems.at[0, j]))
        bases.append(pltpu.make_async_copy(right.at[j], right_v.at[:, cols], sems.at[1, j]))
    rest = [
        pltpu.make_async_copy(order, order_v, sems.at[2, 1]),
        pltpu.make_async_copy(rhs, rhs_v, sems.at[2, 2]),
        pltpu.make_async_copy(leaf, leaf_v, sems.at[2, 3]),
        pltpu.make_async_copy(left.at[top - 2], left_mid.at[:, :rank], sems.at[3, 0]),
        pltpu.make_async_copy(left.at[top - 1], left_mid.at[:, rank:], sems.at[3, 1]),
        pltpu.make_async_copy(right.at[top - 3], right_mid.at[:, :rank], sems.at[3, 2]),
        pltpu.make_async_copy(right.at[top - 2], right_mid.at[:, rank:], sems.at[3, 3]),
    ]
    for copy in bases + rest:
        copy.start()
    for copy in bases:
        copy.wait()
    half = parity_of(lax.axis_index(AXES), top) == 1
    grams = dot(left_v[...], right_v[...], TN)
    at = 0
    for k in range(count, 0, -1):
        w = k * rank
        value = grams[w - rank : w, :w]
        keep[:, at : at + w] = jnp.where(half, value[n:], value[:n])
        send[:, at : at + w] = jnp.where(half, value[:n], value[n:])
        at += w
    for copy in rest:
        copy.wait()


def sides(split, size):
    border = split[...]
    return (
        lax.broadcasted_iota(jnp.int32, (1, size), 1) < border,
        lax.broadcasted_iota(jnp.int32, (size, 1), 0) < border,
    )


def leaf_kernel(
    top, order, split, rhs, leaf, right_low, left_mid, right_mid, left, right, coupling, current,
    gram_top, gram_next, right_last, left_top, right_top, coupling_v, sems,
):
    rank = left_top.shape[1]
    count, size = rhs.shape
    copies = [
        pltpu.make_async_copy(right.at[top], right_top, sems.at[0]),
        pltpu.make_async_copy(coupling.at[0, pl.ds(top - 2, 3)], coupling_v, sems.at[1]),
        pltpu.make_async_copy(left.at[top], left_top, sems.at[2]),
        pltpu.make_async_copy(right.at[top - 1], right_last, sems.at[3]),
    ]
    for copy in copies:
        copy.start()
    local = order[...] - lax.axis_index(AXES) * size
    pick = (lax.broadcasted_iota(jnp.int32, (size, size), 0) == local).astype(F32).astype(BF16)
    high, low = parts(rhs[...])
    moved = product(jnp.concatenate([high, low], axis=0), pick, NN).astype(BF16)
    columns, rows = sides(split, size)
    lh, ll = parts(jnp.where(rows == columns, leaf[...], 0.0))
    both = product(moved, lh, NN)
    current[...] = both[:count] + (both[count:] + product(moved[:count], ll, NN))
    low_w = right_low.shape[1]
    upper = left_mid[...]
    value = dot(upper, right_low[...], TN)
    gram_next[:, :low_w] = value[:rank]
    gram_top[:, :low_w] = value[rank:]
    value = dot(upper, right_mid[...], TN)
    gram_next[:, low_w:] = value[:rank, :rank]
    gram_top[:, low_w:] = value[rank:]
    for copy in copies:
        copy.wait()


def fetch_kernel(top, left, coupling, _, left_first, coupling_v, sems):
    copies = [
        pltpu.make_async_copy(coupling.at[0, pl.ds(0, top - 2)], coupling_v, sems.at[0]),
        pltpu.make_async_copy(left.at[0], left_first, sems.at[1]),
    ]
    for copy in copies:
        copy.start()
    for copy in copies:
        copy.wait()


def put_rows(out, at, value):
    rows, w = out.shape[0], value.shape[1]
    for row in range(0, value.shape[0], rows):
        out[:, at : at + w] = value[row : row + rows, :]
        at += w
    return at


def take_rows(packed, at, height, w):
    rows = packed.shape[0]
    return jnp.concatenate(
        [packed[:, at + i * w : at + (i + 1) * w] for i in range(height // rows)], axis=0
    )


def local_kernel(
    top, split, first, left_top, right_top, right_low, right_mid, right_last, coupling, gram_top,
    gram_next, _, current_out, keep, send,
):
    rank = left_top.shape[1]
    count, size = first.shape
    current = first[...]
    is_left, _ = sides(split, size)
    halves = jnp.concatenate(
        [jnp.where(is_left, current, 0.0), jnp.where(is_left, 0.0, current)], axis=0
    )
    w = dot(halves, right_top[...])
    z = dot(jnp.concatenate([w[:count], w[count:]], axis=1), coupling[2])
    update = dot(jnp.concatenate([z[:, :rank], z[:, rank:]], axis=0), left_top[...], NT)
    current = current - jnp.where(is_left, update[:count], update[count:])
    current_out[...] = current
    half = parity_of(lax.axis_index(AXES), top) == 1
    n = count // 2
    at = 0
    for basis in (right_low, right_mid, right_last):
        sums = dot(current, basis[...])
        w = basis.shape[1]
        keep[:, at : at + w] = jnp.where(half, sums[n:], sums[:n])
        send[:, at : at + w] = jnp.where(half, sums[:n], sums[n:])
        at += w
    at = put_rows(send, at, gram_top[...])
    put_rows(send, at, gram_next[...])


def beside(own, got, on_right):
    return jnp.concatenate(
        [jnp.where(on_right, got, own), jnp.where(on_right, own, got)], axis=1
    )


def top_kernel(top, keep, got, gram_top, coupling, sums, next_sums, z_mine, z_other, pair):
    rank = gram_top.shape[0]
    w = (top - 1) * rank
    right = lax.axis_index(AXES) & 1
    own_at, got_at = right * rank, (1 - right) * rank
    pair[pl.ds(pl.multiple_of(own_at, rank), rank), :] = gram_top[...]
    pair[pl.ds(pl.multiple_of(got_at, rank), rank), :] = take_rows(got, top * rank, rank, w)
    is_right = right == 1
    z = dot(beside(keep[:, w:], got[:, w : top * rank], is_right), coupling[1])
    value = keep[:, :w] + got[:, :w] - dot(z, pair[...])
    sums[...] = value[:, : w - rank]
    next_sums[...] = value[:, w - rank :]
    z_mine[...] = jnp.where(is_right, z[:, rank:], z[:, :rank])
    z_other[...] = jnp.where(is_right, z[:, :rank], z[:, rank:])


def side_of(coupling, k, right):
    rank = coupling.shape[2] // 2
    return jnp.where(right, coupling[k, :, rank:], coupling[k, :, :rank])


def next_kernel(top, mine, got, sums, gram_next, got_gram, coupling, z_out, sums_out):
    rank, w = gram_next.shape
    right = (lax.axis_index(AXES) >> 1) & 1 == 1
    z = dot(beside(mine[...], got[...], right), side_of(coupling, 0, right))
    at = top * rank + rank // got_gram.shape[0] * (w + rank)
    gram = gram_next[...] + take_rows(got_gram, at, rank, w)
    z_out[...] = z
    sums_out[...] = sums[...] - dot(z, gram)


def joined(mine, other, top):
    half = parity_of(lax.axis_index(AXES), top) == 1
    return jnp.concatenate(
        [jnp.where(half, other, mine), jnp.where(half, mine, other)], axis=0
    )


def add_kernel(low, got, _, out):
    out[...] = low[...] + got[...]


def cut_kernel(low, got, _, *out):
    rank = out[0].shape[1]
    w = (len(out) - 1) * rank
    for j, piece in enumerate(out[:-1]):
        piece[...] = got[:, j * rank : (j + 1) * rank]
    out[-1][...] = low[:, w:] + got[:, w:]


def couple_kernel(top, k, sums, got, coupling, both, z):
    rank = both.shape[1] // 2
    right = (lax.axis_index(AXES) >> (top - 1 - k)) & 1 == 1
    w = k * rank
    both[...] = beside(sums[:, w:], got[:, w:], right)
    z[...] = dot(both[...], coupling[k])


def level_kernel(top, k, sums, got, z, low, got_low, other, *refs):
    got_others, rests, (out, pair) = refs[:k], refs[k:-2], refs[-2:]
    n = low.shape[0]
    rank, w = 2 * n, k * 2 * n
    bit = top - 1 - k
    device_id = lax.axis_index(AXES)
    half = parity_of(device_id, top)
    right = (device_id >> bit) & 1

    def put(child, mine, theirs, cols):
        pair[pl.ds(pl.multiple_of(child * rank + half * n, n), n), cols] = mine
        pair[pl.ds(pl.multiple_of(child * rank + (1 - half) * n, n), n), cols] = theirs

    for j in range(k):
        cols = slice(j * rank, (j + 1) * rank)
        put(right, low[:, cols], other[:, cols], cols)
        put(1 - right, got_low[:, cols], got_others[j][...], cols)
    out[:, :w] = sums[:, :w] + got[:, :w] - dot(z[...], pair[...])
    if rests:
        put_rows(out, w, joined(rests[0][...], rests[1][...], top))


def first_kernel(top, packed, got, coupling, out, both, pair):
    rank = out.shape[1]
    right = (lax.axis_index(AXES) >> (top - 2)) & 1
    for child, value in ((right, packed), (1 - right, got)):
        pair[pl.ds(pl.multiple_of(child * rank, rank), rank), :] = take_rows(
            value, 2 * rank, rank, rank
        )
    both[...] = beside(packed[:, rank : 2 * rank], got[:, rank : 2 * rank], right == 1)
    z = dot(both[...], coupling[1])
    out[...] = packed[:, :rank] + got[:, :rank] - dot(z, pair[...])


def early_kernel(top, current, *refs):
    left_first, left_low, left_mid, coupling, out, factor = refs[-6:]
    rank = left_first.shape[1]
    device_id = lax.axis_index(AXES)
    z = []
    for k in range(1, top):
        pair = joined(refs[2 * k - 2][...], refs[2 * k - 1][...], top)
        right = (device_id >> (top - 1 - k)) & 1 == 1
        z.append(pair if k >= top - 2 else dot(pair, side_of(coupling, k, right)))
    low = dot(jnp.concatenate(z[: top - 3], axis=1), left_low[...], NT)
    high = dot(jnp.concatenate(z[top - 3 :], axis=1), left_mid[...], NT)
    out[...] = current[...] - (low + high)
    right = (device_id >> (top - 1)) & 1 == 1
    factor[...] = dot(side_of(coupling, 0, right), left_first[...], NT)


def last_kernel(top, current, mine, other, factor, out):
    out[...] = current[...] - dot(joined(mine[...], other[...], top), factor[...])


def call(kernel, outs, in_specs, out_specs, scratch, *args):
    return pl.pallas_call(
        kernel,
        out_shape=outs,
        in_specs=in_specs,
        out_specs=out_specs,
        scratch_shapes=scratch,
        cost_estimate=pl.CostEstimate(flops=1, bytes_accessed=1, transcendentals=0),
        compiler_params=pltpu.CompilerParams(vmem_limit_bytes=LIMIT),
    )(*args)


def shape(*dims, dtype=F32):
    return jax.ShapeDtypeStruct(dims, dtype)


def in_hbm(*arrays):
    return [pltpu.with_memory_space_constraint(x, pltpu.HBM) for x in arrays]


def exchange(value, mask):
    return lax.ppermute(value, AXES, [(i, i ^ mask) for i in range(lax.axis_size(AXES))])


def per_device(right_side, order, leaf_split, leaf_inverse, basis_left, basis_right, coupling):
    count, size = right_side.shape
    levels, _, rank = basis_left.shape
    top = levels - 1
    n = rank // 2
    rows = count // 2
    wide = top * rank
    low_w = rank * (top - 2) * (top - 3) // 2
    next_w = (top - 2) * rank
    device_id = lax.axis_index(AXES)
    split = leaf_split.reshape(1, 1)
    keep, send, left_low, right_low, rhs, leaf, order, left_mid, right_mid = call(
        functools.partial(low_kernel, top),
        [
            shape(n, low_w),
            shape(n, low_w),
            shape(size, (top - 3) * rank),
            shape(size, (top - 3) * rank),
            shape(count, size),
            shape(size, size),
            shape(1, size, dtype=jnp.int32),
            shape(size, 2 * rank),
            shape(size, 2 * rank),
        ],
        [HBM] * 5,
        [VMEM] * 9,
        [pltpu.SemaphoreType.DMA((4, max(4, top - 3)))],
        *in_hbm(basis_left, basis_right, right_side, leaf_inverse, order.reshape(1, size)),
    )
    got_low = exchange(send, 1)
    current, gram_top, gram_next, right_last, left_top, right_top, near = call(
        functools.partial(leaf_kernel, top),
        [
            shape(count, size),
            shape(rank, wide - rank),
            shape(rank, next_w),
            shape(size, rank),
            shape(size, rank),
            shape(size, rank),
            shape(3, 2 * rank, 2 * rank),
        ],
        [VMEM] * 7 + [HBM] * 3,
        [VMEM] * 7,
        [pltpu.SemaphoreType.DMA((5,))],
        order,
        split,
        rhs,
        leaf,
        right_low,
        left_mid,
        right_mid,
        *in_hbm(basis_left, basis_right, coupling),
    )
    low = keep + got_low
    current, keep, send = call(
        functools.partial(local_kernel, top),
        [
            shape(count, size),
            shape(rows, wide),
            shape(rows, wide + rank // rows * (wide - rank + next_w)),
        ],
        [VMEM] * 10 + [ANY],
        [VMEM] * 3,
        [],
        split,
        current,
        left_top,
        right_top,
        right_low,
        right_mid,
        right_last,
        near,
        gram_top,
        gram_next,
        low,
    )
    got = exchange(send, 1)
    sums, next_sums, z_mine, z_other = call(
        functools.partial(top_kernel, top),
        [shape(rows, next_w), shape(rows, rank), shape(rows, rank), shape(rows, rank)],
        [VMEM] * 4,
        [VMEM] * 4,
        [pltpu.VMEM((2 * rank, wide - rank), F32)],
        keep,
        got,
        gram_top,
        near,
    )
    known = {top - 1: (z_mine, z_other)}
    got_low = exchange(low, 3)
    got_next = exchange(next_sums, 3)
    z, sums = call(
        functools.partial(next_kernel, top),
        [shape(rows, rank), shape(rows, next_w)],
        [VMEM] * 6,
        [VMEM] * 2,
        [],
        next_sums,
        got_next,
        sums,
        gram_next,
        got,
        near,
    )
    known[top - 2] = (z, z)
    low = call(add_kernel, shape(*low.shape), [VMEM, VMEM, ANY], VMEM, [], low, got_low, got_next)
    sums = sums + exchange(sums, 3)
    left_first, coup = call(
        functools.partial(fetch_kernel, top),
        [shape(size, rank), shape(top - 2, 2 * rank, 2 * rank)],
        [HBM] * 2 + [ANY],
        [VMEM] * 2,
        [pltpu.SemaphoreType.DMA((2,))],
        *in_hbm(basis_left, coupling),
        sums,
    )
    for k in range(top - 3, 1, -1):
        mask = 1 << (top - 1 - k) | 1
        w = k * rank
        last = k == 2
        got_low = exchange(low, mask)
        got = exchange(sums, mask)
        others = exchange(low[:, :w], 1)
        *pieces, rest = call(
            cut_kernel,
            [shape(n, rank)] * k + [shape(n, low.shape[1] - w)],
            [VMEM, VMEM, ANY],
            [VMEM] * (k + 1),
            [],
            low,
            got_low,
            coup,
        )
        pieces = [exchange(piece, 1) for piece in pieces]
        rests = [rest, exchange(rest, 1)] if last else []
        both, z = call(
            functools.partial(couple_kernel, top, k),
            [shape(rows, 2 * rank), shape(rows, 2 * rank)],
            [VMEM] * 3,
            [VMEM] * 2,
            [],
            sums,
            got,
            coup,
        )
        sums = call(
            functools.partial(level_kernel, top, k),
            shape(rows, w + (rank // rows * rank if last else 0)),
            [VMEM] * (6 + k + len(rests)),
            VMEM,
            [pltpu.VMEM((2 * rank, w), F32)],
            sums,
            got,
            z,
            low,
            got_low,
            others,
            *pieces,
            *rests,
        )
        known[k] = (both, both)
        low = rest
    sums, both = call(
        functools.partial(first_kernel, top),
        [shape(rows, rank), shape(rows, 2 * rank)],
        [VMEM] * 3,
        [VMEM] * 2,
        [pltpu.VMEM((2 * rank, rank), F32)],
        sums,
        exchange(sums, 1 << (top - 2) | 1),
        coup,
    )
    known[1] = (both, both)
    got_sums = exchange(sums, 1 << (top - 1) | 1)
    names = range(1, top)
    others = exchange(jnp.concatenate([known[k][1] for k in names], axis=1), 1)
    args, at = [], 0
    for k in names:
        mine = known[k][0]
        args += [mine, others[:, at : at + mine.shape[1]]]
        at += mine.shape[1]
    current, factor = call(
        functools.partial(early_kernel, top),
        [shape(count, size), shape(2 * rank, size)],
        [VMEM] * (5 + len(args)),
        [VMEM] * 2,
        [],
        current,
        *args,
        left_first,
        left_low,
        left_mid,
        coup,
    )
    both = beside(sums, got_sums, (device_id >> (top - 1)) & 1 == 1)
    return call(
        functools.partial(last_kernel, top),
        shape(count, size),
        [VMEM] * 4,
        VMEM,
        [],
        current,
        both,
        exchange(both, 1),
        factor,
    )


def solution(mesh):
    in_specs = (
        P(None, AXES),
        P(AXES),
        P(AXES),
        P(AXES, None),
        P(None, AXES, None),
        P(None, AXES, None),
        P(AXES, None, None, None),
    )
    return jax.shard_map(
        per_device, mesh=mesh, in_specs=in_specs, out_specs=P(None, AXES), check_vma=False
    )
```

```python
import functools

import jax
import jax.numpy as jnp
from jax import lax
from jax.experimental import pallas as pl
from jax.experimental.pallas import tpu as pltpu
from jax.sharding import PartitionSpec as P

AXES = ("grp", "sub")
F32, BF16 = jnp.float32, jnp.bfloat16
NN = (((1,), (0,)), ((), ()))
NT = (((1,), (1,)), ((), ()))
TN = (((0,), (0,)), ((), ()))
ANY = pl.BlockSpec(memory_space=pl.ANY)
HBM = pl.BlockSpec(memory_space=pltpu.HBM)
VMEM = pl.BlockSpec(memory_space=pltpu.VMEM)
LIMIT = 24 * 1024 * 1024


def parts(x):
    high = x.astype(BF16)
    return high, (x - high.astype(F32)).astype(BF16)


def product(a, b, dims):
    return lax.dot_general(a, b, dims, preferred_element_type=F32)


def dot(a, b, dims=NN):
    if dims == TN:
        a, dims = a.T, NN
    ah, al = parts(a)
    bh, bl = parts(b)
    rows = a.shape[0]
    both = product(jnp.concatenate([ah, al], axis=0), bh, dims)
    return both[:rows] + (both[rows:] + product(ah, bl, dims))


def parity_of(device_id, bits):
    parity = device_id & 1
    for bit in range(1, bits):
        parity = parity ^ ((device_id >> bit) & 1)
    return parity


def low_kernel(
    top, left, right, rhs, leaf, order, keep, send, left_v, right_v, rhs_v, leaf_v, order_v,
    left_mid, right_mid, sems,
):
    rank = left.shape[2]
    n = rank // 2
    count = top - 3
    bases = []
    for j in range(count):
        cols = slice(j * rank, (j + 1) * rank)
        bases.append(pltpu.make_async_copy(left.at[j + 1], left_v.at[:, cols], sems.at[0, j]))
        bases.append(pltpu.make_async_copy(right.at[j], right_v.at[:, cols], sems.at[1, j]))
    rest = [
        pltpu.make_async_copy(order, order_v, sems.at[2, 1]),
        pltpu.make_async_copy(rhs, rhs_v, sems.at[2, 2]),
        pltpu.make_async_copy(leaf, leaf_v, sems.at[2, 3]),
        pltpu.make_async_copy(left.at[top - 2], left_mid.at[:, :rank], sems.at[3, 0]),
        pltpu.make_async_copy(left.at[top - 1], left_mid.at[:, rank:], sems.at[3, 1]),
        pltpu.make_async_copy(right.at[top - 3], right_mid.at[:, :rank], sems.at[3, 2]),
        pltpu.make_async_copy(right.at[top - 2], right_mid.at[:, rank:], sems.at[3, 3]),
    ]
    for copy in bases + rest:
        copy.start()
    for copy in bases:
        copy.wait()
    half = parity_of(lax.axis_index(AXES), top) == 1
    grams = dot(left_v[...], right_v[...], TN)
    at = 0
    for k in range(count, 0, -1):
        w = k * rank
        value = grams[w - rank : w, :w]
        keep[:, at : at + w] = jnp.where(half, value[n:], value[:n])
        send[:, at : at + w] = jnp.where(half, value[:n], value[n:])
        at += w
    for copy in rest:
        copy.wait()


def sides(split, size):
    border = split[...]
    return (
        lax.broadcasted_iota(jnp.int32, (1, size), 1) < border,
        lax.broadcasted_iota(jnp.int32, (size, 1), 0) < border,
    )


def leaf_kernel(
    top, order, split, rhs, leaf, right_low, left_mid, right_mid, left, right, coupling, current,
    gram_top, gram_next, right_last, left_top, right_top, coupling_v, sems,
):
    rank = left_top.shape[1]
    count, size = rhs.shape
    copies = [
        pltpu.make_async_copy(right.at[top], right_top, sems.at[0]),
        pltpu.make_async_copy(coupling.at[0, pl.ds(top - 2, 3)], coupling_v, sems.at[1]),
        pltpu.make_async_copy(left.at[top], left_top, sems.at[2]),
        pltpu.make_async_copy(right.at[top - 1], right_last, sems.at[3]),
    ]
    for copy in copies:
        copy.start()
    local = order[...] - lax.axis_index(AXES) * size
    pick = (lax.broadcasted_iota(jnp.int32, (size, size), 0) == local).astype(F32).astype(BF16)
    high, low = parts(rhs[...])
    moved = product(jnp.concatenate([high, low], axis=0), pick, NN).astype(BF16)
    columns, rows = sides(split, size)
    lh, ll = parts(jnp.where(rows == columns, leaf[...], 0.0))
    both = product(moved, lh, NN)
    current[...] = both[:count] + (both[count:] + product(moved[:count], ll, NN))
    low_w = right_low.shape[1]
    upper = left_mid[...]
    value = dot(upper, right_low[...], TN)
    gram_next[:, :low_w] = value[:rank]
    gram_top[:, :low_w] = value[rank:]
    value = dot(upper, right_mid[...], TN)
    gram_next[:, low_w:] = value[:rank, :rank]
    gram_top[:, low_w:] = value[rank:]
    for copy in copies:
        copy.wait()


def fetch_kernel(top, left, coupling, _, left_first, coupling_v, sems):
    copies = [
        pltpu.make_async_copy(coupling.at[0, pl.ds(0, top - 2)], coupling_v, sems.at[0]),
        pltpu.make_async_copy(left.at[0], left_first, sems.at[1]),
    ]
    for copy in copies:
        copy.start()
    for copy in copies:
        copy.wait()


def put_rows(out, at, value):
    rows, w = out.shape[0], value.shape[1]
    for row in range(0, value.shape[0], rows):
        out[:, at : at + w] = value[row : row + rows, :]
        at += w
    return at


def take_rows(packed, at, height, w):
    rows = packed.shape[0]
    return jnp.concatenate(
        [packed[:, at + i * w : at + (i + 1) * w] for i in range(height // rows)], axis=0
    )


def local_kernel(
    top, split, first, left_top, right_top, right_low, right_mid, right_last, coupling, gram_top,
    gram_next, _, current_out, keep, send,
):
    rank = left_top.shape[1]
    count, size = first.shape
    current = first[...]
    is_left, _ = sides(split, size)
    halves = jnp.concatenate(
        [jnp.where(is_left, current, 0.0), jnp.where(is_left, 0.0, current)], axis=0
    )
    w = dot(halves, right_top[...])
    z = dot(jnp.concatenate([w[:count], w[count:]], axis=1), coupling[2])
    update = dot(jnp.concatenate([z[:, :rank], z[:, rank:]], axis=0), left_top[...], NT)
    current = current - jnp.where(is_left, update[:count], update[count:])
    current_out[...] = current
    half = parity_of(lax.axis_index(AXES), top) == 1
    n = count // 2
    at = 0
    for basis in (right_low, right_mid, right_last):
        sums = dot(current, basis[...])
        w = basis.shape[1]
        keep[:, at : at + w] = jnp.where(half, sums[n:], sums[:n])
        send[:, at : at + w] = jnp.where(half, sums[:n], sums[n:])
        at += w
    at = put_rows(send, at, gram_top[...])
    put_rows(send, at, gram_next[...])


def beside(own, got, on_right):
    return jnp.concatenate(
        [jnp.where(on_right, got, own), jnp.where(on_right, own, got)], axis=1
    )


def top_kernel(top, keep, got, gram_top, coupling, sums, next_sums, z_mine, z_other, pair):
    rank = gram_top.shape[0]
    w = (top - 1) * rank
    right = lax.axis_index(AXES) & 1
    own_at, got_at = right * rank, (1 - right) * rank
    pair[pl.ds(pl.multiple_of(own_at, rank), rank), :] = gram_top[...]
    pair[pl.ds(pl.multiple_of(got_at, rank), rank), :] = take_rows(got, top * rank, rank, w)
    is_right = right == 1
    z = dot(beside(keep[:, w:], got[:, w : top * rank], is_right), coupling[1])
    value = keep[:, :w] + got[:, :w] - dot(z, pair[...])
    sums[...] = value[:, : w - rank]
    next_sums[...] = value[:, w - rank :]
    z_mine[...] = jnp.where(is_right, z[:, rank:], z[:, :rank])
    z_other[...] = jnp.where(is_right, z[:, :rank], z[:, rank:])


def side_of(coupling, k, right):
    rank = coupling.shape[2] // 2
    return jnp.where(right, coupling[k, :, rank:], coupling[k, :, :rank])


def next_kernel(top, mine, got, sums, gram_next, got_gram, coupling, z_out, sums_out):
    rank, w = gram_next.shape
    right = (lax.axis_index(AXES) >> 1) & 1 == 1
    z = dot(beside(mine[...], got[...], right), side_of(coupling, 0, right))
    at = top * rank + rank // got_gram.shape[0] * (w + rank)
    gram = gram_next[...] + take_rows(got_gram, at, rank, w)
    z_out[...] = z
    sums_out[...] = sums[...] - dot(z, gram)


def joined(mine, other, top):
    half = parity_of(lax.axis_index(AXES), top) == 1
    return jnp.concatenate(
        [jnp.where(half, other, mine), jnp.where(half, mine, other)], axis=0
    )


def add_kernel(low, got, _, out):
    out[...] = low[...] + got[...]


def cut_kernel(low, got, _, *out):
    rank = out[0].shape[1]
    w = (len(out) - 1) * rank
    for j, piece in enumerate(out[:-1]):
        piece[...] = got[:, j * rank : (j + 1) * rank]
    out[-1][...] = low[:, w:] + got[:, w:]


def couple_kernel(top, k, sums, got, coupling, both, z):
    rank = both.shape[1] // 2
    right = (lax.axis_index(AXES) >> (top - 1 - k)) & 1 == 1
    w = k * rank
    both[...] = beside(sums[:, w:], got[:, w:], right)
    z[...] = dot(both[...], coupling[k])


def level_kernel(top, k, sums, got, z, low, got_low, other, *refs):
    got_others, rests, (out, pair) = refs[:k], refs[k:-2], refs[-2:]
    n = low.shape[0]
    rank, w = 2 * n, k * 2 * n
    bit = top - 1 - k
    device_id = lax.axis_index(AXES)
    half = parity_of(device_id, top)
    right = (device_id >> bit) & 1

    def put(child, mine, theirs, cols):
        pair[pl.ds(pl.multiple_of(child * rank + half * n, n), n), cols] = mine
        pair[pl.ds(pl.multiple_of(child * rank + (1 - half) * n, n), n), cols] = theirs

    for j in range(k):
        cols = slice(j * rank, (j + 1) * rank)
        put(right, low[:, cols], other[:, cols], cols)
        put(1 - right, got_low[:, cols], got_others[j][...], cols)
    out[:, :w] = sums[:, :w] + got[:, :w] - dot(z[...], pair[...])
    if rests:
        put_rows(out, w, joined(rests[0][...], rests[1][...], top))


def first_kernel(top, packed, got, coupling, out, both, pair):
    rank = out.shape[1]
    right = (lax.axis_index(AXES) >> (top - 2)) & 1
    for child, value in ((right, packed), (1 - right, got)):
        pair[pl.ds(pl.multiple_of(child * rank, rank), rank), :] = take_rows(
            value, 2 * rank, rank, rank
        )
    both[...] = beside(packed[:, rank : 2 * rank], got[:, rank : 2 * rank], right == 1)
    z = dot(both[...], coupling[1])
    out[...] = packed[:, :rank] + got[:, :rank] - dot(z, pair[...])


def early_kernel(top, current, *refs):
    left_first, left_low, left_mid, coupling, out, factor = refs[-6:]
    rank = left_first.shape[1]
    device_id = lax.axis_index(AXES)
    z = []
    for k in range(1, top):
        pair = joined(refs[2 * k - 2][...], refs[2 * k - 1][...], top)
        right = (device_id >> (top - 1 - k)) & 1 == 1
        z.append(pair if k >= top - 2 else dot(pair, side_of(coupling, k, right)))
    low = dot(jnp.concatenate(z[: top - 3], axis=1), left_low[...], NT)
    high = dot(jnp.concatenate(z[top - 3 :], axis=1), left_mid[...], NT)
    out[...] = current[...] - (low + high)
    right = (device_id >> (top - 1)) & 1 == 1
    factor[...] = dot(side_of(coupling, 0, right), left_first[...], NT)


def last_kernel(top, current, mine, other, factor, out):
    out[...] = current[...] - dot(joined(mine[...], other[...], top), factor[...])


def call(kernel, outs, in_specs, out_specs, scratch, *args):
    return pl.pallas_call(
        kernel,
        out_shape=outs,
        in_specs=in_specs,
        out_specs=out_specs,
        scratch_shapes=scratch,
        cost_estimate=pl.CostEstimate(flops=1, bytes_accessed=1, transcendentals=0),
        compiler_params=pltpu.CompilerParams(vmem_limit_bytes=LIMIT),
    )(*args)


def shape(*dims, dtype=F32):
    return jax.ShapeDtypeStruct(dims, dtype)


def in_hbm(*arrays):
    return [pltpu.with_memory_space_constraint(x, pltpu.HBM) for x in arrays]


def exchange(value, mask):
    return lax.ppermute(value, AXES, [(i, i ^ mask) for i in range(lax.axis_size(AXES))])


def per_device(right_side, order, leaf_split, leaf_inverse, basis_left, basis_right, coupling):
    count, size = right_side.shape
    levels, _, rank = basis_left.shape
    top = levels - 1
    n = rank // 2
    rows = count // 2
    wide = top * rank
    low_w = rank * (top - 2) * (top - 3) // 2
    next_w = (top - 2) * rank
    device_id = lax.axis_index(AXES)
    split = leaf_split.reshape(1, 1)
    keep, send, left_low, right_low, rhs, leaf, order, left_mid, right_mid = call(
        functools.partial(low_kernel, top),
        [
            shape(n, low_w),
            shape(n, low_w),
            shape(size, (top - 3) * rank),
            shape(size, (top - 3) * rank),
            shape(count, size),
            shape(size, size),
            shape(1, size, dtype=jnp.int32),
            shape(size, 2 * rank),
            shape(size, 2 * rank),
        ],
        [HBM] * 5,
        [VMEM] * 9,
        [pltpu.SemaphoreType.DMA((4, max(4, top - 3)))],
        *in_hbm(basis_left, basis_right, right_side, leaf_inverse, order.reshape(1, size)),
    )
    got_low = exchange(send, 1)
    current, gram_top, gram_next, right_last, left_top, right_top, near = call(
        functools.partial(leaf_kernel, top),
        [
            shape(count, size),
            shape(rank, wide - rank),
            shape(rank, next_w),
            shape(size, rank),
            shape(size, rank),
            shape(size, rank),
            shape(3, 2 * rank, 2 * rank),
        ],
        [VMEM] * 7 + [HBM] * 3,
        [VMEM] * 7,
        [pltpu.SemaphoreType.DMA((5,))],
        order,
        split,
        rhs,
        leaf,
        right_low,
        left_mid,
        right_mid,
        *in_hbm(basis_left, basis_right, coupling),
    )
    low = keep + got_low
    current, keep, send = call(
        functools.partial(local_kernel, top),
        [
            shape(count, size),
            shape(rows, wide),
            shape(rows, wide + rank // rows * (wide - rank + next_w)),
        ],
        [VMEM] * 10 + [ANY],
        [VMEM] * 3,
        [],
        split,
        current,
        left_top,
        right_top,
        right_low,
        right_mid,
        right_last,
        near,
        gram_top,
        gram_next,
        low,
    )
    got = exchange(send, 1)
    sums, next_sums, z_mine, z_other = call(
        functools.partial(top_kernel, top),
        [shape(rows, next_w), shape(rows, rank), shape(rows, rank), shape(rows, rank)],
        [VMEM] * 4,
        [VMEM] * 4,
        [pltpu.VMEM((2 * rank, wide - rank), F32)],
        keep,
        got,
        gram_top,
        near,
    )
    known = {top - 1: (z_mine, z_other)}
    got_low = exchange(low, 3)
    got_next = exchange(next_sums, 3)
    z, sums = call(
        functools.partial(next_kernel, top),
        [shape(rows, rank), shape(rows, next_w)],
        [VMEM] * 6,
        [VMEM] * 2,
        [],
        next_sums,
        got_next,
        sums,
        gram_next,
        got,
        near,
    )
    known[top - 2] = (z, z)
    low = call(add_kernel, shape(*low.shape), [VMEM, VMEM, ANY], VMEM, [], low, got_low, got_next)
    sums = sums + exchange(sums, 3)
    left_first, coup = call(
        functools.partial(fetch_kernel, top),
        [shape(size, rank), shape(top - 2, 2 * rank, 2 * rank)],
        [HBM] * 2 + [ANY],
        [VMEM] * 2,
        [pltpu.SemaphoreType.DMA((2,))],
        *in_hbm(basis_left, coupling),
        sums,
    )
    for k in range(top - 3, 1, -1):
        mask = 1 << (top - 1 - k) | 1
        w = k * rank
        last = k == 2
        got_low = exchange(low, mask)
        got = exchange(sums, mask)
        others = exchange(low[:, :w], 1)
        *pieces, rest = call(
            cut_kernel,
            [shape(n, rank)] * k + [shape(n, low.shape[1] - w)],
            [VMEM, VMEM, ANY],
            [VMEM] * (k + 1),
            [],
            low,
            got_low,
            sums,
        )
        pieces = [exchange(piece, 1) for piece in pieces]
        rests = [rest, exchange(rest, 1)] if last else []
        both, z = call(
            functools.partial(couple_kernel, top, k),
            [shape(rows, 2 * rank), shape(rows, 2 * rank)],
            [VMEM] * 3,
            [VMEM] * 2,
            [],
            sums,
            got,
            coup,
        )
        sums = call(
            functools.partial(level_kernel, top, k),
            shape(rows, w + (rank // rows * rank if last else 0)),
            [VMEM] * (6 + k + len(rests)),
            VMEM,
            [pltpu.VMEM((2 * rank, w), F32)],
            sums,
            got,
            z,
            low,
            got_low,
            others,
            *pieces,
            *rests,
        )
        known[k] = (both, both)
        low = rest
    sums, both = call(
        functools.partial(first_kernel, top),
        [shape(rows, rank), shape(rows, 2 * rank)],
        [VMEM] * 3,
        [VMEM] * 2,
        [pltpu.VMEM((2 * rank, rank), F32)],
        sums,
        exchange(sums, 1 << (top - 2) | 1),
        coup,
    )
    known[1] = (both, both)
    got_sums = exchange(sums, 1 << (top - 1) | 1)
    names = range(1, top)
    others = exchange(jnp.concatenate([known[k][1] for k in names], axis=1), 1)
    args, at = [], 0
    for k in names:
        mine = known[k][0]
        args += [mine, others[:, at : at + mine.shape[1]]]
        at += mine.shape[1]
    current, factor = call(
        functools.partial(early_kernel, top),
        [shape(count, size), shape(2 * rank, size)],
        [VMEM] * (5 + len(args)),
        [VMEM] * 2,
        [],
        current,
        *args,
        left_first,
        left_low,
        left_mid,
        coup,
    )
    both = beside(sums, got_sums, (device_id >> (top - 1)) & 1 == 1)
    return call(
        functools.partial(last_kernel, top),
        shape(count, size),
        [VMEM] * 4,
        VMEM,
        [],
        current,
        both,
        exchange(both, 1),
        factor,
    )


def solution(mesh):
    in_specs = (
        P(None, AXES),
        P(AXES),
        P(AXES),
        P(AXES, None),
        P(None, AXES, None),
        P(None, AXES, None),
        P(AXES, None, None, None),
    )
    return jax.shard_map(
        per_device, mesh=mesh, in_specs=in_specs, out_specs=P(None, AXES), check_vma=False
    )
```

```python
import functools

import jax
import jax.numpy as jnp
from jax import lax
from jax.experimental import pallas as pl
from jax.experimental.pallas import tpu as pltpu
from jax.sharding import PartitionSpec as P

AXES = ("grp", "sub")
F32, BF16 = jnp.float32, jnp.bfloat16
NN = (((1,), (0,)), ((), ()))
NT = (((1,), (1,)), ((), ()))
TN = (((0,), (0,)), ((), ()))
ANY = pl.BlockSpec(memory_space=pl.ANY)
HBM = pl.BlockSpec(memory_space=pltpu.HBM)
SMEM = pl.BlockSpec(memory_space=pltpu.SMEM)
VMEM = pl.BlockSpec(memory_space=pltpu.VMEM)
LIMIT = 24 * 1024 * 1024


def parts(x):
    high = x.astype(BF16)
    return high, (x - high.astype(F32)).astype(BF16)


def product(a, b, dims):
    return lax.dot_general(a, b, dims, preferred_element_type=F32)


def dot(a, b, dims=NN):
    if dims == TN:
        a, dims = a.T, NN
    ah, al = parts(a)
    bh, bl = parts(b)
    rows = a.shape[0]
    both = product(jnp.concatenate([ah, al], axis=0), bh, dims)
    return both[:rows] + (both[rows:] + product(ah, bl, dims))


def parity_of(device_id, bits):
    parity = device_id & 1
    for bit in range(1, bits):
        parity = parity ^ ((device_id >> bit) & 1)
    return parity


def sides(split, size):
    border = split[0:1, 0:1]
    return (
        lax.broadcasted_iota(jnp.int32, (1, size), 1) < border,
        lax.broadcasted_iota(jnp.int32, (size, 1), 0) < border,
    )


def first_reads(
    top, left, right, coupling, rhs, leaf, order, split, keep, send, current, gram_top, gram_next,
    left_low, right_low, left_mid, right_mid, left_top, right_top, right_last, near, split_v,
    rhs_v, leaf_v, order_v, sems,
):
    rank = left.shape[2]
    n = rank // 2
    count = top - 3
    bases = []
    for j in range(count):
        cols = slice(j * rank, (j + 1) * rank)
        bases.append(pltpu.make_async_copy(left.at[j + 1], left_low.at[:, cols], sems.at[0, j]))
        bases.append(pltpu.make_async_copy(right.at[j], right_low.at[:, cols], sems.at[1, j]))
    rows = [
        pltpu.make_async_copy(order, order_v, sems.at[2, 0]),
        pltpu.make_async_copy(rhs, rhs_v, sems.at[2, 1]),
    ]
    leaf_copy = pltpu.make_async_copy(leaf, leaf_v, sems.at[2, 2])
    mid = [
        pltpu.make_async_copy(left.at[top - 2], left_mid.at[:, :rank], sems.at[3, 0]),
        pltpu.make_async_copy(left.at[top - 1], left_mid.at[:, rank:], sems.at[3, 1]),
        pltpu.make_async_copy(right.at[top - 3], right_mid.at[:, :rank], sems.at[3, 2]),
        pltpu.make_async_copy(right.at[top - 2], right_mid.at[:, rank:], sems.at[3, 3]),
    ]
    rest = [
        pltpu.make_async_copy(right.at[top], right_top, sems.at[4, 0]),
        pltpu.make_async_copy(coupling.at[0, pl.ds(top - 2, 3)], near, sems.at[4, 1]),
        pltpu.make_async_copy(left.at[top], left_top, sems.at[4, 2]),
        pltpu.make_async_copy(right.at[top - 1], right_last, sems.at[4, 3]),
    ]
    for copy in rows + bases + [leaf_copy] + mid + rest:
        copy.start()
    split_v[...] = jnp.full(split_v.shape, split[0], jnp.int32)
    device_id = lax.axis_index(AXES)
    half = parity_of(device_id, top) == 1
    size = rhs_v.shape[1]
    for copy in rows:
        copy.wait()
    local = order_v[...] - device_id * size
    pick = (lax.broadcasted_iota(jnp.int32, (size, size), 0) == local).astype(F32).astype(BF16)
    high, low = parts(rhs_v[...])
    moved = product(jnp.concatenate([high, low], axis=0), pick, NN).astype(BF16)
    for copy in bases:
        copy.wait()
    grams = dot(left_low[...], right_low[...], TN)
    at = 0
    for k in range(count, 0, -1):
        w = k * rank
        value = grams[w - rank : w, :w]
        keep[:, at : at + w] = jnp.where(half, value[n:], value[:n])
        send[:, at : at + w] = jnp.where(half, value[:n], value[n:])
        at += w
    leaf_copy.wait()
    rows_n = rhs_v.shape[0]
    is_left, left_rows = sides(split_v, size)
    lh, ll = parts(jnp.where(left_rows == is_left, leaf_v[...], 0.0))
    both = product(moved, lh, NN)
    current[...] = both[:rows_n] + (both[rows_n:] + product(moved[:rows_n], ll, NN))
    for copy in mid:
        copy.wait()
    low_w = right_low.shape[1]
    upper = left_mid[...]
    value = dot(upper, right_low[...], TN)
    gram_next[:, :low_w] = value[:rank]
    gram_top[:, :low_w] = value[rank:]
    value = dot(upper, right_mid[...], TN)
    gram_next[:, low_w:] = value[:rank, :rank]
    gram_top[:, low_w:] = value[rank:]
    put_rows(send, at, gram_next[...])
    for copy in rest:
        copy.wait()


def fetch_kernel(top, left, coupling, _, left_first, coupling_v, sems):
    copies = [
        pltpu.make_async_copy(coupling.at[0, pl.ds(0, top - 2)], coupling_v, sems.at[0]),
        pltpu.make_async_copy(left.at[0], left_first, sems.at[1]),
    ]
    for copy in copies:
        copy.start()
    for copy in copies:
        copy.wait()


def put_rows(out, at, value):
    rows, w = out.shape[0], value.shape[1]
    for row in range(0, value.shape[0], rows):
        out[:, at : at + w] = value[row : row + rows, :]
        at += w
    return at


def take_rows(packed, at, height, w):
    rows = packed.shape[0]
    return jnp.concatenate(
        [packed[:, at + i * w : at + (i + 1) * w] for i in range(height // rows)], axis=0
    )


def local_kernel(
    top, split, first, left_top, right_top, right_low, right_mid, right_last, coupling, gram_top,
    current_out, keep, send,
):
    rank = left_top.shape[1]
    count, size = first.shape
    current = first[...]
    is_left, _ = sides(split, size)
    halves = jnp.concatenate(
        [jnp.where(is_left, current, 0.0), jnp.where(is_left, 0.0, current)], axis=0
    )
    w = dot(halves, right_top[...])
    z = dot(jnp.concatenate([w[:count], w[count:]], axis=1), coupling[2])
    update = dot(jnp.concatenate([z[:, :rank], z[:, rank:]], axis=0), left_top[...], NT)
    current = current - jnp.where(is_left, update[:count], update[count:])
    current_out[...] = current
    half = parity_of(lax.axis_index(AXES), top) == 1
    n = count // 2
    at = 0
    for basis in (right_low, right_mid, right_last):
        sums = dot(current, basis[...])
        w = basis.shape[1]
        keep[:, at : at + w] = jnp.where(half, sums[n:], sums[:n])
        send[:, at : at + w] = jnp.where(half, sums[:n], sums[n:])
        at += w
    put_rows(send, at, gram_top[...])


def beside(own, got, on_right):
    return jnp.concatenate(
        [jnp.where(on_right, got, own), jnp.where(on_right, own, got)], axis=1
    )


def top_kernel(top, keep, got, gram_top, coupling, sums, next_sums, z_mine, z_other, pair):
    rank = gram_top.shape[0]
    w = (top - 1) * rank
    right = lax.axis_index(AXES) & 1
    own_at, got_at = right * rank, (1 - right) * rank
    pair[pl.ds(pl.multiple_of(own_at, rank), rank), :] = gram_top[...]
    pair[pl.ds(pl.multiple_of(got_at, rank), rank), :] = take_rows(got, top * rank, rank, w)
    is_right = right == 1
    z = dot(beside(keep[:, w:], got[:, w : top * rank], is_right), coupling[1])
    value = keep[:, :w] + got[:, :w] - dot(z, pair[...])
    sums[...] = value[:, : w - rank]
    next_sums[...] = value[:, w - rank :]
    z_mine[...] = jnp.where(is_right, z[:, rank:], z[:, :rank])
    z_other[...] = jnp.where(is_right, z[:, :rank], z[:, rank:])


def side_of(coupling, k, right):
    rank = coupling.shape[2] // 2
    return jnp.where(right, coupling[k, :, rank:], coupling[k, :, :rank])


def next_kernel(top, mine, got, sums, gram_next, got_gram, coupling, z_out, sums_out):
    rank, w = gram_next.shape
    right = (lax.axis_index(AXES) >> 1) & 1 == 1
    z = dot(beside(mine[...], got[...], right), side_of(coupling, 0, right))
    at = got_gram.shape[1] - rank // got_gram.shape[0] * w
    gram = gram_next[...] + take_rows(got_gram, at, rank, w)
    z_out[...] = z
    sums_out[...] = sums[...] - dot(z, gram)


def joined(mine, other, top):
    half = parity_of(lax.axis_index(AXES), top) == 1
    return jnp.concatenate(
        [jnp.where(half, other, mine), jnp.where(half, mine, other)], axis=0
    )


def add_kernel(low, got, _, out):
    out[...] = low[...] + got[...]


def cut_kernel(low, got, _, *out):
    rank = out[0].shape[1]
    w = (len(out) - 1) * rank
    for j, piece in enumerate(out[:-1]):
        piece[...] = got[:, j * rank : (j + 1) * rank]
    out[-1][...] = low[:, w:] + got[:, w:]


def couple_kernel(top, k, sums, got, coupling, both, z):
    rank = both.shape[1] // 2
    right = (lax.axis_index(AXES) >> (top - 1 - k)) & 1 == 1
    w = k * rank
    both[...] = beside(sums[:, w:], got[:, w:], right)
    z[...] = dot(both[...], coupling[k])


def level_kernel(top, k, sums, got, z, low, got_low, other, *refs):
    got_others, rests, (out, pair) = refs[:k], refs[k:-2], refs[-2:]
    n = low.shape[0]
    rank, w = 2 * n, k * 2 * n
    bit = top - 1 - k
    device_id = lax.axis_index(AXES)
    half = parity_of(device_id, top)
    right = (device_id >> bit) & 1

    def put(child, mine, theirs, cols):
        pair[pl.ds(pl.multiple_of(child * rank + half * n, n), n), cols] = mine
        pair[pl.ds(pl.multiple_of(child * rank + (1 - half) * n, n), n), cols] = theirs

    for j in range(k):
        cols = slice(j * rank, (j + 1) * rank)
        put(right, low[:, cols], other[:, cols], cols)
        put(1 - right, got_low[:, cols], got_others[j][...], cols)
    out[:, :w] = sums[:, :w] + got[:, :w] - dot(z[...], pair[...])
    if rests:
        put_rows(out, w, joined(rests[0][...], rests[1][...], top))


def first_kernel(top, packed, got, coupling, out, both, pair):
    rank = out.shape[1]
    right = (lax.axis_index(AXES) >> (top - 2)) & 1
    for child, value in ((right, packed), (1 - right, got)):
        pair[pl.ds(pl.multiple_of(child * rank, rank), rank), :] = take_rows(
            value, 2 * rank, rank, rank
        )
    both[...] = beside(packed[:, rank : 2 * rank], got[:, rank : 2 * rank], right == 1)
    z = dot(both[...], coupling[1])
    out[...] = packed[:, :rank] + got[:, :rank] - dot(z, pair[...])


def early_kernel(top, current, *refs):
    left_first, left_low, left_mid, coupling, out, factor = refs[-6:]
    rank = left_first.shape[1]
    device_id = lax.axis_index(AXES)
    z = []
    for k in range(1, top):
        pair = joined(refs[2 * k - 2][...], refs[2 * k - 1][...], top)
        right = (device_id >> (top - 1 - k)) & 1 == 1
        z.append(pair if k >= top - 2 else dot(pair, side_of(coupling, k, right)))
    low = dot(jnp.concatenate(z[: top - 3], axis=1), left_low[...], NT)
    high = dot(jnp.concatenate(z[top - 3 :], axis=1), left_mid[...], NT)
    out[...] = current[...] - (low + high)
    right = (device_id >> (top - 1)) & 1 == 1
    factor[...] = dot(side_of(coupling, 0, right), left_first[...], NT)


def last_kernel(top, current, mine, other, factor, out):
    out[...] = current[...] - dot(joined(mine[...], other[...], top), factor[...])


def call(kernel, outs, in_specs, out_specs, scratch, *args):
    return pl.pallas_call(
        kernel,
        out_shape=outs,
        in_specs=in_specs,
        out_specs=out_specs,
        scratch_shapes=scratch,
        cost_estimate=pl.CostEstimate(flops=1, bytes_accessed=1, transcendentals=0),
        compiler_params=pltpu.CompilerParams(vmem_limit_bytes=LIMIT),
    )(*args)


def shape(*dims, dtype=F32):
    return jax.ShapeDtypeStruct(dims, dtype)


def in_hbm(*arrays):
    return [pltpu.with_memory_space_constraint(x, pltpu.HBM) for x in arrays]


def exchange(value, mask):
    return lax.ppermute(value, AXES, [(i, i ^ mask) for i in range(lax.axis_size(AXES))])


def per_device(right_side, order, leaf_split, leaf_inverse, basis_left, basis_right, coupling):
    count, size = right_side.shape
    levels, _, rank = basis_left.shape
    top = levels - 1
    n = rank // 2
    rows = count // 2
    wide = top * rank
    low_w = rank * (top - 2) * (top - 3) // 2
    next_w = (top - 2) * rank
    device_id = lax.axis_index(AXES)
    f32_shapes = [
        shape(n, low_w),
        shape(n, low_w + 2 * next_w),
        shape(count, size),
        shape(rank, wide - rank),
        shape(rank, next_w),
        shape(size, (top - 3) * rank),
        shape(size, (top - 3) * rank),
        shape(size, 2 * rank),
        shape(size, 2 * rank),
        shape(size, rank),
        shape(size, rank),
        shape(size, rank),
        shape(3, 2 * rank, 2 * rank),
    ]
    (
        keep, send, current, gram_top, gram_next, left_low, right_low, left_mid, right_mid, left_top,
        right_top, right_last, near, split,
    ) = call(
        functools.partial(first_reads, top),
        f32_shapes + [shape(8, 128, dtype=jnp.int32)],
        [HBM] * 6 + [SMEM],
        [VMEM] * 14,
        [
            pltpu.VMEM((count, size), F32),
            pltpu.VMEM((size, size), F32),
            pltpu.VMEM((1, size), jnp.int32),
            pltpu.SemaphoreType.DMA((5, max(4, top - 3))),
        ],
        *in_hbm(basis_left, basis_right, coupling, right_side, leaf_inverse),
        *in_hbm(order.reshape(1, size)),
        leaf_split,
    )
    got_gram = exchange(send, 1)
    low = keep + got_gram[:, :low_w]
    current, keep, send = call(
        functools.partial(local_kernel, top),
        [
            shape(count, size),
            shape(rows, wide),
            shape(rows, wide + rank // rows * (wide - rank)),
        ],
        [VMEM] * 9,
        [VMEM] * 3,
        [],
        split,
        current,
        left_top,
        right_top,
        right_low,
        right_mid,
        right_last,
        near,
        gram_top,
    )
    got = exchange(send, 1)
    sums, next_sums, z_mine, z_other = call(
        functools.partial(top_kernel, top),
        [shape(rows, next_w), shape(rows, rank), shape(rows, rank), shape(rows, rank)],
        [VMEM] * 4,
        [VMEM] * 4,
        [pltpu.VMEM((2 * rank, wide - rank), F32)],
        keep,
        got,
        gram_top,
        near,
    )
    known = {top - 1: (z_mine, z_other)}
    got_low = exchange(low, 3)
    got_next = exchange(next_sums, 3)
    z, sums = call(
        functools.partial(next_kernel, top),
        [shape(rows, rank), shape(rows, next_w)],
        [VMEM] * 6,
        [VMEM] * 2,
        [],
        next_sums,
        got_next,
        sums,
        gram_next,
        got_gram,
        near,
    )
    known[top - 2] = (z, z)
    low = call(add_kernel, shape(*low.shape), [VMEM, VMEM, ANY], VMEM, [], low, got_low, got_next)
    sums = sums + exchange(sums, 3)
    left_first, coup = call(
        functools.partial(fetch_kernel, top),
        [shape(size, rank), shape(top - 2, 2 * rank, 2 * rank)],
        [HBM] * 2 + [ANY],
        [VMEM] * 2,
        [pltpu.SemaphoreType.DMA((2,))],
        *in_hbm(basis_left, coupling),
        sums,
    )
    for k in range(top - 3, 1, -1):
        mask = 1 << (top - 1 - k) | 1
        w = k * rank
        last = k == 2
        got_low = exchange(low, mask)
        got = exchange(sums, mask)
        others = exchange(low[:, :w], 1)
        *pieces, rest = call(
            cut_kernel,
            [shape(n, rank)] * k + [shape(n, low.shape[1] - w)],
            [VMEM, VMEM, ANY],
            [VMEM] * (k + 1),
            [],
            low,
            got_low,
            sums,
        )
        pieces = [exchange(piece, 1) for piece in pieces]
        rests = [rest, exchange(rest, 1)] if last else []
        both, z = call(
            functools.partial(couple_kernel, top, k),
            [shape(rows, 2 * rank), shape(rows, 2 * rank)],
            [VMEM] * 3,
            [VMEM] * 2,
            [],
            sums,
            got,
            coup,
        )
        sums = call(
            functools.partial(level_kernel, top, k),
            shape(rows, w + (rank // rows * rank if last else 0)),
            [VMEM] * (6 + k + len(rests)),
            VMEM,
            [pltpu.VMEM((2 * rank, w), F32)],
            sums,
            got,
            z,
            low,
            got_low,
            others,
            *pieces,
            *rests,
        )
        known[k] = (both, both)
        low = rest
    sums, both = call(
        functools.partial(first_kernel, top),
        [shape(rows, rank), shape(rows, 2 * rank)],
        [VMEM] * 3,
        [VMEM] * 2,
        [pltpu.VMEM((2 * rank, rank), F32)],
        sums,
        exchange(sums, 1 << (top - 2) | 1),
        coup,
    )
    known[1] = (both, both)
    got_sums = exchange(sums, 1 << (top - 1) | 1)
    names = range(1, top)
    others = exchange(jnp.concatenate([known[k][1] for k in names], axis=1), 1)
    args, at = [], 0
    for k in names:
        mine = known[k][0]
        args += [mine, others[:, at : at + mine.shape[1]]]
        at += mine.shape[1]
    current, factor = call(
        functools.partial(early_kernel, top),
        [shape(count, size), shape(2 * rank, size)],
        [VMEM] * (5 + len(args)),
        [VMEM] * 2,
        [],
        current,
        *args,
        left_first,
        left_low,
        left_mid,
        coup,
    )
    both = beside(sums, got_sums, (device_id >> (top - 1)) & 1 == 1)
    return call(
        functools.partial(last_kernel, top),
        shape(count, size),
        [VMEM] * 4,
        VMEM,
        [],
        current,
        both,
        exchange(both, 1),
        factor,
    )


def solution(mesh):
    in_specs = (
        P(None, AXES),
        P(AXES),
        P(AXES),
        P(AXES, None),
        P(None, AXES, None),
        P(None, AXES, None),
        P(AXES, None, None, None),
    )
    return jax.shard_map(
        per_device, mesh=mesh, in_specs=in_specs, out_specs=P(None, AXES), check_vma=False
    )
```

```python
import functools

import jax
import jax.numpy as jnp
from jax import lax
from jax.experimental import pallas as pl
from jax.experimental.pallas import tpu as pltpu
from jax.sharding import PartitionSpec as P

AXES = ("grp", "sub")
F32, BF16 = jnp.float32, jnp.bfloat16
NN = (((1,), (0,)), ((), ()))
NT = (((1,), (1,)), ((), ()))
TN = (((0,), (0,)), ((), ()))
ANY = pl.BlockSpec(memory_space=pl.ANY)
HBM = pl.BlockSpec(memory_space=pltpu.HBM)
SMEM = pl.BlockSpec(memory_space=pltpu.SMEM)
VMEM = pl.BlockSpec(memory_space=pltpu.VMEM)
LIMIT = 24 * 1024 * 1024


def parts(x):
    high = x.astype(BF16)
    return high, (x - high.astype(F32)).astype(BF16)


def product(a, b, dims):
    return lax.dot_general(a, b, dims, preferred_element_type=F32)


def dot(a, b, dims=NN):
    if dims == TN:
        a, dims = a.T, NN
    ah, al = parts(a)
    bh, bl = parts(b)
    rows = a.shape[0]
    both = product(jnp.concatenate([ah, al], axis=0), bh, dims)
    return both[:rows] + (both[rows:] + product(ah, bl, dims))


def parity_of(device_id, bits):
    parity = device_id & 1
    for bit in range(1, bits):
        parity = parity ^ ((device_id >> bit) & 1)
    return parity


def sides(split, size):
    border = split[0:1, 0:1]
    return (
        lax.broadcasted_iota(jnp.int32, (1, size), 1) < border,
        lax.broadcasted_iota(jnp.int32, (size, 1), 0) < border,
    )


def first_reads(
    top, left, right, coupling, rhs, leaf, order, split, keep, send, current, gram_top, gram_next,
    left_low, right_low, left_mid, right_mid, left_top, right_top, right_last, near, split_v,
    rhs_v, leaf_v, order_v, sems,
):
    rank = left.shape[2]
    n = rank // 2
    count = top - 3
    bases = []
    for j in range(count):
        cols = slice(j * rank, (j + 1) * rank)
        bases.append(pltpu.make_async_copy(left.at[j + 1], left_low.at[:, cols], sems.at[0, j]))
        bases.append(pltpu.make_async_copy(right.at[j], right_low.at[:, cols], sems.at[1, j]))
    rows = [
        pltpu.make_async_copy(order, order_v, sems.at[2, 0]),
        pltpu.make_async_copy(rhs, rhs_v, sems.at[2, 1]),
    ]
    leaf_copy = pltpu.make_async_copy(leaf, leaf_v, sems.at[2, 2])
    mid = [
        pltpu.make_async_copy(left.at[top - 2], left_mid.at[:, :rank], sems.at[3, 0]),
        pltpu.make_async_copy(left.at[top - 1], left_mid.at[:, rank:], sems.at[3, 1]),
        pltpu.make_async_copy(right.at[top - 3], right_mid.at[:, :rank], sems.at[3, 2]),
        pltpu.make_async_copy(right.at[top - 2], right_mid.at[:, rank:], sems.at[3, 3]),
    ]
    rest = [
        pltpu.make_async_copy(right.at[top], right_top, sems.at[4, 0]),
        pltpu.make_async_copy(coupling.at[0, pl.ds(top - 2, 3)], near, sems.at[4, 1]),
        pltpu.make_async_copy(left.at[top], left_top, sems.at[4, 2]),
        pltpu.make_async_copy(right.at[top - 1], right_last, sems.at[4, 3]),
    ]
    for copy in rows + bases + [leaf_copy] + mid + rest:
        copy.start()
    split_v[...] = jnp.full(split_v.shape, split[0], jnp.int32)
    device_id = lax.axis_index(AXES)
    half = parity_of(device_id, top) == 1
    size = rhs_v.shape[1]
    for copy in rows:
        copy.wait()
    local = order_v[...] - device_id * size
    pick = (lax.broadcasted_iota(jnp.int32, (size, size), 0) == local).astype(F32).astype(BF16)
    high, low = parts(rhs_v[...])
    moved = product(jnp.concatenate([high, low], axis=0), pick, NN).astype(BF16)
    for copy in bases:
        copy.wait()
    grams = dot(left_low[...], right_low[...], TN)
    at = 0
    for k in range(count, 0, -1):
        w = k * rank
        value = grams[w - rank : w, :w]
        keep[:, at : at + w] = jnp.where(half, value[n:], value[:n])
        send[:, at : at + w] = jnp.where(half, value[:n], value[n:])
        at += w
    leaf_copy.wait()
    rows_n = rhs_v.shape[0]
    is_left, left_rows = sides(split_v, size)
    lh, ll = parts(jnp.where(left_rows == is_left, leaf_v[...], 0.0))
    both = product(moved, lh, NN)
    current[...] = both[:rows_n] + (both[rows_n:] + product(moved[:rows_n], ll, NN))
    for copy in mid:
        copy.wait()
    low_w = right_low.shape[1]
    upper = left_mid[...]
    value = dot(upper, right_low[...], TN)
    gram_next[:, :low_w] = value[:rank]
    gram_top[:, :low_w] = value[rank:]
    value = dot(upper, right_mid[...], TN)
    gram_next[:, low_w:] = value[:rank, :rank]
    gram_top[:, low_w:] = value[rank:]
    put_rows(send, at, gram_next[...])
    for copy in rest:
        copy.wait()


def fetch_kernel(top, left, coupling, _, left_first, coupling_v, sems):
    copies = [
        pltpu.make_async_copy(coupling.at[0, pl.ds(0, top - 2)], coupling_v, sems.at[0]),
        pltpu.make_async_copy(left.at[0], left_first, sems.at[1]),
    ]
    for copy in copies:
        copy.start()
    for copy in copies:
        copy.wait()


def put_rows(out, at, value):
    rows, w = out.shape[0], value.shape[1]
    for row in range(0, value.shape[0], rows):
        out[:, at : at + w] = value[row : row + rows, :]
        at += w
    return at


def take_rows(packed, at, height, w):
    rows = packed.shape[0]
    return jnp.concatenate(
        [packed[:, at + i * w : at + (i + 1) * w] for i in range(height // rows)], axis=0
    )


def local_kernel(
    top, split, first, left_top, right_top, right_low, right_mid, right_last, coupling, gram_top,
    current_out, keep, send,
):
    rank = left_top.shape[1]
    count, size = first.shape
    current = first[...]
    is_left, _ = sides(split, size)
    halves = jnp.concatenate(
        [jnp.where(is_left, current, 0.0), jnp.where(is_left, 0.0, current)], axis=0
    )
    w = dot(halves, right_top[...])
    z = dot(jnp.concatenate([w[:count], w[count:]], axis=1), coupling[2])
    update = dot(jnp.concatenate([z[:, :rank], z[:, rank:]], axis=0), left_top[...], NT)
    current = current - jnp.where(is_left, update[:count], update[count:])
    current_out[...] = current
    half = parity_of(lax.axis_index(AXES), top) == 1
    n = count // 2
    at = 0
    for basis in (right_low, right_mid, right_last):
        sums = dot(current, basis[...])
        w = basis.shape[1]
        keep[:, at : at + w] = jnp.where(half, sums[n:], sums[:n])
        send[:, at : at + w] = jnp.where(half, sums[:n], sums[n:])
        at += w
    put_rows(send, at, gram_top[...])


def beside(own, got, on_right):
    return jnp.concatenate(
        [jnp.where(on_right, got, own), jnp.where(on_right, own, got)], axis=1
    )


def top_kernel(top, keep, got, gram_top, coupling, sums, next_sums, z_mine, z_other, pair):
    rank = gram_top.shape[0]
    w = (top - 1) * rank
    right = lax.axis_index(AXES) & 1
    own_at, got_at = right * rank, (1 - right) * rank
    pair[pl.ds(pl.multiple_of(own_at, rank), rank), :] = gram_top[...]
    pair[pl.ds(pl.multiple_of(got_at, rank), rank), :] = take_rows(got, top * rank, rank, w)
    is_right = right == 1
    z = dot(beside(keep[:, w:], got[:, w : top * rank], is_right), coupling[1])
    value = keep[:, :w] + got[:, :w] - dot(z, pair[...])
    sums[...] = value[:, : w - rank]
    next_sums[...] = value[:, w - rank :]
    z_mine[...] = jnp.where(is_right, z[:, rank:], z[:, :rank])
    z_other[...] = jnp.where(is_right, z[:, :rank], z[:, rank:])


def side_of(coupling, k, right):
    rank = coupling.shape[2] // 2
    return jnp.where(right, coupling[k, :, rank:], coupling[k, :, :rank])


def next_kernel(top, mine, got, sums, gram_next, got_gram, coupling, z_out, sums_out):
    rank, w = gram_next.shape
    right = (lax.axis_index(AXES) >> 1) & 1 == 1
    z = dot(beside(mine[...], got[...], right), side_of(coupling, 0, right))
    at = got_gram.shape[1] - rank // got_gram.shape[0] * w
    gram = gram_next[...] + take_rows(got_gram, at, rank, w)
    z_out[...] = z
    sums_out[...] = sums[...] - dot(z, gram)


def joined(mine, other, top):
    half = parity_of(lax.axis_index(AXES), top) == 1
    return jnp.concatenate(
        [jnp.where(half, other, mine), jnp.where(half, mine, other)], axis=0
    )


def add_kernel(low, got, _, out):
    out[...] = low[...] + got[...]


def cut_kernel(low, got, _, *out):
    rank = out[0].shape[1]
    w = (len(out) - 1) * rank
    for j, piece in enumerate(out[:-1]):
        piece[...] = got[:, j * rank : (j + 1) * rank]
    out[-1][...] = low[:, w:] + got[:, w:]


def factor_kernel(top, k, low, got_low, other, *refs):
    got_others, (coupling, out, pair) = refs[:k], refs[-3:]
    n = low.shape[0]
    rank = 2 * n
    bit = top - 1 - k
    device_id = lax.axis_index(AXES)
    half = parity_of(device_id, top)
    right = (device_id >> bit) & 1

    def put(child, mine, theirs, cols):
        pair[pl.ds(pl.multiple_of(child * rank + half * n, n), n), cols] = mine
        pair[pl.ds(pl.multiple_of(child * rank + (1 - half) * n, n), n), cols] = theirs

    for j in range(k):
        cols = slice(j * rank, (j + 1) * rank)
        put(right, low[:, cols], other[:, cols], cols)
        put(1 - right, got_low[:, cols], got_others[j][...], cols)
    out[...] = dot(coupling[k], pair[...])


def level_kernel(top, k, sums, got, factor, *refs):
    rests, (out, both) = refs[:-2], refs[-2:]
    w = factor.shape[1]
    right = (lax.axis_index(AXES) >> (top - 1 - k)) & 1 == 1
    both[...] = beside(sums[:, w:], got[:, w:], right)
    out[:, :w] = sums[:, :w] + got[:, :w] - dot(both[...], factor[...])
    if rests:
        put_rows(out, w, joined(rests[0][...], rests[1][...], top))


def first_kernel(top, packed, got, coupling, out, both, pair):
    rank = out.shape[1]
    right = (lax.axis_index(AXES) >> (top - 2)) & 1
    for child, value in ((right, packed), (1 - right, got)):
        pair[pl.ds(pl.multiple_of(child * rank, rank), rank), :] = take_rows(
            value, 2 * rank, rank, rank
        )
    both[...] = beside(packed[:, rank : 2 * rank], got[:, rank : 2 * rank], right == 1)
    z = dot(both[...], coupling[1])
    out[...] = packed[:, :rank] + got[:, :rank] - dot(z, pair[...])


def early_kernel(top, current, *refs):
    left_first, left_low, left_mid, coupling, out, factor = refs[-6:]
    rank = left_first.shape[1]
    device_id = lax.axis_index(AXES)
    z = []
    for k in range(1, top):
        pair = joined(refs[2 * k - 2][...], refs[2 * k - 1][...], top)
        right = (device_id >> (top - 1 - k)) & 1 == 1
        z.append(pair if k >= top - 2 else dot(pair, side_of(coupling, k, right)))
    low = dot(jnp.concatenate(z[: top - 3], axis=1), left_low[...], NT)
    high = dot(jnp.concatenate(z[top - 3 :], axis=1), left_mid[...], NT)
    out[...] = current[...] - (low + high)
    right = (device_id >> (top - 1)) & 1 == 1
    factor[...] = dot(side_of(coupling, 0, right), left_first[...], NT)


def last_kernel(top, current, mine, other, factor, out):
    out[...] = current[...] - dot(joined(mine[...], other[...], top), factor[...])


def call(kernel, outs, in_specs, out_specs, scratch, *args):
    return pl.pallas_call(
        kernel,
        out_shape=outs,
        in_specs=in_specs,
        out_specs=out_specs,
        scratch_shapes=scratch,
        cost_estimate=pl.CostEstimate(flops=1, bytes_accessed=1, transcendentals=0),
        compiler_params=pltpu.CompilerParams(vmem_limit_bytes=LIMIT),
    )(*args)


def shape(*dims, dtype=F32):
    return jax.ShapeDtypeStruct(dims, dtype)


def in_hbm(*arrays):
    return [pltpu.with_memory_space_constraint(x, pltpu.HBM) for x in arrays]


def exchange(value, mask):
    return lax.ppermute(value, AXES, [(i, i ^ mask) for i in range(lax.axis_size(AXES))])


def per_device(right_side, order, leaf_split, leaf_inverse, basis_left, basis_right, coupling):
    count, size = right_side.shape
    levels, _, rank = basis_left.shape
    top = levels - 1
    n = rank // 2
    rows = count // 2
    wide = top * rank
    low_w = rank * (top - 2) * (top - 3) // 2
    next_w = (top - 2) * rank
    device_id = lax.axis_index(AXES)
    f32_shapes = [
        shape(n, low_w),
        shape(n, low_w + 2 * next_w),
        shape(count, size),
        shape(rank, wide - rank),
        shape(rank, next_w),
        shape(size, (top - 3) * rank),
        shape(size, (top - 3) * rank),
        shape(size, 2 * rank),
        shape(size, 2 * rank),
        shape(size, rank),
        shape(size, rank),
        shape(size, rank),
        shape(3, 2 * rank, 2 * rank),
    ]
    (
        keep, send, current, gram_top, gram_next, left_low, right_low, left_mid, right_mid, left_top,
        right_top, right_last, near, split,
    ) = call(
        functools.partial(first_reads, top),
        f32_shapes + [shape(8, 128, dtype=jnp.int32)],
        [HBM] * 6 + [SMEM],
        [VMEM] * 14,
        [
            pltpu.VMEM((count, size), F32),
            pltpu.VMEM((size, size), F32),
            pltpu.VMEM((1, size), jnp.int32),
            pltpu.SemaphoreType.DMA((5, max(4, top - 3))),
        ],
        *in_hbm(basis_left, basis_right, coupling, right_side, leaf_inverse),
        *in_hbm(order.reshape(1, size)),
        leaf_split,
    )
    got_gram = exchange(send, 1)
    low = keep + got_gram[:, :low_w]
    current, keep, send = call(
        functools.partial(local_kernel, top),
        [
            shape(count, size),
            shape(rows, wide),
            shape(rows, wide + rank // rows * (wide - rank)),
        ],
        [VMEM] * 9,
        [VMEM] * 3,
        [],
        split,
        current,
        left_top,
        right_top,
        right_low,
        right_mid,
        right_last,
        near,
        gram_top,
    )
    got = exchange(send, 1)
    sums, next_sums, z_mine, z_other = call(
        functools.partial(top_kernel, top),
        [shape(rows, next_w), shape(rows, rank), shape(rows, rank), shape(rows, rank)],
        [VMEM] * 4,
        [VMEM] * 4,
        [pltpu.VMEM((2 * rank, wide - rank), F32)],
        keep,
        got,
        gram_top,
        near,
    )
    known = {top - 1: (z_mine, z_other)}
    got_low = exchange(low, 3)
    got_next = exchange(next_sums, 3)
    z, sums = call(
        functools.partial(next_kernel, top),
        [shape(rows, rank), shape(rows, next_w)],
        [VMEM] * 6,
        [VMEM] * 2,
        [],
        next_sums,
        got_next,
        sums,
        gram_next,
        got_gram,
        near,
    )
    known[top - 2] = (z, z)
    low = call(add_kernel, shape(*low.shape), [VMEM, VMEM, ANY], VMEM, [], low, got_low, got_next)
    sums = sums + exchange(sums, 3)
    left_first, coup = call(
        functools.partial(fetch_kernel, top),
        [shape(size, rank), shape(top - 2, 2 * rank, 2 * rank)],
        [HBM] * 2 + [ANY],
        [VMEM] * 2,
        [pltpu.SemaphoreType.DMA((2,))],
        *in_hbm(basis_left, coupling),
        sums,
    )
    for k in range(top - 3, 1, -1):
        mask = 1 << (top - 1 - k) | 1
        w = k * rank
        last = k == 2
        got_low = exchange(low, mask)
        got = exchange(sums, mask)
        others = exchange(low[:, :w], 1)
        *pieces, rest = call(
            cut_kernel,
            [shape(n, rank)] * k + [shape(n, low.shape[1] - w)],
            [VMEM, VMEM, ANY],
            [VMEM] * (k + 1),
            [],
            low,
            got_low,
            sums,
        )
        pieces = [exchange(piece, 1) for piece in pieces]
        rests = [rest, exchange(rest, 1)] if last else []
        factor = call(
            functools.partial(factor_kernel, top, k),
            shape(2 * rank, w),
            [VMEM] * (4 + k),
            VMEM,
            [pltpu.VMEM((2 * rank, w), F32)],
            low,
            got_low,
            others,
            *pieces,
            coup,
        )
        sums, both = call(
            functools.partial(level_kernel, top, k),
            [shape(rows, w + (rank // rows * rank if last else 0)), shape(rows, 2 * rank)],
            [VMEM] * (3 + len(rests)),
            [VMEM] * 2,
            [],
            sums,
            got,
            factor,
            *rests,
        )
        known[k] = (both, both)
        low = rest
    sums, both = call(
        functools.partial(first_kernel, top),
        [shape(rows, rank), shape(rows, 2 * rank)],
        [VMEM] * 3,
        [VMEM] * 2,
        [pltpu.VMEM((2 * rank, rank), F32)],
        sums,
        exchange(sums, 1 << (top - 2) | 1),
        coup,
    )
    known[1] = (both, both)
    got_sums = exchange(sums, 1 << (top - 1) | 1)
    names = range(1, top)
    others = exchange(jnp.concatenate([known[k][1] for k in names], axis=1), 1)
    args, at = [], 0
    for k in names:
        mine = known[k][0]
        args += [mine, others[:, at : at + mine.shape[1]]]
        at += mine.shape[1]
    current, factor = call(
        functools.partial(early_kernel, top),
        [shape(count, size), shape(2 * rank, size)],
        [VMEM] * (5 + len(args)),
        [VMEM] * 2,
        [],
        current,
        *args,
        left_first,
        left_low,
        left_mid,
        coup,
    )
    both = beside(sums, got_sums, (device_id >> (top - 1)) & 1 == 1)
    return call(
        functools.partial(last_kernel, top),
        shape(count, size),
        [VMEM] * 4,
        VMEM,
        [],
        current,
        both,
        exchange(both, 1),
        factor,
    )


def solution(mesh):
    in_specs = (
        P(None, AXES),
        P(AXES),
        P(AXES),
        P(AXES, None),
        P(None, AXES, None),
        P(None, AXES, None),
        P(AXES, None, None, None),
    )
    return jax.shard_map(
        per_device, mesh=mesh, in_specs=in_specs, out_specs=P(None, AXES), check_vma=False
    )
```

```python
import functools

import jax
import jax.numpy as jnp
from jax import lax
from jax.experimental import pallas as pl
from jax.experimental.pallas import tpu as pltpu
from jax.sharding import PartitionSpec as P

AXES = ("grp", "sub")
F32, BF16 = jnp.float32, jnp.bfloat16
NN = (((1,), (0,)), ((), ()))
NT = (((1,), (1,)), ((), ()))
TN = (((0,), (0,)), ((), ()))
ANY = pl.BlockSpec(memory_space=pl.ANY)
HBM = pl.BlockSpec(memory_space=pltpu.HBM)
SMEM = pl.BlockSpec(memory_space=pltpu.SMEM)
VMEM = pl.BlockSpec(memory_space=pltpu.VMEM)
LIMIT = 24 * 1024 * 1024


def parts(x):
    high = x.astype(BF16)
    return high, (x - high.astype(F32)).astype(BF16)


def product(a, b, dims):
    return lax.dot_general(a, b, dims, preferred_element_type=F32)


def dot(a, b, dims=NN):
    if dims == TN:
        a, dims = a.T, NN
    ah, al = parts(a)
    bh, bl = parts(b)
    rows = a.shape[0]
    both = product(jnp.concatenate([ah, al], axis=0), bh, dims)
    return both[:rows] + (both[rows:] + product(ah, bl, dims))


def parity_of(device_id, bits):
    parity = device_id & 1
    for bit in range(1, bits):
        parity = parity ^ ((device_id >> bit) & 1)
    return parity


def sides(split, size):
    border = split[0:1, 0:1]
    return (
        lax.broadcasted_iota(jnp.int32, (1, size), 1) < border,
        lax.broadcasted_iota(jnp.int32, (size, 1), 0) < border,
    )


def first_reads(
    top, left, right, coupling, rhs, leaf, order, split, keep, send, current, gram_top, gram_next,
    left_low, right_low, left_mid, right_mid, left_top, right_top, right_last, near, split_v,
    rhs_v, leaf_v, order_v, sems,
):
    rank = left.shape[2]
    n = rank // 2
    count = top - 3
    bases = []
    for j in range(count):
        cols = slice(j * rank, (j + 1) * rank)
        bases.append(pltpu.make_async_copy(left.at[j + 1], left_low.at[:, cols], sems.at[0, j]))
        bases.append(pltpu.make_async_copy(right.at[j], right_low.at[:, cols], sems.at[1, j]))
    rows = [
        pltpu.make_async_copy(order, order_v, sems.at[2, 0]),
        pltpu.make_async_copy(rhs, rhs_v, sems.at[2, 1]),
    ]
    leaf_copy = pltpu.make_async_copy(leaf, leaf_v, sems.at[2, 2])
    mid = [
        pltpu.make_async_copy(left.at[top - 2], left_mid.at[:, :rank], sems.at[3, 0]),
        pltpu.make_async_copy(left.at[top - 1], left_mid.at[:, rank:], sems.at[3, 1]),
        pltpu.make_async_copy(right.at[top - 3], right_mid.at[:, :rank], sems.at[3, 2]),
        pltpu.make_async_copy(right.at[top - 2], right_mid.at[:, rank:], sems.at[3, 3]),
    ]
    rest = [
        pltpu.make_async_copy(right.at[top], right_top, sems.at[4, 0]),
        pltpu.make_async_copy(coupling.at[0, pl.ds(top - 2, 3)], near, sems.at[4, 1]),
        pltpu.make_async_copy(left.at[top], left_top, sems.at[4, 2]),
        pltpu.make_async_copy(right.at[top - 1], right_last, sems.at[4, 3]),
    ]
    for copy in rows + bases + [leaf_copy] + mid + rest:
        copy.start()
    split_v[...] = jnp.full(split_v.shape, split[0], jnp.int32)
    device_id = lax.axis_index(AXES)
    half = parity_of(device_id, top) == 1
    size = rhs_v.shape[1]
    for copy in rows:
        copy.wait()
    local = order_v[...] - device_id * size
    pick = (lax.broadcasted_iota(jnp.int32, (size, size), 0) == local).astype(F32).astype(BF16)
    high, low = parts(rhs_v[...])
    moved = product(jnp.concatenate([high, low], axis=0), pick, NN).astype(BF16)
    for copy in bases:
        copy.wait()
    grams = dot(left_low[...], right_low[...], TN)
    at = 0
    for k in range(count, 0, -1):
        w = k * rank
        value = grams[w - rank : w, :w]
        keep[:, at : at + w] = jnp.where(half, value[n:], value[:n])
        send[:, at : at + w] = jnp.where(half, value[:n], value[n:])
        at += w
    leaf_copy.wait()
    rows_n = rhs_v.shape[0]
    is_left, _ = sides(split_v, size)
    lh, ll = parts(leaf_v[...])
    zero = jnp.zeros_like(moved)
    side_left, side_right = jnp.where(is_left, moved, zero), jnp.where(is_left, zero, moved)
    both = product(jnp.concatenate([side_left, side_right], axis=0), lh, NN)
    fine = product(
        jnp.concatenate([side_left[:rows_n], side_right[:rows_n]], axis=0), ll, NN
    )
    of_left = both[:rows_n] + (both[rows_n : 2 * rows_n] + fine[:rows_n])
    of_right = both[2 * rows_n : 3 * rows_n] + (both[3 * rows_n :] + fine[rows_n:])
    current[...] = jnp.where(is_left, of_left, of_right)
    for copy in mid:
        copy.wait()
    low_w = right_low.shape[1]
    upper = left_mid[...]
    value = dot(upper, right_low[...], TN)
    gram_next[:, :low_w] = value[:rank]
    gram_top[:, :low_w] = value[rank:]
    value = dot(upper, right_mid[...], TN)
    gram_next[:, low_w:] = value[:rank, :rank]
    gram_top[:, low_w:] = value[rank:]
    put_rows(send, at, gram_next[...])
    for copy in rest:
        copy.wait()


def fetch_kernel(top, left, coupling, _, left_first, coupling_v, sems):
    copies = [
        pltpu.make_async_copy(coupling.at[0, pl.ds(0, top - 2)], coupling_v, sems.at[0]),
        pltpu.make_async_copy(left.at[0], left_first, sems.at[1]),
    ]
    for copy in copies:
        copy.start()
    for copy in copies:
        copy.wait()


def put_rows(out, at, value):
    rows, w = out.shape[0], value.shape[1]
    for row in range(0, value.shape[0], rows):
        out[:, at : at + w] = value[row : row + rows, :]
        at += w
    return at


def take_rows(packed, at, height, w):
    rows = packed.shape[0]
    return jnp.concatenate(
        [packed[:, at + i * w : at + (i + 1) * w] for i in range(height // rows)], axis=0
    )


def local_kernel(
    top, split, first, left_top, right_top, right_low, right_mid, right_last, coupling, gram_top,
    current_out, keep, send,
):
    rank = left_top.shape[1]
    count, size = first.shape
    current = first[...]
    is_left, _ = sides(split, size)
    halves = jnp.concatenate(
        [jnp.where(is_left, current, 0.0), jnp.where(is_left, 0.0, current)], axis=0
    )
    w = dot(halves, right_top[...])
    z = dot(jnp.concatenate([w[:count], w[count:]], axis=1), coupling[2])
    update = dot(jnp.concatenate([z[:, :rank], z[:, rank:]], axis=0), left_top[...], NT)
    current = current - jnp.where(is_left, update[:count], update[count:])
    current_out[...] = current
    half = parity_of(lax.axis_index(AXES), top) == 1
    n = count // 2
    at = 0
    for basis in (right_low, right_mid, right_last):
        sums = dot(current, basis[...])
        w = basis.shape[1]
        keep[:, at : at + w] = jnp.where(half, sums[n:], sums[:n])
        send[:, at : at + w] = jnp.where(half, sums[:n], sums[n:])
        at += w
    put_rows(send, at, gram_top[...])


def beside(own, got, on_right):
    return jnp.concatenate(
        [jnp.where(on_right, got, own), jnp.where(on_right, own, got)], axis=1
    )


def top_kernel(top, keep, got, gram_top, coupling, sums, next_sums, z_mine, z_other, pair):
    rank = gram_top.shape[0]
    w = (top - 1) * rank
    right = lax.axis_index(AXES) & 1
    own_at, got_at = right * rank, (1 - right) * rank
    pair[pl.ds(pl.multiple_of(own_at, rank), rank), :] = gram_top[...]
    pair[pl.ds(pl.multiple_of(got_at, rank), rank), :] = take_rows(got, top * rank, rank, w)
    is_right = right == 1
    z = dot(beside(keep[:, w:], got[:, w : top * rank], is_right), coupling[1])
    value = keep[:, :w] + got[:, :w] - dot(z, pair[...])
    sums[...] = value[:, : w - rank]
    next_sums[...] = value[:, w - rank :]
    z_mine[...] = jnp.where(is_right, z[:, rank:], z[:, :rank])
    z_other[...] = jnp.where(is_right, z[:, :rank], z[:, rank:])


def side_of(coupling, k, right):
    rank = coupling.shape[2] // 2
    return jnp.where(right, coupling[k, :, rank:], coupling[k, :, :rank])


def next_kernel(top, mine, got, sums, gram_next, got_gram, coupling, z_out, sums_out):
    rank, w = gram_next.shape
    right = (lax.axis_index(AXES) >> 1) & 1 == 1
    z = dot(beside(mine[...], got[...], right), side_of(coupling, 0, right))
    at = got_gram.shape[1] - rank // got_gram.shape[0] * w
    gram = gram_next[...] + take_rows(got_gram, at, rank, w)
    z_out[...] = z
    sums_out[...] = sums[...] - dot(z, gram)


def joined(mine, other, top):
    half = parity_of(lax.axis_index(AXES), top) == 1
    return jnp.concatenate(
        [jnp.where(half, other, mine), jnp.where(half, mine, other)], axis=0
    )


def add_kernel(low, got, _, out):
    out[...] = low[...] + got[...]


def cut_kernel(low, got, _, *out):
    rank = out[0].shape[1]
    w = (len(out) - 1) * rank
    for j, piece in enumerate(out[:-1]):
        piece[...] = got[:, j * rank : (j + 1) * rank]
    out[-1][...] = low[:, w:] + got[:, w:]


def factor_kernel(top, k, low, got_low, other, *refs):
    got_others, (coupling, out, pair) = refs[:k], refs[-3:]
    n = low.shape[0]
    rank = 2 * n
    bit = top - 1 - k
    device_id = lax.axis_index(AXES)
    half = parity_of(device_id, top)
    right = (device_id >> bit) & 1

    def put(child, mine, theirs, cols):
        pair[pl.ds(pl.multiple_of(child * rank + half * n, n), n), cols] = mine
        pair[pl.ds(pl.multiple_of(child * rank + (1 - half) * n, n), n), cols] = theirs

    for j in range(k):
        cols = slice(j * rank, (j + 1) * rank)
        put(right, low[:, cols], other[:, cols], cols)
        put(1 - right, got_low[:, cols], got_others[j][...], cols)
    out[...] = dot(coupling[k], pair[...])


def level_kernel(top, k, sums, got, factor, *refs):
    rests, (out, both) = refs[:-2], refs[-2:]
    w = factor.shape[1]
    right = (lax.axis_index(AXES) >> (top - 1 - k)) & 1 == 1
    both[...] = beside(sums[:, w:], got[:, w:], right)
    out[:, :w] = sums[:, :w] + got[:, :w] - dot(both[...], factor[...])
    if rests:
        put_rows(out, w, joined(rests[0][...], rests[1][...], top))


def first_kernel(top, packed, got, coupling, _, out, both, pair):
    rank = out.shape[1]
    right = (lax.axis_index(AXES) >> (top - 2)) & 1
    for child, value in ((right, packed), (1 - right, got)):
        pair[pl.ds(pl.multiple_of(child * rank, rank), rank), :] = take_rows(
            value, 2 * rank, rank, rank
        )
    both[...] = beside(packed[:, rank : 2 * rank], got[:, rank : 2 * rank], right == 1)
    z = dot(both[...], coupling[1])
    out[...] = packed[:, :rank] + got[:, :rank] - dot(z, pair[...])


def early_kernel(top, current, *refs):
    left_low, left_mid, coupling, out = refs[-4:]
    rank = left_mid.shape[1] // 2
    device_id = lax.axis_index(AXES)
    z = []
    for k in range(1, top):
        pair = joined(refs[2 * k - 2][...], refs[2 * k - 1][...], top)
        right = (device_id >> (top - 1 - k)) & 1 == 1
        z.append(pair if k >= top - 2 else dot(pair, side_of(coupling, k, right)))
    low = dot(jnp.concatenate(z[: top - 3], axis=1), left_low[...], NT)
    high = dot(jnp.concatenate(z[top - 3 :], axis=1), left_mid[...], NT)
    out[...] = current[...] - (low + high)


def root_kernel(top, left_first, coupling, out):
    right = (lax.axis_index(AXES) >> (top - 1)) & 1 == 1
    out[...] = dot(side_of(coupling, 0, right), left_first[...], NT)


def last_kernel(top, current, mine, other, factor, out):
    out[...] = current[...] - dot(joined(mine[...], other[...], top), factor[...])


def call(kernel, outs, in_specs, out_specs, scratch, *args):
    return pl.pallas_call(
        kernel,
        out_shape=outs,
        in_specs=in_specs,
        out_specs=out_specs,
        scratch_shapes=scratch,
        cost_estimate=pl.CostEstimate(flops=1, bytes_accessed=1, transcendentals=0),
        compiler_params=pltpu.CompilerParams(vmem_limit_bytes=LIMIT),
    )(*args)


def shape(*dims, dtype=F32):
    return jax.ShapeDtypeStruct(dims, dtype)


def in_hbm(*arrays):
    return [pltpu.with_memory_space_constraint(x, pltpu.HBM) for x in arrays]


def exchange(value, mask):
    return lax.ppermute(value, AXES, [(i, i ^ mask) for i in range(lax.axis_size(AXES))])


def per_device(right_side, order, leaf_split, leaf_inverse, basis_left, basis_right, coupling):
    count, size = right_side.shape
    levels, _, rank = basis_left.shape
    top = levels - 1
    n = rank // 2
    rows = count // 2
    wide = top * rank
    low_w = rank * (top - 2) * (top - 3) // 2
    next_w = (top - 2) * rank
    device_id = lax.axis_index(AXES)
    f32_shapes = [
        shape(n, low_w),
        shape(n, low_w + 2 * next_w),
        shape(count, size),
        shape(rank, wide - rank),
        shape(rank, next_w),
        shape(size, (top - 3) * rank),
        shape(size, (top - 3) * rank),
        shape(size, 2 * rank),
        shape(size, 2 * rank),
        shape(size, rank),
        shape(size, rank),
        shape(size, rank),
        shape(3, 2 * rank, 2 * rank),
    ]
    (
        keep, send, current, gram_top, gram_next, left_low, right_low, left_mid, right_mid, left_top,
        right_top, right_last, near, split,
    ) = call(
        functools.partial(first_reads, top),
        f32_shapes + [shape(8, 128, dtype=jnp.int32)],
        [HBM] * 6 + [SMEM],
        [VMEM] * 14,
        [
            pltpu.VMEM((count, size), F32),
            pltpu.VMEM((size, size), F32),
            pltpu.VMEM((1, size), jnp.int32),
            pltpu.SemaphoreType.DMA((5, max(4, top - 3))),
        ],
        *in_hbm(basis_left, basis_right, coupling, right_side, leaf_inverse),
        *in_hbm(order.reshape(1, size)),
        leaf_split,
    )
    got_gram = exchange(send, 1)
    low = keep + got_gram[:, :low_w]
    current, keep, send = call(
        functools.partial(local_kernel, top),
        [
            shape(count, size),
            shape(rows, wide),
            shape(rows, wide + rank // rows * (wide - rank)),
        ],
        [VMEM] * 9,
        [VMEM] * 3,
        [],
        split,
        current,
        left_top,
        right_top,
        right_low,
        right_mid,
        right_last,
        near,
        gram_top,
    )
    got = exchange(send, 1)
    sums, next_sums, z_mine, z_other = call(
        functools.partial(top_kernel, top),
        [shape(rows, next_w), shape(rows, rank), shape(rows, rank), shape(rows, rank)],
        [VMEM] * 4,
        [VMEM] * 4,
        [pltpu.VMEM((2 * rank, wide - rank), F32)],
        keep,
        got,
        gram_top,
        near,
    )
    known = {top - 1: (z_mine, z_other)}
    got_low = exchange(low, 3)
    got_next = exchange(next_sums, 3)
    z, sums = call(
        functools.partial(next_kernel, top),
        [shape(rows, rank), shape(rows, next_w)],
        [VMEM] * 6,
        [VMEM] * 2,
        [],
        next_sums,
        got_next,
        sums,
        gram_next,
        got_gram,
        near,
    )
    known[top - 2] = (z, z)
    low = call(add_kernel, shape(*low.shape), [VMEM, VMEM, ANY], VMEM, [], low, got_low, got_next)
    sums = sums + exchange(sums, 3)
    left_first, coup = call(
        functools.partial(fetch_kernel, top),
        [shape(size, rank), shape(top - 2, 2 * rank, 2 * rank)],
        [HBM] * 2 + [ANY],
        [VMEM] * 2,
        [pltpu.SemaphoreType.DMA((2,))],
        *in_hbm(basis_left, coupling),
        sums,
    )
    for k in range(top - 3, 1, -1):
        mask = 1 << (top - 1 - k) | 1
        w = k * rank
        last = k == 2
        got_low = exchange(low, mask)
        got = exchange(sums, mask)
        others = exchange(low[:, :w], 1)
        *pieces, rest = call(
            cut_kernel,
            [shape(n, rank)] * k + [shape(n, low.shape[1] - w)],
            [VMEM, VMEM, ANY],
            [VMEM] * (k + 1),
            [],
            low,
            got_low,
            sums,
        )
        pieces = [exchange(piece, 1) for piece in pieces]
        rests = [rest, exchange(rest, 1)] if last else []
        factor = call(
            functools.partial(factor_kernel, top, k),
            shape(2 * rank, w),
            [VMEM] * (4 + k),
            VMEM,
            [pltpu.VMEM((2 * rank, w), F32)],
            low,
            got_low,
            others,
            *pieces,
            coup,
        )
        sums, both = call(
            functools.partial(level_kernel, top, k),
            [shape(rows, w + (rank // rows * rank if last else 0)), shape(rows, 2 * rank)],
            [VMEM] * (3 + len(rests)),
            [VMEM] * 2,
            [],
            sums,
            got,
            factor,
            *rests,
        )
        known[k] = (both, both)
        low = rest
    factor = call(
        functools.partial(root_kernel, top),
        shape(2 * rank, size),
        [VMEM] * 2,
        VMEM,
        [],
        left_first,
        coup,
    )
    sums, both = call(
        functools.partial(first_kernel, top),
        [shape(rows, rank), shape(rows, 2 * rank)],
        [VMEM] * 3 + [ANY],
        [VMEM] * 2,
        [pltpu.VMEM((2 * rank, rank), F32)],
        sums,
        exchange(sums, 1 << (top - 2) | 1),
        coup,
        factor,
    )
    known[1] = (both, both)
    got_sums = exchange(sums, 1 << (top - 1) | 1)
    names = range(1, top)
    others = exchange(jnp.concatenate([known[k][1] for k in names], axis=1), 1)
    args, at = [], 0
    for k in names:
        mine = known[k][0]
        args += [mine, others[:, at : at + mine.shape[1]]]
        at += mine.shape[1]
    current = call(
        functools.partial(early_kernel, top),
        shape(count, size),
        [VMEM] * (4 + len(args)),
        VMEM,
        [],
        current,
        *args,
        left_low,
        left_mid,
        coup,
    )
    both = beside(sums, got_sums, (device_id >> (top - 1)) & 1 == 1)
    return call(
        functools.partial(last_kernel, top),
        shape(count, size),
        [VMEM] * 4,
        VMEM,
        [],
        current,
        both,
        exchange(both, 1),
        factor,
    )


def solution(mesh):
    in_specs = (
        P(None, AXES),
        P(AXES),
        P(AXES),
        P(AXES, None),
        P(None, AXES, None),
        P(None, AXES, None),
        P(AXES, None, None, None),
    )
    return jax.shard_map(
        per_device, mesh=mesh, in_specs=in_specs, out_specs=P(None, AXES), check_vma=False
    )
```

```python
import functools

import jax
import jax.numpy as jnp
from jax import lax
from jax.experimental import pallas as pl
from jax.experimental.pallas import tpu as pltpu
from jax.sharding import PartitionSpec as P

AXES = ("grp", "sub")
F32, BF16 = jnp.float32, jnp.bfloat16
NN = (((1,), (0,)), ((), ()))
NT = (((1,), (1,)), ((), ()))
TN = (((0,), (0,)), ((), ()))
ANY = pl.BlockSpec(memory_space=pl.ANY)
HBM = pl.BlockSpec(memory_space=pltpu.HBM)
SMEM = pl.BlockSpec(memory_space=pltpu.SMEM)
VMEM = pl.BlockSpec(memory_space=pltpu.VMEM)
LIMIT = 24 * 1024 * 1024


def parts(x):
    high = x.astype(BF16)
    return high, (x - high.astype(F32)).astype(BF16)


def product(a, b, dims):
    return lax.dot_general(a, b, dims, preferred_element_type=F32)


def dot(a, b, dims=NN):
    if dims == TN:
        a, dims = a.T, NN
    ah, al = parts(a)
    bh, bl = parts(b)
    rows = a.shape[0]
    both = product(jnp.concatenate([ah, al], axis=0), bh, dims)
    return both[:rows] + (both[rows:] + product(ah, bl, dims))


def parity_of(device_id, bits):
    parity = device_id & 1
    for bit in range(1, bits):
        parity = parity ^ ((device_id >> bit) & 1)
    return parity


def sides(split, size):
    border = split[0:1, 0:1]
    return (
        lax.broadcasted_iota(jnp.int32, (1, size), 1) < border,
        lax.broadcasted_iota(jnp.int32, (size, 1), 0) < border,
    )


def first_reads(
    top, left, right, coupling, rhs, leaf, order, split, keep, send, current, gram_top, gram_next,
    left_low, right_low, left_mid, right_mid, left_top, right_top, right_last, near, split_v,
    rhs_v, leaf_v, order_v, sems,
):
    rank = left.shape[2]
    n = rank // 2
    count = top - 3
    bases = []
    for j in range(count):
        cols = slice(j * rank, (j + 1) * rank)
        bases.append(pltpu.make_async_copy(left.at[j + 1], left_low.at[:, cols], sems.at[0, j]))
        bases.append(pltpu.make_async_copy(right.at[j], right_low.at[:, cols], sems.at[1, j]))
    rows = [
        pltpu.make_async_copy(order, order_v, sems.at[2, 0]),
        pltpu.make_async_copy(rhs, rhs_v, sems.at[2, 1]),
    ]
    leaf_copy = pltpu.make_async_copy(leaf, leaf_v, sems.at[2, 2])
    mid = [
        pltpu.make_async_copy(left.at[top - 2], left_mid.at[:, :rank], sems.at[3, 0]),
        pltpu.make_async_copy(left.at[top - 1], left_mid.at[:, rank:], sems.at[3, 1]),
        pltpu.make_async_copy(right.at[top - 3], right_mid.at[:, :rank], sems.at[3, 2]),
        pltpu.make_async_copy(right.at[top - 2], right_mid.at[:, rank:], sems.at[3, 3]),
    ]
    rest = [
        pltpu.make_async_copy(right.at[top], right_top, sems.at[4, 0]),
        pltpu.make_async_copy(coupling.at[0, pl.ds(top - 2, 3)], near, sems.at[4, 1]),
        pltpu.make_async_copy(left.at[top], left_top, sems.at[4, 2]),
        pltpu.make_async_copy(right.at[top - 1], right_last, sems.at[4, 3]),
    ]
    for copy in rows + bases + [leaf_copy] + mid + rest:
        copy.start()
    split_v[...] = jnp.full(split_v.shape, split[0], jnp.int32)
    device_id = lax.axis_index(AXES)
    half = parity_of(device_id, top) == 1
    size = rhs_v.shape[1]
    for copy in rows:
        copy.wait()
    local = order_v[...] - device_id * size
    pick = (lax.broadcasted_iota(jnp.int32, (size, size), 0) == local).astype(F32).astype(BF16)
    high, low = parts(rhs_v[...])
    moved = product(jnp.concatenate([high, low], axis=0), pick, NN).astype(BF16)
    for copy in bases:
        copy.wait()
    grams = dot(left_low[...], right_low[...], TN)
    at = 0
    for k in range(count, 0, -1):
        w = k * rank
        value = grams[w - rank : w, :w]
        keep[:, at : at + w] = jnp.where(half, value[n:], value[:n])
        send[:, at : at + w] = jnp.where(half, value[:n], value[n:])
        at += w
    leaf_copy.wait()
    rows_n = rhs_v.shape[0]
    is_left, _ = sides(split_v, size)
    lh, ll = parts(leaf_v[...])
    zero = jnp.zeros_like(moved)
    side_left, side_right = jnp.where(is_left, moved, zero), jnp.where(is_left, zero, moved)
    both = product(jnp.concatenate([side_left, side_right], axis=0), lh, NN)
    fine = product(
        jnp.concatenate([side_left[:rows_n], side_right[:rows_n]], axis=0), ll, NN
    )
    of_left = both[:rows_n] + (both[rows_n : 2 * rows_n] + fine[:rows_n])
    of_right = both[2 * rows_n : 3 * rows_n] + (both[3 * rows_n :] + fine[rows_n:])
    current[...] = jnp.where(is_left, of_left, of_right)
    for copy in mid:
        copy.wait()
    low_w = right_low.shape[1]
    upper = left_mid[...]
    value = dot(upper, right_low[...], TN)
    gram_next[:, :low_w] = value[:rank]
    gram_top[:, :low_w] = value[rank:]
    value = dot(upper, right_mid[...], TN)
    gram_next[:, low_w:] = value[:rank, :rank]
    gram_top[:, low_w:] = value[rank:]
    put_rows(send, at, gram_next[...])
    for copy in rest:
        copy.wait()


def fetch_kernel(top, coupling, _, coupling_v, sem):
    copy = pltpu.make_async_copy(coupling.at[0, pl.ds(2, top - 4)], coupling_v, sem)
    copy.start()
    copy.wait()


def put_rows(out, at, value):
    rows, w = out.shape[0], value.shape[1]
    for row in range(0, value.shape[0], rows):
        out[:, at : at + w] = value[row : row + rows, :]
        at += w
    return at


def take_rows(packed, at, height, w):
    rows = packed.shape[0]
    return jnp.concatenate(
        [packed[:, at + i * w : at + (i + 1) * w] for i in range(height // rows)], axis=0
    )


def local_kernel(
    top, split, first, left_top, right_top, right_low, right_mid, right_last, coupling, gram_top,
    current_out, keep, send,
):
    rank = left_top.shape[1]
    count, size = first.shape
    current = first[...]
    is_left, _ = sides(split, size)
    halves = jnp.concatenate(
        [jnp.where(is_left, current, 0.0), jnp.where(is_left, 0.0, current)], axis=0
    )
    w = dot(halves, right_top[...])
    z = dot(jnp.concatenate([w[:count], w[count:]], axis=1), coupling[2])
    update = dot(jnp.concatenate([z[:, :rank], z[:, rank:]], axis=0), left_top[...], NT)
    current = current - jnp.where(is_left, update[:count], update[count:])
    current_out[...] = current
    half = parity_of(lax.axis_index(AXES), top) == 1
    n = count // 2
    at = 0
    for basis in (right_low, right_mid, right_last):
        sums = dot(current, basis[...])
        w = basis.shape[1]
        keep[:, at : at + w] = jnp.where(half, sums[n:], sums[:n])
        send[:, at : at + w] = jnp.where(half, sums[:n], sums[n:])
        at += w
    put_rows(send, at, gram_top[...])


def beside(own, got, on_right):
    return jnp.concatenate(
        [jnp.where(on_right, got, own), jnp.where(on_right, own, got)], axis=1
    )


def top_kernel(top, keep, got, gram_top, coupling, sums, next_sums, z_mine, z_other, pair):
    rank = gram_top.shape[0]
    w = (top - 1) * rank
    right = lax.axis_index(AXES) & 1
    own_at, got_at = right * rank, (1 - right) * rank
    pair[pl.ds(pl.multiple_of(own_at, rank), rank), :] = gram_top[...]
    pair[pl.ds(pl.multiple_of(got_at, rank), rank), :] = take_rows(got, top * rank, rank, w)
    is_right = right == 1
    z = dot(beside(keep[:, w:], got[:, w : top * rank], is_right), coupling[1])
    value = keep[:, :w] + got[:, :w] - dot(z, pair[...])
    sums[...] = value[:, : w - rank]
    next_sums[...] = value[:, w - rank :]
    z_mine[...] = jnp.where(is_right, z[:, rank:], z[:, :rank])
    z_other[...] = jnp.where(is_right, z[:, :rank], z[:, rank:])


def side_of(coupling, k, right):
    rank = coupling.shape[2] // 2
    return jnp.where(right, coupling[k, :, rank:], coupling[k, :, :rank])


def next_kernel(top, mine, got, sums, gram_next, got_gram, coupling, z_out, sums_out):
    rank, w = gram_next.shape
    right = (lax.axis_index(AXES) >> 1) & 1 == 1
    z = dot(beside(mine[...], got[...], right), side_of(coupling, 0, right))
    at = got_gram.shape[1] - rank // got_gram.shape[0] * w
    gram = gram_next[...] + take_rows(got_gram, at, rank, w)
    z_out[...] = z
    sums_out[...] = sums[...] - dot(z, gram)


def joined(mine, other, top):
    half = parity_of(lax.axis_index(AXES), top) == 1
    return jnp.concatenate(
        [jnp.where(half, other, mine), jnp.where(half, mine, other)], axis=0
    )


def add_kernel(low, got, _, out):
    out[...] = low[...] + got[...]


def cut_kernel(low, got, _, *out):
    rank = out[0].shape[1]
    w = (len(out) - 1) * rank
    for j, piece in enumerate(out[:-1]):
        piece[...] = got[:, j * rank : (j + 1) * rank]
    out[-1][...] = low[:, w:] + got[:, w:]


def factor_kernel(top, k, low, got_low, other, *refs):
    got_others, (coupling, out, pair) = refs[:k], refs[-3:]
    n = low.shape[0]
    rank = 2 * n
    bit = top - 1 - k
    device_id = lax.axis_index(AXES)
    half = parity_of(device_id, top)
    right = (device_id >> bit) & 1

    def put(child, mine, theirs, cols):
        pair[pl.ds(pl.multiple_of(child * rank + half * n, n), n), cols] = mine
        pair[pl.ds(pl.multiple_of(child * rank + (1 - half) * n, n), n), cols] = theirs

    for j in range(k):
        cols = slice(j * rank, (j + 1) * rank)
        put(right, low[:, cols], other[:, cols], cols)
        put(1 - right, got_low[:, cols], got_others[j][...], cols)
    out[...] = dot(coupling[k - 2], pair[...])


def level_kernel(top, k, sums, got, factor, *refs):
    rests, (out, both) = refs[:-2], refs[-2:]
    w = factor.shape[1]
    right = (lax.axis_index(AXES) >> (top - 1 - k)) & 1 == 1
    both[...] = beside(sums[:, w:], got[:, w:], right)
    out[:, :w] = sums[:, :w] + got[:, :w] - dot(both[...], factor[...])
    if rests:
        put_rows(out, w, joined(rests[0][...], rests[1][...], top))


def first_kernel(top, packed, got, coupling, _, out, both, pair):
    rank = out.shape[1]
    right = (lax.axis_index(AXES) >> (top - 2)) & 1
    for child, value in ((right, packed), (1 - right, got)):
        pair[pl.ds(pl.multiple_of(child * rank, rank), rank), :] = take_rows(
            value, 2 * rank, rank, rank
        )
    both[...] = beside(packed[:, rank : 2 * rank], got[:, rank : 2 * rank], right == 1)
    z = dot(both[...], coupling[1])
    out[...] = packed[:, :rank] + got[:, :rank] - dot(z, pair[...])


def early_kernel(top, current, *refs):
    left_low, left_mid, root_coupling, coupling, out = refs[-5:]
    rank = left_mid.shape[1] // 2
    device_id = lax.axis_index(AXES)
    z = []
    for k in range(1, top):
        pair = joined(refs[2 * k - 2][...], refs[2 * k - 1][...], top)
        right = (device_id >> (top - 1 - k)) & 1 == 1
        if k >= top - 2:
            z.append(pair)
        elif k == 1:
            z.append(dot(pair, side_of(root_coupling, 1, right)))
        else:
            z.append(dot(pair, side_of(coupling, k - 2, right)))
    low = dot(jnp.concatenate(z[: top - 3], axis=1), left_low[...], NT)
    high = dot(jnp.concatenate(z[top - 3 :], axis=1), left_mid[...], NT)
    out[...] = current[...] - (low + high)


def root_kernel(top, left, coupling, _, out, coupling_v, left_v, sems):
    copies = [
        pltpu.make_async_copy(coupling.at[0, pl.ds(0, 2)], coupling_v, sems.at[0]),
        pltpu.make_async_copy(left.at[0], left_v, sems.at[1]),
    ]
    for copy in copies:
        copy.start()
    for copy in copies:
        copy.wait()
    right = (lax.axis_index(AXES) >> (top - 1)) & 1 == 1
    out[...] = dot(side_of(coupling_v, 0, right), left_v[...], NT)


def last_kernel(top, current, mine, other, factor, out):
    out[...] = current[...] - dot(joined(mine[...], other[...], top), factor[...])


def call(kernel, outs, in_specs, out_specs, scratch, *args):
    return pl.pallas_call(
        kernel,
        out_shape=outs,
        in_specs=in_specs,
        out_specs=out_specs,
        scratch_shapes=scratch,
        cost_estimate=pl.CostEstimate(flops=1, bytes_accessed=1, transcendentals=0),
        compiler_params=pltpu.CompilerParams(vmem_limit_bytes=LIMIT),
    )(*args)


def shape(*dims, dtype=F32):
    return jax.ShapeDtypeStruct(dims, dtype)


def in_hbm(*arrays):
    return [pltpu.with_memory_space_constraint(x, pltpu.HBM) for x in arrays]


def exchange(value, mask):
    return lax.ppermute(value, AXES, [(i, i ^ mask) for i in range(lax.axis_size(AXES))])


def per_device(right_side, order, leaf_split, leaf_inverse, basis_left, basis_right, coupling):
    count, size = right_side.shape
    levels, _, rank = basis_left.shape
    top = levels - 1
    n = rank // 2
    rows = count // 2
    wide = top * rank
    low_w = rank * (top - 2) * (top - 3) // 2
    next_w = (top - 2) * rank
    device_id = lax.axis_index(AXES)
    f32_shapes = [
        shape(n, low_w),
        shape(n, low_w + 2 * next_w),
        shape(count, size),
        shape(rank, wide - rank),
        shape(rank, next_w),
        shape(size, (top - 3) * rank),
        shape(size, (top - 3) * rank),
        shape(size, 2 * rank),
        shape(size, 2 * rank),
        shape(size, rank),
        shape(size, rank),
        shape(size, rank),
        shape(3, 2 * rank, 2 * rank),
    ]
    (
        keep, send, current, gram_top, gram_next, left_low, right_low, left_mid, right_mid, left_top,
        right_top, right_last, near, split,
    ) = call(
        functools.partial(first_reads, top),
        f32_shapes + [shape(8, 128, dtype=jnp.int32)],
        [HBM] * 6 + [SMEM],
        [VMEM] * 14,
        [
            pltpu.VMEM((count, size), F32),
            pltpu.VMEM((size, size), F32),
            pltpu.VMEM((1, size), jnp.int32),
            pltpu.SemaphoreType.DMA((5, max(4, top - 3))),
        ],
        *in_hbm(basis_left, basis_right, coupling, right_side, leaf_inverse),
        *in_hbm(order.reshape(1, size)),
        leaf_split,
    )
    got_gram = exchange(send, 1)
    low = keep + got_gram[:, :low_w]
    current, keep, send = call(
        functools.partial(local_kernel, top),
        [
            shape(count, size),
            shape(rows, wide),
            shape(rows, wide + rank // rows * (wide - rank)),
        ],
        [VMEM] * 9,
        [VMEM] * 3,
        [],
        split,
        current,
        left_top,
        right_top,
        right_low,
        right_mid,
        right_last,
        near,
        gram_top,
    )
    got = exchange(send, 1)
    sums, next_sums, z_mine, z_other = call(
        functools.partial(top_kernel, top),
        [shape(rows, next_w), shape(rows, rank), shape(rows, rank), shape(rows, rank)],
        [VMEM] * 4,
        [VMEM] * 4,
        [pltpu.VMEM((2 * rank, wide - rank), F32)],
        keep,
        got,
        gram_top,
        near,
    )
    known = {top - 1: (z_mine, z_other)}
    got_low = exchange(low, 3)
    got_next = exchange(next_sums, 3)
    z, sums = call(
        functools.partial(next_kernel, top),
        [shape(rows, rank), shape(rows, next_w)],
        [VMEM] * 6,
        [VMEM] * 2,
        [],
        next_sums,
        got_next,
        sums,
        gram_next,
        got_gram,
        near,
    )
    known[top - 2] = (z, z)
    low = call(add_kernel, shape(*low.shape), [VMEM, VMEM, ANY], VMEM, [], low, got_low, got_next)
    sums = sums + exchange(sums, 3)
    coup = call(
        functools.partial(fetch_kernel, top),
        shape(top - 4, 2 * rank, 2 * rank),
        [HBM, ANY],
        VMEM,
        [pltpu.SemaphoreType.DMA],
        *in_hbm(coupling),
        sums,
    )
    for k in range(top - 3, 1, -1):
        mask = 1 << (top - 1 - k) | 1
        w = k * rank
        last = k == 2
        got_low = exchange(low, mask)
        got = exchange(sums, mask)
        others = exchange(low[:, :w], 1)
        *pieces, rest = call(
            cut_kernel,
            [shape(n, rank)] * k + [shape(n, low.shape[1] - w)],
            [VMEM, VMEM, ANY],
            [VMEM] * (k + 1),
            [],
            low,
            got_low,
            sums,
        )
        pieces = [exchange(piece, 1) for piece in pieces]
        rests = [rest, exchange(rest, 1)] if last else []
        factor = call(
            functools.partial(factor_kernel, top, k),
            shape(2 * rank, w),
            [VMEM] * (4 + k),
            VMEM,
            [pltpu.VMEM((2 * rank, w), F32)],
            low,
            got_low,
            others,
            *pieces,
            coup,
        )
        sums, both = call(
            functools.partial(level_kernel, top, k),
            [shape(rows, w + (rank // rows * rank if last else 0)), shape(rows, 2 * rank)],
            [VMEM] * (3 + len(rests)),
            [VMEM] * 2,
            [],
            sums,
            got,
            factor,
            *rests,
        )
        known[k] = (both, both)
        low = rest
    factor, root_coup = call(
        functools.partial(root_kernel, top),
        [shape(2 * rank, size), shape(2, 2 * rank, 2 * rank)],
        [HBM] * 2 + [ANY],
        [VMEM] * 2,
        [pltpu.VMEM((size, rank), F32), pltpu.SemaphoreType.DMA((2,))],
        *in_hbm(basis_left, coupling),
        sums,
    )
    sums, both = call(
        functools.partial(first_kernel, top),
        [shape(rows, rank), shape(rows, 2 * rank)],
        [VMEM] * 3 + [ANY],
        [VMEM] * 2,
        [pltpu.VMEM((2 * rank, rank), F32)],
        sums,
        exchange(sums, 1 << (top - 2) | 1),
        root_coup,
        factor,
    )
    known[1] = (both, both)
    got_sums = exchange(sums, 1 << (top - 1) | 1)
    names = range(1, top)
    others = exchange(jnp.concatenate([known[k][1] for k in names], axis=1), 1)
    args, at = [], 0
    for k in names:
        mine = known[k][0]
        args += [mine, others[:, at : at + mine.shape[1]]]
        at += mine.shape[1]
    current = call(
        functools.partial(early_kernel, top),
        shape(count, size),
        [VMEM] * (5 + len(args)),
        VMEM,
        [],
        current,
        *args,
        left_low,
        left_mid,
        root_coup,
        coup,
    )
    both = beside(sums, got_sums, (device_id >> (top - 1)) & 1 == 1)
    return call(
        functools.partial(last_kernel, top),
        shape(count, size),
        [VMEM] * 4,
        VMEM,
        [],
        current,
        both,
        exchange(both, 1),
        factor,
    )


def solution(mesh):
    in_specs = (
        P(None, AXES),
        P(AXES),
        P(AXES),
        P(AXES, None),
        P(None, AXES, None),
        P(None, AXES, None),
        P(AXES, None, None, None),
    )
    return jax.shard_map(
        per_device, mesh=mesh, in_specs=in_specs, out_specs=P(None, AXES), check_vma=False
    )
```

```python
import functools

import jax
import jax.numpy as jnp
from jax import lax
from jax.experimental import pallas as pl
from jax.experimental.pallas import tpu as pltpu
from jax.sharding import PartitionSpec as P

AXES = ("grp", "sub")
F32, BF16 = jnp.float32, jnp.bfloat16
NN = (((1,), (0,)), ((), ()))
NT = (((1,), (1,)), ((), ()))
TN = (((0,), (0,)), ((), ()))
ANY = pl.BlockSpec(memory_space=pl.ANY)
HBM = pl.BlockSpec(memory_space=pltpu.HBM)
SMEM = pl.BlockSpec(memory_space=pltpu.SMEM)
VMEM = pl.BlockSpec(memory_space=pltpu.VMEM)
LIMIT = 24 * 1024 * 1024


def parts(x):
    high = x.astype(BF16)
    return high, (x - high.astype(F32)).astype(BF16)


def product(a, b, dims):
    return lax.dot_general(a, b, dims, preferred_element_type=F32)


def dot(a, b, dims=NN):
    return dot_parts(a, *parts(b), dims)


def dot_parts(a, bh, bl, dims=NN):
    if dims == TN:
        a, dims = a.T, NN
    ah, al = parts(a)
    rows = a.shape[0]
    both = product(jnp.concatenate([ah, al], axis=0), bh, dims)
    return both[:rows] + (both[rows:] + product(ah, bl, dims))


def parity_of(device_id, bits):
    parity = device_id & 1
    for bit in range(1, bits):
        parity = parity ^ ((device_id >> bit) & 1)
    return parity


def sides(split, size):
    border = split[0:1, 0:1]
    return (
        lax.broadcasted_iota(jnp.int32, (1, size), 1) < border,
        lax.broadcasted_iota(jnp.int32, (size, 1), 0) < border,
    )


def first_reads(
    top, left, right, coupling, rhs, leaf, order, split, keep, send, current, gram_top, gram_next,
    left_low, right_low, left_mid, right_mid, left_top, right_top, right_last, near, split_v,
    rhs_v, leaf_v, order_v, sems,
):
    rank = left.shape[2]
    n = rank // 2
    count = top - 3
    bases = []
    for j in range(count):
        cols = slice(j * rank, (j + 1) * rank)
        bases.append(pltpu.make_async_copy(left.at[j + 1], left_low.at[:, cols], sems.at[0, j]))
        bases.append(pltpu.make_async_copy(right.at[j], right_low.at[:, cols], sems.at[1, j]))
    rows = [
        pltpu.make_async_copy(order, order_v, sems.at[2, 0]),
        pltpu.make_async_copy(rhs, rhs_v, sems.at[2, 1]),
    ]
    leaf_copy = pltpu.make_async_copy(leaf, leaf_v, sems.at[2, 2])
    mid = [
        pltpu.make_async_copy(left.at[top - 2], left_mid.at[:, :rank], sems.at[3, 0]),
        pltpu.make_async_copy(left.at[top - 1], left_mid.at[:, rank:], sems.at[3, 1]),
        pltpu.make_async_copy(right.at[top - 3], right_mid.at[:, :rank], sems.at[3, 2]),
        pltpu.make_async_copy(right.at[top - 2], right_mid.at[:, rank:], sems.at[3, 3]),
    ]
    rest = [
        pltpu.make_async_copy(right.at[top], right_top, sems.at[4, 0]),
        pltpu.make_async_copy(coupling.at[0, pl.ds(top - 2, 3)], near, sems.at[4, 1]),
        pltpu.make_async_copy(left.at[top], left_top, sems.at[4, 2]),
        pltpu.make_async_copy(right.at[top - 1], right_last, sems.at[4, 3]),
    ]
    for copy in rows + bases + [leaf_copy] + mid + rest:
        copy.start()
    split_v[...] = jnp.full(split_v.shape, split[0], jnp.int32)
    device_id = lax.axis_index(AXES)
    half = parity_of(device_id, top) == 1
    size = rhs_v.shape[1]
    for copy in rows:
        copy.wait()
    local = order_v[...] - device_id * size
    pick = (lax.broadcasted_iota(jnp.int32, (size, size), 0) == local).astype(F32).astype(BF16)
    high, low = parts(rhs_v[...])
    moved = product(jnp.concatenate([high, low], axis=0), pick, NN).astype(BF16)
    for copy in bases:
        copy.wait()
    low_parts = parts(right_low[...])
    grams = dot_parts(left_low[...], *low_parts, TN)
    at = 0
    for k in range(count, 0, -1):
        w = k * rank
        value = grams[w - rank : w, :w]
        keep[:, at : at + w] = jnp.where(half, value[n:], value[:n])
        send[:, at : at + w] = jnp.where(half, value[:n], value[n:])
        at += w
    leaf_copy.wait()
    rows_n = rhs_v.shape[0]
    is_left, _ = sides(split_v, size)
    lh, ll = parts(leaf_v[...])
    zero = jnp.zeros_like(moved)
    side_left, side_right = jnp.where(is_left, moved, zero), jnp.where(is_left, zero, moved)
    both = product(jnp.concatenate([side_left, side_right], axis=0), lh, NN)
    fine = product(
        jnp.concatenate([side_left[:rows_n], side_right[:rows_n]], axis=0), ll, NN
    )
    of_left = both[:rows_n] + (both[rows_n : 2 * rows_n] + fine[:rows_n])
    of_right = both[2 * rows_n : 3 * rows_n] + (both[3 * rows_n :] + fine[rows_n:])
    current[...] = jnp.where(is_left, of_left, of_right)
    for copy in mid:
        copy.wait()
    low_w = right_low.shape[1]
    upper = left_mid[...]
    value = dot_parts(upper, *low_parts, TN)
    gram_next[:, :low_w] = value[:rank]
    gram_top[:, :low_w] = value[rank:]
    value = dot(upper, right_mid[...], TN)
    gram_next[:, low_w:] = value[:rank, :rank]
    gram_top[:, low_w:] = value[rank:]
    put_rows(send, at, gram_next[...])
    for copy in rest:
        copy.wait()


def fetch_kernel(top, coupling, _, coupling_v, sem):
    copy = pltpu.make_async_copy(coupling.at[0, pl.ds(2, top - 4)], coupling_v, sem)
    copy.start()
    copy.wait()


def put_rows(out, at, value):
    rows, w = out.shape[0], value.shape[1]
    for row in range(0, value.shape[0], rows):
        out[:, at : at + w] = value[row : row + rows, :]
        at += w
    return at


def take_rows(packed, at, height, w):
    rows = packed.shape[0]
    return jnp.concatenate(
        [packed[:, at + i * w : at + (i + 1) * w] for i in range(height // rows)], axis=0
    )


def local_kernel(
    top, split, first, left_top, right_top, right_low, right_mid, right_last, coupling, gram_top,
    current_out, keep, send,
):
    rank = left_top.shape[1]
    count, size = first.shape
    current = first[...]
    is_left, _ = sides(split, size)
    halves = jnp.concatenate(
        [jnp.where(is_left, current, 0.0), jnp.where(is_left, 0.0, current)], axis=0
    )
    w = dot(halves, right_top[...])
    z = dot(jnp.concatenate([w[:count], w[count:]], axis=1), coupling[2])
    update = dot(jnp.concatenate([z[:, :rank], z[:, rank:]], axis=0), left_top[...], NT)
    current = current - jnp.where(is_left, update[:count], update[count:])
    current_out[...] = current
    half = parity_of(lax.axis_index(AXES), top) == 1
    n = count // 2
    at = 0
    for basis in (right_low, right_mid, right_last):
        sums = dot(current, basis[...])
        w = basis.shape[1]
        keep[:, at : at + w] = jnp.where(half, sums[n:], sums[:n])
        send[:, at : at + w] = jnp.where(half, sums[:n], sums[n:])
        at += w
    put_rows(send, at, gram_top[...])


def beside(own, got, on_right):
    return jnp.concatenate(
        [jnp.where(on_right, got, own), jnp.where(on_right, own, got)], axis=1
    )


def top_kernel(top, keep, got, gram_top, coupling, sums, next_sums, z_mine, z_other, pair):
    rank = gram_top.shape[0]
    w = (top - 1) * rank
    right = lax.axis_index(AXES) & 1
    own_at, got_at = right * rank, (1 - right) * rank
    pair[pl.ds(pl.multiple_of(own_at, rank), rank), :] = gram_top[...]
    pair[pl.ds(pl.multiple_of(got_at, rank), rank), :] = take_rows(got, top * rank, rank, w)
    is_right = right == 1
    z = dot(beside(keep[:, w:], got[:, w : top * rank], is_right), coupling[1])
    value = keep[:, :w] + got[:, :w] - dot(z, pair[...])
    sums[...] = value[:, : w - rank]
    next_sums[...] = value[:, w - rank :]
    z_mine[...] = jnp.where(is_right, z[:, rank:], z[:, :rank])
    z_other[...] = jnp.where(is_right, z[:, :rank], z[:, rank:])


def side_of(coupling, k, right):
    rank = coupling.shape[2] // 2
    return jnp.where(right, coupling[k, :, rank:], coupling[k, :, :rank])


def next_kernel(top, mine, got, sums, gram_next, got_gram, coupling, z_out, sums_out):
    rank, w = gram_next.shape
    right = (lax.axis_index(AXES) >> 1) & 1 == 1
    z = dot(beside(mine[...], got[...], right), side_of(coupling, 0, right))
    at = got_gram.shape[1] - rank // got_gram.shape[0] * w
    gram = gram_next[...] + take_rows(got_gram, at, rank, w)
    z_out[...] = z
    sums_out[...] = sums[...] - dot(z, gram)


def joined(mine, other, top):
    half = parity_of(lax.axis_index(AXES), top) == 1
    return jnp.concatenate(
        [jnp.where(half, other, mine), jnp.where(half, mine, other)], axis=0
    )


def add_kernel(low, got, _, out):
    out[...] = low[...] + got[...]


def cut_kernel(low, got, _, *out):
    rank = out[0].shape[1]
    w = (len(out) - 1) * rank
    for j, piece in enumerate(out[:-1]):
        piece[...] = got[:, j * rank : (j + 1) * rank]
    out[-1][...] = low[:, w:] + got[:, w:]


def factor_kernel(top, k, low, got_low, other, *refs):
    got_others, (coupling, out, pair) = refs[:k], refs[-3:]
    n = low.shape[0]
    rank = 2 * n
    bit = top - 1 - k
    device_id = lax.axis_index(AXES)
    half = parity_of(device_id, top)
    right = (device_id >> bit) & 1

    def put(child, mine, theirs, cols):
        pair[pl.ds(pl.multiple_of(child * rank + half * n, n), n), cols] = mine
        pair[pl.ds(pl.multiple_of(child * rank + (1 - half) * n, n), n), cols] = theirs

    for j in range(k):
        cols = slice(j * rank, (j + 1) * rank)
        put(right, low[:, cols], other[:, cols], cols)
        put(1 - right, got_low[:, cols], got_others[j][...], cols)
    out[...] = dot(coupling[k - 2], pair[...])


def level_kernel(top, k, sums, got, factor, *refs):
    rests, (out, both) = refs[:-2], refs[-2:]
    w = factor.shape[1]
    right = (lax.axis_index(AXES) >> (top - 1 - k)) & 1 == 1
    both[...] = beside(sums[:, w:], got[:, w:], right)
    out[:, :w] = sums[:, :w] + got[:, :w] - dot(both[...], factor[...])
    if rests:
        put_rows(out, w, joined(rests[0][...], rests[1][...], top))


def first_kernel(top, packed, got, coupling, _, out, both, pair):
    rank = out.shape[1]
    right = (lax.axis_index(AXES) >> (top - 2)) & 1
    for child, value in ((right, packed), (1 - right, got)):
        pair[pl.ds(pl.multiple_of(child * rank, rank), rank), :] = take_rows(
            value, 2 * rank, rank, rank
        )
    both[...] = beside(packed[:, rank : 2 * rank], got[:, rank : 2 * rank], right == 1)
    z = dot(both[...], coupling[1])
    out[...] = packed[:, :rank] + got[:, :rank] - dot(z, pair[...])


def early_kernel(top, current, *refs):
    left_low, left_mid, root_coupling, coupling, out = refs[-5:]
    rank = left_mid.shape[1] // 2
    device_id = lax.axis_index(AXES)
    z = []
    for k in range(1, top):
        pair = joined(refs[2 * k - 2][...], refs[2 * k - 1][...], top)
        right = (device_id >> (top - 1 - k)) & 1 == 1
        if k >= top - 2:
            z.append(pair)
        elif k == 1:
            z.append(dot(pair, side_of(root_coupling, 1, right)))
        else:
            z.append(dot(pair, side_of(coupling, k - 2, right)))
    low = dot(jnp.concatenate(z[: top - 3], axis=1), left_low[...], NT)
    high = dot(jnp.concatenate(z[top - 3 :], axis=1), left_mid[...], NT)
    out[...] = current[...] - (low + high)


def root_kernel(top, left, coupling, _, out, coupling_v, left_v, sems):
    copies = [
        pltpu.make_async_copy(coupling.at[0, pl.ds(0, 2)], coupling_v, sems.at[0]),
        pltpu.make_async_copy(left.at[0], left_v, sems.at[1]),
    ]
    for copy in copies:
        copy.start()
    for copy in copies:
        copy.wait()
    right = (lax.axis_index(AXES) >> (top - 1)) & 1 == 1
    out[...] = dot(side_of(coupling_v, 0, right), left_v[...], NT)


def last_kernel(top, current, mine, other, factor, out):
    out[...] = current[...] - dot(joined(mine[...], other[...], top), factor[...])


def call(kernel, outs, in_specs, out_specs, scratch, *args):
    return pl.pallas_call(
        kernel,
        out_shape=outs,
        in_specs=in_specs,
        out_specs=out_specs,
        scratch_shapes=scratch,
        cost_estimate=pl.CostEstimate(flops=1, bytes_accessed=1, transcendentals=0),
        compiler_params=pltpu.CompilerParams(vmem_limit_bytes=LIMIT),
    )(*args)


def shape(*dims, dtype=F32):
    return jax.ShapeDtypeStruct(dims, dtype)


def in_hbm(*arrays):
    return [pltpu.with_memory_space_constraint(x, pltpu.HBM) for x in arrays]


def exchange(value, mask):
    return lax.ppermute(value, AXES, [(i, i ^ mask) for i in range(lax.axis_size(AXES))])


def per_device(right_side, order, leaf_split, leaf_inverse, basis_left, basis_right, coupling):
    count, size = right_side.shape
    levels, _, rank = basis_left.shape
    top = levels - 1
    n = rank // 2
    rows = count // 2
    wide = top * rank
    low_w = rank * (top - 2) * (top - 3) // 2
    next_w = (top - 2) * rank
    device_id = lax.axis_index(AXES)
    f32_shapes = [
        shape(n, low_w),
        shape(n, low_w + 2 * next_w),
        shape(count, size),
        shape(rank, wide - rank),
        shape(rank, next_w),
        shape(size, (top - 3) * rank),
        shape(size, (top - 3) * rank),
        shape(size, 2 * rank),
        shape(size, 2 * rank),
        shape(size, rank),
        shape(size, rank),
        shape(size, rank),
        shape(3, 2 * rank, 2 * rank),
    ]
    (
        keep, send, current, gram_top, gram_next, left_low, right_low, left_mid, right_mid, left_top,
        right_top, right_last, near, split,
    ) = call(
        functools.partial(first_reads, top),
        f32_shapes + [shape(8, 128, dtype=jnp.int32)],
        [HBM] * 6 + [SMEM],
        [VMEM] * 14,
        [
            pltpu.VMEM((count, size), F32),
            pltpu.VMEM((size, size), F32),
            pltpu.VMEM((1, size), jnp.int32),
            pltpu.SemaphoreType.DMA((5, max(4, top - 3))),
        ],
        *in_hbm(basis_left, basis_right, coupling, right_side, leaf_inverse),
        *in_hbm(order.reshape(1, size)),
        leaf_split,
    )
    got_gram = exchange(send, 1)
    low = keep + got_gram[:, :low_w]
    current, keep, send = call(
        functools.partial(local_kernel, top),
        [
            shape(count, size),
            shape(rows, wide),
            shape(rows, wide + rank // rows * (wide - rank)),
        ],
        [VMEM] * 9,
        [VMEM] * 3,
        [],
        split,
        current,
        left_top,
        right_top,
        right_low,
        right_mid,
        right_last,
        near,
        gram_top,
    )
    got = exchange(send, 1)
    sums, next_sums, z_mine, z_other = call(
        functools.partial(top_kernel, top),
        [shape(rows, next_w), shape(rows, rank), shape(rows, rank), shape(rows, rank)],
        [VMEM] * 4,
        [VMEM] * 4,
        [pltpu.VMEM((2 * rank, wide - rank), F32)],
        keep,
        got,
        gram_top,
        near,
    )
    known = {top - 1: (z_mine, z_other)}
    got_low = exchange(low, 3)
    got_next = exchange(next_sums, 3)
    z, sums = call(
        functools.partial(next_kernel, top),
        [shape(rows, rank), shape(rows, next_w)],
        [VMEM] * 6,
        [VMEM] * 2,
        [],
        next_sums,
        got_next,
        sums,
        gram_next,
        got_gram,
        near,
    )
    known[top - 2] = (z, z)
    low = call(add_kernel, shape(*low.shape), [VMEM, VMEM, ANY], VMEM, [], low, got_low, got_next)
    sums = sums + exchange(sums, 3)
    coup = call(
        functools.partial(fetch_kernel, top),
        shape(top - 4, 2 * rank, 2 * rank),
        [HBM, ANY],
        VMEM,
        [pltpu.SemaphoreType.DMA],
        *in_hbm(coupling),
        sums,
    )
    for k in range(top - 3, 1, -1):
        mask = 1 << (top - 1 - k) | 1
        w = k * rank
        last = k == 2
        got_low = exchange(low, mask)
        got = exchange(sums, mask)
        others = exchange(low[:, :w], 1)
        *pieces, rest = call(
            cut_kernel,
            [shape(n, rank)] * k + [shape(n, low.shape[1] - w)],
            [VMEM, VMEM, ANY],
            [VMEM] * (k + 1),
            [],
            low,
            got_low,
            sums,
        )
        pieces = [exchange(piece, 1) for piece in pieces]
        rests = [rest, exchange(rest, 1)] if last else []
        factor = call(
            functools.partial(factor_kernel, top, k),
            shape(2 * rank, w),
            [VMEM] * (4 + k),
            VMEM,
            [pltpu.VMEM((2 * rank, w), F32)],
            low,
            got_low,
            others,
            *pieces,
            coup,
        )
        sums, both = call(
            functools.partial(level_kernel, top, k),
            [shape(rows, w + (rank // rows * rank if last else 0)), shape(rows, 2 * rank)],
            [VMEM] * (3 + len(rests)),
            [VMEM] * 2,
            [],
            sums,
            got,
            factor,
            *rests,
        )
        known[k] = (both, both)
        low = rest
    factor, root_coup = call(
        functools.partial(root_kernel, top),
        [shape(2 * rank, size), shape(2, 2 * rank, 2 * rank)],
        [HBM] * 2 + [ANY],
        [VMEM] * 2,
        [pltpu.VMEM((size, rank), F32), pltpu.SemaphoreType.DMA((2,))],
        *in_hbm(basis_left, coupling),
        sums,
    )
    sums, both = call(
        functools.partial(first_kernel, top),
        [shape(rows, rank), shape(rows, 2 * rank)],
        [VMEM] * 3 + [ANY],
        [VMEM] * 2,
        [pltpu.VMEM((2 * rank, rank), F32)],
        sums,
        exchange(sums, 1 << (top - 2) | 1),
        root_coup,
        factor,
    )
    known[1] = (both, both)
    got_sums = exchange(sums, 1 << (top - 1) | 1)
    names = range(1, top)
    others = exchange(jnp.concatenate([known[k][1] for k in names], axis=1), 1)
    args, at = [], 0
    for k in names:
        mine = known[k][0]
        args += [mine, others[:, at : at + mine.shape[1]]]
        at += mine.shape[1]
    current = call(
        functools.partial(early_kernel, top),
        shape(count, size),
        [VMEM] * (5 + len(args)),
        VMEM,
        [],
        current,
        *args,
        left_low,
        left_mid,
        root_coup,
        coup,
    )
    both = beside(sums, got_sums, (device_id >> (top - 1)) & 1 == 1)
    return call(
        functools.partial(last_kernel, top),
        shape(count, size),
        [VMEM] * 4,
        VMEM,
        [],
        current,
        both,
        exchange(both, 1),
        factor,
    )


def solution(mesh):
    in_specs = (
        P(None, AXES),
        P(AXES),
        P(AXES),
        P(AXES, None),
        P(None, AXES, None),
        P(None, AXES, None),
        P(AXES, None, None, None),
    )
    return jax.shard_map(
        per_device, mesh=mesh, in_specs=in_specs, out_specs=P(None, AXES), check_vma=False
    )
```
